32 devices in a mesh: parts: 2 (over y), tensor: 4 (over z), dp: 4 (over x, core).
Axes of the slice: x: 2, y: 2, z: 4, core: 2. Of those that a mesh axis runs over, the one named last changes fastest.
Arguments:
- hidden_acts: bfloat16 [2048, 28672], P(('parts', 'dp'), 'tensor'), parts along dimension 0, may hold values from -6 to 6
- output_grad: bfloat16 [4, 4, 512, 2048], P('tensor', None, None, ('parts', 'dp')), parts along dimension 3, may hold values from -6 to 6
- down_weight: bfloat16 [4, 4, 512, 28672], P(None, 'dp', None, 'tensor'), may hold values from -0.0625 to 0.0625
- input_basis: bfloat16 [28672, 64], P('tensor'), may hold values from -0.03125 to 0.03125
- output_basis: bfloat16 [4, 4, 512, 64], P('tensor'), may hold values from -0.0625 to 0.0625
- token_example: int32 [8, 256], P(('parts', 'dp')), parts along dimension 0, may hold values from 0 to 3, never falling along the last dimension, each value on 1 to 128 neighbouring positions
- example_group: int32 [32], P(('parts', 'dp')), parts along dimension 0, may hold values from 0 to 7
Outputs:
- hidden_grad: bfloat16 [2048, 28672], P(('parts', 'dp'), 'tensor'), parts along dimension 0
- fisher: float32 [8192, 4096], P(('parts', 'dp'), 'tensor'), parts along dimension 0
- group_grad: float32 [16, 4096], P('parts', 'tensor'), parts along dimension 0
The draws below stay inside these ranges and needn't reach their ends.
There are 2 independent parts, one for each index of `parts`. The reference program is written for one: setup_inputs(seed, part) draws one part's arguments, and reference() takes and returns one part's arrays. A program takes and returns all parts, laid end to end along the dimension named above; an argument that names none is the same for every part. Nothing has to cross between parts.
Inputs may be any that keep to these rules, and one draw needn't show every extreme that they name: `token_example`: within each row the ids never fall, and each of the 4 examples takes 1 to 128 consecutive tokens.
All inputs are finite; a program needn't handle non-finite values.
Results may differ from the reference program's by a relative error of at most 0.009.
Values may be sent and summed in bfloat16 or wider, within the bound.
No kernel may reach another device: no remote copies, remote signals or barrier semaphores. Data moves between devices by JAX's collectives and lax.ppermute only.
A program may use at most 128 MiB of HBM per device.

```python
import math
import jax
import jax.numpy as jnp
import numpy as np
from jax import lax

D = 8192
FF = 28672
K = 64
TOK_DEV = 256
EX_DEV = 4
SEG_MOST = 128
GROUPS = 8
DA = 4
DB = 4
DS = 512
TOKENS = 1024
EXAMPLES = 16


def set_ends(array, rng, least, high):
    index_at = [jax.random.randint(jax.random.fold_in(rng, axis), (), 0, length) for axis, length in enumerate(array.shape)]
    longest = array.shape.index(max(array.shape))
    beside = index_at[:longest] + [(index_at[longest] + 1) % array.shape[longest]] + index_at[longest + 1:]
    return array.at[tuple(index_at)].set(least).at[tuple(beside)].set(high)


def shard_levels(own_key, extent, cuts, smallest, largest):
    factor_of = 1.0
    for axis_at, blocks in cuts:
        steps = jax.random.uniform(jax.random.fold_in(jax.random.fold_in(own_key, 6), axis_at), (blocks,), jnp.float32, smallest / len(cuts), largest / len(cuts))
        factor_of = factor_of * jnp.repeat(jnp.exp(steps), extent[axis_at] // blocks).reshape((-1,) + (1,) * (len(extent) - 1 - axis_at))
    return factor_of


def profile(number_of, total, most, lean):
    loads = [(1 << 20) // math.isqrt(standing ** lean) + 1 for standing in range(2, number_of + 1)]
    rest, given = total - most - (number_of - 1), [1] * (number_of - 1)
    while rest > 0:
        free = [i for i in range(number_of - 1) if given[i] < most]
        pool, budget = sum([loads[i] for i in free]), rest
        for i in free:
            addition = min(most - given[i], max(1, budget * loads[i] // pool), rest)
            given[i] = given[i] + addition
            rest = rest - addition
    return np.array([most] + given)


def ragged(own_key, count, total, reach, skew):
    if count == 2:
        one = jax.random.randint(own_key, (), max(1, total - reach), min(reach, total - 1) + 1)
        return jnp.stack([one, total - one])
    tallies = jnp.asarray(profile(count, total, reach, skew), jnp.int32)
    twos = (count - 1) // 2
    giver, sink = tallies[1:1 + 2 * twos:2], tallies[2:2 + 2 * twos:2]
    slack = jnp.minimum(giver - 1, reach - sink)
    moved = jax.random.randint(jax.random.fold_in(own_key, 1), (twos,), 0, 1 << 20) % (slack + 1)
    tallies = tallies.at[1:1 + 2 * twos:2].set(giver - moved).at[2:2 + 2 * twos:2].set(sink + moved)
    return tallies[jax.random.permutation(jax.random.fold_in(own_key, 2), count)]


def centred(key, dims, deviation, limit, shards=(), kind=jnp.bfloat16):
    loudness = shard_levels(key, dims, shards, -0.22, 0.18) if shards else 1.0
    values = jax.random.normal(key, dims, jnp.float32) * deviation * loudness
    return jnp.minimum(jnp.maximum(values, -limit), limit).astype(kind)


def setup_inputs(seed: int = 0, part: int = 0) -> dict:
    keys = jax.random.split(jax.random.key(seed), 8)
    own_keys = jax.random.split(jax.random.fold_in(keys[7], part), 8)
    hidden_acts = centred(own_keys[0], (TOKENS, FF), 1.0, 6.0, ((0, 4), (1, 4)))
    output_grad = centred(own_keys[1], (DA, DB, DS, TOKENS), 1.0, 6.0, ((0, 4), (3, 4)))
    down_weight = centred(keys[2], (DA, DB, DS, FF), D ** -0.5, 0.0625, ((1, 4), (3, 4)))
    input_basis = centred(keys[3], (FF, K), FF ** -0.5, 0.03125, ((0, 4),))
    output_basis = centred(keys[4], (DA, DB, DS, K), D ** -0.5, 0.0625, ((0, 4),))
    token_example = jax.vmap(lambda own: jnp.searchsorted(jnp.cumsum(ragged(own, EX_DEV, TOK_DEV, SEG_MOST, 1)), jnp.arange(TOK_DEV), side="right"))(jax.random.split(own_keys[5], DB)).reshape((DB, TOK_DEV)).astype(jnp.int32)
    example_group = set_ends(jax.random.randint(own_keys[6], (EXAMPLES,), 0, GROUPS), jax.random.fold_in(own_keys[6], 1), 0, GROUPS - 1).astype(jnp.int32)
    return {"hidden_acts": hidden_acts, "output_grad": output_grad, "down_weight": down_weight, "input_basis": input_basis, "output_basis": output_basis, "token_example": token_example, "example_group": example_group}


highest = lax.Precision.HIGHEST


def reference(hidden_acts, output_grad, down_weight, input_basis, output_basis, token_example, example_group):
    acts_low = jnp.dot(hidden_acts, input_basis, preferred_element_type=jnp.float32)
    flat_grad = output_grad.reshape(D, TOKENS)
    grads_low = jnp.dot(flat_grad.T, output_basis.reshape(D, K), preferred_element_type=jnp.float32)
    running = jnp.zeros((TOKENS, FF), jnp.float32)
    for block_index in range(DB):
        grad_block = output_grad[:, block_index].reshape(DA * DS, TOKENS)
        weight_block = down_weight[:, block_index].reshape(DA * DS, FF)
        block_terms = jnp.dot(grad_block.T, weight_block, preferred_element_type=jnp.float32)
        rounded = lax.optimization_barrier(block_terms.astype(jnp.bfloat16))
        running = running + rounded.astype(jnp.float32)
    hidden_grad = running.astype(jnp.bfloat16)
    example_index = (token_example + EX_DEV * jnp.arange(DB, dtype=jnp.int32)[:, None]).reshape(TOKENS)
    onehot = (example_index[:, None] == jnp.arange(EXAMPLES, dtype=jnp.int32)[None, :]).astype(jnp.float32)
    counts = jnp.sum(onehot, axis=0)
    spread = onehot[:, :, None] * acts_low[:, None, :]
    outer_sum = jnp.einsum("tea,tb->eab", spread, grads_low, precision=highest)
    example_grad = (outer_sum.reshape(EXAMPLES, K * K) / counts[:, None]).astype(jnp.bfloat16)
    fisher = jnp.dot(example_grad.T, example_grad, preferred_element_type=jnp.float32)
    member = (example_group[:, None] == jnp.arange(GROUPS, dtype=jnp.int32)[None, :]).astype(jnp.bfloat16)
    group_grad = jnp.dot(member.T, example_grad, preferred_element_type=jnp.float32)
    return hidden_grad, fisher, group_grad
```

```python
import jax
import jax.numpy as jnp
from jax import lax
from jax.sharding import PartitionSpec as P

GROUPS = 8


highest = lax.Precision.HIGHEST


def feature_dot(grad_block, weight_block):
    return lax.dot_general(
        grad_block,
        weight_block,
        (((0, 1, 2), (0, 1, 2)), ((), ())),
        preferred_element_type=jnp.float32,
    )


def example_gradients(acts_low, grads_low, local_ids, examples):
    onehot = (local_ids[:, None] == jnp.arange(examples, dtype=jnp.int32)[None, :]).astype(
        jnp.float32
    )
    counts = jnp.sum(onehot, axis=0)
    spread = (onehot[:, :, None] * acts_low[:, None, :]).reshape(onehot.shape[0], -1)
    outer_sum = lax.dot_general(
        spread,
        grads_low,
        (((0,), (0,)), ((), ())),
        precision=highest,
        preferred_element_type=jnp.float32,
    )
    basis_rank = acts_low.shape[1]
    outer_sum = outer_sum.reshape(examples, basis_rank * grads_low.shape[1]) / counts[:, None]
    return outer_sum.astype(jnp.bfloat16)


def fisher_and_groups(example_grad, example_group):
    flat_width = example_grad.shape[1]
    row_count = flat_width // lax.axis_size("dp")
    col_count = flat_width // lax.axis_size("tensor")
    col_start = lax.axis_index("tensor") * col_count
    row_start = lax.axis_index("dp") * row_count
    group_column = jnp.broadcast_to(
        example_group.astype(jnp.bfloat16)[:, None], (example_grad.shape[0], 128)
    )
    every = lax.all_gather(
        jnp.concatenate([example_grad, group_column], axis=1), "dp", axis=0, tiled=True
    )
    every_grad = every[:, :flat_width]
    every_group = every[:, flat_width].astype(jnp.int32)
    rows_part = lax.dynamic_slice_in_dim(every_grad, row_start, row_count, 1)
    cols_part = lax.dynamic_slice_in_dim(every_grad, col_start, col_count, 1)
    fisher = lax.dot_general(
        rows_part, cols_part, (((0,), (0,)), ((), ())), preferred_element_type=jnp.float32
    )
    member = (every_group[:, None] == jnp.arange(GROUPS, dtype=jnp.int32)[None, :]).astype(
        jnp.bfloat16
    )
    group_grad = lax.dot_general(
        member, cols_part, (((0,), (0,)), ((), ())), preferred_element_type=jnp.float32
    )
    return fisher, group_grad


def per_device(
    hidden_acts, output_grad, down_weight, input_basis, output_basis, token_example, example_group
):
    pieces = lax.all_to_all(output_grad, "dp", split_axis=1, concat_axis=3, tiled=True)
    columns = lax.all_gather(pieces, "tensor", axis=0, tiled=True)
    acts_part = jnp.dot(hidden_acts, input_basis, preferred_element_type=jnp.float32)
    grads_part = feature_dot(output_grad, output_basis)
    acts_low, grads_low = lax.psum((acts_part, grads_part), "tensor")
    hidden_grad = lax.psum_scatter(
        feature_dot(columns, down_weight).astype(jnp.bfloat16),
        "dp",
        scatter_dimension=0,
        tiled=True,
    )
    example_grad = example_gradients(acts_low, grads_low, token_example[0], example_group.shape[0])
    fisher, group_grad = fisher_and_groups(example_grad, example_group)
    return (hidden_grad, fisher, group_grad)


def solution(mesh):
    return jax.shard_map(
        per_device,
        mesh=mesh,
        in_specs=(
            P(("parts", "dp"), "tensor"),
            P("tensor", None, None, ("parts", "dp")),
            P(None, "dp", None, "tensor"),
            P("tensor", None),
            P("tensor", None, None, None),
            P(("parts", "dp"), None),
            P(("parts", "dp")),
        ),
        out_specs=(
            P(("parts", "dp"), "tensor"),
            P(("parts", "dp"), "tensor"),
            P("parts", "tensor"),
        ),
        check_vma=False,
    )
```

```python
import functools

import jax
import jax.numpy as jnp
from jax import lax
from jax.experimental import pallas as pl
from jax.experimental.pallas import tpu as pltpu
from jax.sharding import PartitionSpec as P

GROUPS = 8
FAR_PARTS = 2
COL_PARTS = 2

highest = lax.Precision.HIGHEST
f32, bf16 = jnp.float32, jnp.bfloat16


def swap(value, step):
    size = lax.axis_size("dp")
    return lax.ppermute(value, "dp", [(d, d ^ step) for d in range(size)])


def after(value, *earlier):
    return lax.optimization_barrier((value,) + earlier)[0]


def relay(block):
    size = lax.axis_size("tensor")
    up, down = [block], [block]
    for step in range(1, size):
        up.append(
            lax.ppermute(up[-1], "tensor", [(t, t + 1) for t in range(step - 1, size - 1)])
        )
        down.append(
            lax.ppermute(down[-1], "tensor", [(t, t - 1) for t in range(1, size - step + 1)])
        )
    return [block] + up[1:] + down[1:]


def terms_kernel(size, place_ref, *refs):
    blocks, (w_ref, out_ref, feats) = refs[: 2 * size - 1], refs[2 * size - 1 :]
    own, up, down = blocks[0], blocks[1:size], blocks[size:]
    width = own.shape[1]

    @pl.when(pl.program_id(0) == 0)
    def _():
        place = place_ref[0]

        def put(source, value):
            feats[:, pl.ds(pl.multiple_of(source * width, width), width)] = value

        put(place, own[...])
        for step in range(1, size):
            source = lax.rem(place - step + size, size)

            @pl.when(place >= step)
            def _():
                put(source, up[step - 1][...])

            @pl.when(place < step)
            def _():
                put(source, down[size - step - 1][...])

    weight = w_ref[...].reshape(size * width, w_ref.shape[3])
    out_ref[...] = jnp.dot(feats[...], weight, preferred_element_type=f32).astype(bf16)


def block_terms(blocks, down_weight, col_start, cols):
    size, _, width, _ = down_weight.shape
    rows = blocks[0].shape[0]
    tile = max(n for n in range(128, 1025, 128) if cols % n == 0 and n <= 512)
    first = col_start // tile
    whole = pl.BlockSpec((rows, width), lambda j, place: (0, 0))
    return pl.pallas_call(
        functools.partial(terms_kernel, size),
        out_shape=jax.ShapeDtypeStruct((rows, cols), bf16),
        grid_spec=pltpu.PrefetchScalarGridSpec(
            num_scalar_prefetch=1,
            grid=(cols // tile,),
            in_specs=[whole] * len(blocks)
            + [pl.BlockSpec((size, 1, width, tile), lambda j, place: (0, 0, 0, j + first))],
            out_specs=pl.BlockSpec((rows, tile), lambda j, place: (0, j)),
            scratch_shapes=[pltpu.VMEM((rows, size * width), bf16)],
        ),
        compiler_params=pltpu.CompilerParams(vmem_limit_bytes=32 << 20),
        cost_estimate=pl.CostEstimate(
            flops=2 * rows * size * width * cols,
            bytes_accessed=2 * (size * width * (cols + rows) + rows * cols),
            transcendentals=0,
        ),
        name="terms",
    )(lax.axis_index("tensor").reshape(1), *blocks, down_weight)


def gathered_terms(gathered, down_weight, col_start, cols):
    weight = lax.slice_in_dim(down_weight, col_start, col_start + cols, axis=3)
    return lax.dot_general(
        gathered, weight[:, 0], (((0, 2), (0, 1)), ((), ())), preferred_element_type=f32
    ).astype(bf16)


def add(*values):
    total = values[0].astype(f32)
    for value in values[1:]:
        total = total + value.astype(f32)
    return total.astype(bf16)


def hidden_gradient(output_grad, down_weight):
    groups, cols = lax.axis_size("dp"), down_weight.shape[3]
    place = lax.axis_index("dp")
    line = lax.axis_size("tensor") <= 8 and down_weight.shape[2] % 128 == 0
    col_parts = COL_PARTS if cols % (256 * COL_PARTS) == 0 else 1
    part = cols // col_parts

    def spread(block):
        return relay(block) if line else lax.all_gather(block, "tensor", axis=0)

    def multiply(blocks, at):
        return (block_terms if line else gathered_terms)(blocks, down_weight, at * part, part)

    turned = jnp.transpose(output_grad[0], (0, 2, 1))
    pieces = [
        lax.dynamic_index_in_dim(turned, place ^ step, 0, keepdims=False) for step in range(groups)
    ]
    tokens = pieces[0].shape[0]
    rows = tokens // FAR_PARTS

    blocks = []
    for half in range(FAR_PARTS):
        cut = slice(half * rows, (half + 1) * rows)
        for step in range(2, groups, 2):
            sent = [swap(pieces[step + 1][cut], step + 1), swap(pieces[step][cut], step)]
            blocks.append(jnp.concatenate(sent))
    blocks.append(swap(pieces[1], 1))
    blocks.append(pieces[0])
    lines = []
    for block in blocks:
        if lines:
            last = lines[-1]
            block = after(block, last[len(last) // 2], last[-2]) if line else after(block, last)
        lines.append(spread(block))

    calls = [(index, at) for index in range(len(lines)) for at in range(col_parts)]
    far_calls = (len(lines) - 2) * col_parts
    terms, pairs, sums, near_pairs = {}, [], {}, {}
    for count, (index, at) in enumerate(calls):
        held = lines[index]
        if count >= 2:
            ready = pairs[count - 2]
            held = [after(held[0], ready)] + held[1:] if line else after(held, ready)
        both = multiply(held, at)
        if count < far_calls:
            half, step = divmod(index, groups // 2 - 1)
            pair = add(both[rows:], swap(both[:rows], 1))
            sums.setdefault((half, at), []).append(swap(pair, 2 * step + 2))
            pairs.append(pair)
        else:
            terms[index, at] = both
            if index == len(lines) - 2:
                near_pairs[at] = swap(both, 1)
                pairs.append(both)
    result = jnp.zeros((tokens, cols), bf16)
    for (half, at), arrived in sums.items():
        cut = slice(half * rows, (half + 1) * rows)
        value = add(terms[len(lines) - 1, at][cut], near_pairs[at][cut], *arrived)
        result = lax.dynamic_update_slice(result, value, (half * rows, at * part))
    return result, pairs[0]


def example_gradients(acts_low, grads_low, local_ids, examples):
    onehot = (local_ids[:, None] == jnp.arange(examples, dtype=jnp.int32)[None, :]).astype(f32)
    counts = jnp.sum(onehot, axis=0)
    spread = (onehot[:, :, None] * acts_low[:, None, :]).reshape(onehot.shape[0], -1)
    outer_sum = lax.dot_general(
        spread,
        grads_low,
        (((0,), (0,)), ((), ())),
        precision=highest,
        preferred_element_type=f32,
    )
    basis_rank = acts_low.shape[1]
    outer_sum = outer_sum.reshape(examples, basis_rank * grads_low.shape[1]) / counts[:, None]
    return outer_sum.astype(bf16)


def fisher_and_groups(example_grad, example_group):
    flat_width = example_grad.shape[1]
    row_count = flat_width // lax.axis_size("dp")
    col_count = flat_width // lax.axis_size("tensor")
    col_start = lax.axis_index("tensor") * col_count
    row_start = lax.axis_index("dp") * row_count
    group_column = jnp.broadcast_to(
        example_group.astype(bf16)[:, None], (example_grad.shape[0], 128)
    )
    held = jnp.concatenate([example_grad, group_column], axis=1)
    every = jnp.concatenate(
        [held] + [swap(held, step) for step in range(1, lax.axis_size("dp"))], axis=0
    )
    every_group = every[:, flat_width].astype(jnp.int32)
    rows_part = lax.dynamic_slice_in_dim(every, row_start, row_count, 1)
    cols_part = lax.dynamic_slice_in_dim(every, col_start, col_count, 1)
    fisher = lax.dot_general(
        rows_part, cols_part, (((0,), (0,)), ((), ())), preferred_element_type=f32
    )
    member = (every_group[:, None] == jnp.arange(GROUPS, dtype=jnp.int32)[None, :]).astype(bf16)
    group_grad = lax.dot_general(
        member, cols_part, (((0,), (0,)), ((), ())), preferred_element_type=f32
    )
    return fisher, group_grad


def per_device(
    hidden_acts, output_grad, down_weight, input_basis, output_basis, token_example, example_group
):
    hidden_grad, first_pair = hidden_gradient(output_grad, down_weight)
    acts_part = jnp.dot(hidden_acts, input_basis, preferred_element_type=f32)
    grads_part = lax.dot_general(
        output_grad,
        output_basis,
        (((0, 1, 2), (0, 1, 2)), ((), ())),
        preferred_element_type=f32,
    )
    acts_low, grads_low = lax.psum((acts_part, grads_part), "tensor")
    acts_low = after(acts_low, first_pair)
    grads_low = after(grads_low, first_pair)
    example_grad = example_gradients(acts_low, grads_low, token_example[0], example_group.shape[0])
    fisher, group_grad = fisher_and_groups(example_grad, example_group)
    return (hidden_grad, fisher, group_grad)


def solution(mesh):
    return jax.shard_map(
        per_device,
        mesh=mesh,
        in_specs=(
            P(("parts", "dp"), "tensor"),
            P("tensor", None, None, ("parts", "dp")),
            P(None, "dp", None, "tensor"),
            P("tensor", None),
            P("tensor", None, None, None),
            P(("parts", "dp"), None),
            P(("parts", "dp")),
        ),
        out_specs=(
            P(("parts", "dp"), "tensor"),
            P(("parts", "dp"), "tensor"),
            P("parts", "tensor"),
        ),
        check_vma=False,
    )
```

```python
import functools

import jax
import jax.numpy as jnp
from jax import lax
from jax.experimental import pallas as pl
from jax.experimental.pallas import tpu as pltpu
from jax.sharding import PartitionSpec as P

GROUPS = 8
FAR_PARTS = 2
COL_PARTS = 2

highest = lax.Precision.HIGHEST
f32, bf16 = jnp.float32, jnp.bfloat16


def swap(value, step):
    size = lax.axis_size("dp")
    return lax.ppermute(value, "dp", [(d, d ^ step) for d in range(size)])


def after(value, *earlier):
    return lax.optimization_barrier((value,) + earlier)[0]


def across(value, step, places=None):
    size = lax.axis_size("tensor")
    pairs = [(t, t ^ step) for t in range(size) if places is None or t in places]
    return lax.ppermute(value, "tensor", pairs)


def spread(block):
    second = across(block, 2)
    first = across(block, 1)
    middle = across(block, 3, (1, 2))
    ends = across(second, 1, (1, 2))
    return [block, first, second, middle, ends]


def terms_kernel(size, count, first, place_ref, *refs):
    blocks, (w_ref, out_ref, feats, held, sems, held_sems) = refs[:count], refs[count:]
    width, tile = feats.shape[1] // size, out_ref.shape[1]
    j, steps = pl.program_id(0), pl.num_programs(0)
    slots = held.shape[0]

    def put(value, source, slot):
        at = pl.ds(pl.multiple_of(source * width, width), width)
        return pltpu.make_async_copy(value, feats.at[:, at], sems.at[slot])

    def fetch(step):
        slot = lax.rem(step, slots)
        at = pl.ds(pl.multiple_of(first + step * tile, tile), tile)
        return pltpu.make_async_copy(w_ref.at[:, 0, :, at], held.at[slot], held_sems.at[slot])

    @pl.when(j == 0)
    def _():
        for step in range(slots):

            @pl.when(step < steps)
            def _():
                fetch(step).start()

        if count == 1:
            copies = [put(blocks[0].at[source], source, source) for source in range(size)]
            for copy in copies:
                copy.start()
            for copy in copies:
                copy.wait()
        else:
            place = place_ref[0]
            copies = [put(blocks[step], lax.bitwise_xor(place, step), step) for step in range(3)]
            for copy in copies:
                copy.start()
            inside = jnp.logical_or(place == 1, place == 2)
            for chosen, block in ((inside, blocks[3]), (jnp.logical_not(inside), blocks[4])):

                @pl.when(chosen)
                def _():
                    last = put(block, lax.bitwise_xor(place, 3), 3)
                    last.start()
                    last.wait()

            for copy in copies:
                copy.wait()

    fetch(j).wait()
    weight = held[lax.rem(j, slots)].reshape(size * width, tile)
    out_ref[...] = jnp.dot(feats[...], weight, preferred_element_type=f32).astype(bf16)

    @pl.when(j + slots < steps)
    def _():
        fetch(j + slots).start()


def block_terms(blocks, down_weight, col_start, cols):
    size, _, width, _ = down_weight.shape
    rows = blocks[-1].shape[-2]
    tile = max(n for n in range(128, 513, 128) if cols % n == 0)
    slots = min(4, cols // tile)
    return pl.pallas_call(
        functools.partial(terms_kernel, size, len(blocks), col_start),
        out_shape=jax.ShapeDtypeStruct((rows, cols), bf16),
        grid_spec=pltpu.PrefetchScalarGridSpec(
            num_scalar_prefetch=1,
            grid=(cols // tile,),
            in_specs=[pl.BlockSpec(memory_space=pl.ANY)] * (len(blocks) + 1),
            out_specs=pl.BlockSpec((rows, tile), lambda j, place: (0, j)),
            scratch_shapes=[
                pltpu.VMEM((rows, size * width), bf16),
                pltpu.VMEM((slots, size, width, tile), bf16),
                pltpu.SemaphoreType.DMA((size,)),
                pltpu.SemaphoreType.DMA((slots,)),
            ],
        ),
        compiler_params=pltpu.CompilerParams(vmem_limit_bytes=40 << 20),
        cost_estimate=pl.CostEstimate(flops=1000, bytes_accessed=1000, transcendentals=0),
        name="terms",
    )(lax.axis_index("tensor").reshape(1), *blocks, down_weight)


def gathered_terms(blocks, down_weight, col_start, cols):
    weight = lax.slice_in_dim(down_weight, col_start, col_start + cols, axis=3)
    return lax.dot_general(
        blocks[0], weight[:, 0], (((0, 2), (0, 1)), ((), ())), preferred_element_type=f32
    ).astype(bf16)


def add(*values):
    total = values[0].astype(f32)
    for value in values[1:]:
        total = total + value.astype(f32)
    return total.astype(bf16)


def far_features(output_grad):
    groups, place = lax.axis_size("dp"), lax.axis_index("dp")
    line = lax.axis_size("tensor") == 4

    def gather(block):
        return [lax.all_gather(block, "tensor", axis=0)]

    turned = jnp.transpose(output_grad[0], (0, 2, 1))
    pieces = [
        lax.dynamic_index_in_dim(turned, place ^ step, 0, keepdims=False) for step in range(groups)
    ]
    rows = pieces[0].shape[0] // FAR_PARTS
    far, beside = [], None
    last = None
    for half in range(FAR_PARTS):
        cut = slice(half * rows, (half + 1) * rows)
        for step in range(2, groups, 2):
            sent = [swap(pieces[step + 1][cut], step + 1), swap(pieces[step][cut], step)]
            block = jnp.concatenate(sent)
            if last is not None:
                block = after(block, last)
            far.append((half, step, spread(block) if line else gather(block)))
            last = far[-1][2][2] if line else far[-1][2][0]
            if beside is None:
                beside = swap(after(pieces[1], last), 1)
                far[0] = far[0][:2] + ([after(far[0][2][0], beside)] + far[0][2][1:],)
    beside = gather(after(beside, last))
    own = gather(after(pieces[0], last))
    return far, beside, own, last


def example_gradients(acts_low, grads_low, local_ids, examples):
    onehot = (local_ids[:, None] == jnp.arange(examples, dtype=jnp.int32)[None, :]).astype(f32)
    counts = jnp.sum(onehot, axis=0)
    spread = (onehot[:, :, None] * acts_low[:, None, :]).reshape(onehot.shape[0], -1)
    outer_sum = lax.dot_general(
        spread,
        grads_low,
        (((0,), (0,)), ((), ())),
        precision=highest,
        preferred_element_type=f32,
    )
    basis_rank = acts_low.shape[1]
    outer_sum = outer_sum.reshape(examples, basis_rank * grads_low.shape[1]) / counts[:, None]
    return outer_sum.astype(bf16)


def gather_examples(example_grad, example_group):
    count, width = example_grad.shape
    groups = lax.axis_size("dp")
    group_column = jnp.broadcast_to(example_group.astype(bf16)[:, None], (count, 128))
    held = jnp.concatenate([example_grad, group_column], axis=1)
    every = jnp.zeros((groups * count, width + 128), bf16)
    for step in range(groups):
        value = swap(held, step) if step else held
        row = (lax.axis_index("dp") ^ step) * count
        every = lax.dynamic_update_slice_in_dim(every, value, row, 0)
    return every


def fisher_and_groups(every, flat_width):
    row_count = flat_width // lax.axis_size("dp")
    col_count = flat_width // lax.axis_size("tensor")
    col_start = lax.axis_index("tensor") * col_count
    row_start = lax.axis_index("dp") * row_count
    every_group = every[:, flat_width].astype(jnp.int32)
    rows_part = lax.dynamic_slice_in_dim(every, row_start, row_count, 1)
    cols_part = lax.dynamic_slice_in_dim(every, col_start, col_count, 1)
    fisher = lax.dot_general(
        rows_part, cols_part, (((0,), (0,)), ((), ())), preferred_element_type=f32
    )
    member = (every_group[:, None] == jnp.arange(GROUPS, dtype=jnp.int32)[None, :]).astype(bf16)
    group_grad = lax.dot_general(
        member, cols_part, (((0,), (0,)), ((), ())), preferred_element_type=f32
    )
    return fisher, group_grad


def per_device(
    hidden_acts, output_grad, down_weight, input_basis, output_basis, token_example, example_group
):
    tokens, cols = hidden_acts.shape
    col_parts = COL_PARTS if cols % (256 * COL_PARTS) == 0 else 1
    part, rows = cols // col_parts, tokens // FAR_PARTS
    far, beside, own, last = far_features(output_grad)

    def multiply(blocks, at):
        kernel = block_terms if down_weight.shape[2] % 128 == 0 else gathered_terms
        return kernel(blocks, down_weight, at * part, part)

    acts_part = jnp.dot(hidden_acts, input_basis, preferred_element_type=f32)
    grads_part = lax.dot_general(
        output_grad,
        output_basis,
        (((0, 1, 2), (0, 1, 2)), ((), ())),
        preferred_element_type=f32,
    )
    parts = jnp.concatenate([acts_part, grads_part], axis=1)
    if lax.axis_size("tensor") == 4:
        low = parts = after(parts, last)
        far[0] = far[0][:2] + ([after(far[0][2][0], parts)] + far[0][2][1:],)
        for step in (1, 2):
            low = low + across(low, step)
    else:
        low = lax.psum(parts, "tensor")

    units = [(blocks, half, step, at) for half, step, blocks in far for at in range(col_parts)]
    held, pairs, arrived = [], [], []

    def settle(latest):
        count = len(pairs)
        both, other = held[count]
        pairs.append(add(after(both[rows:], latest), other))
        arrived.append(swap(pairs[count], units[count][2]))

    for count, (blocks, half, step, at) in enumerate(units):
        earlier = pairs[-1:] + arrived[:-1][-1:]
        if count == 1:
            earlier = earlier + far[-1][2] + [every]
        if count == 3:
            earlier.append(beside[0])
        if earlier:
            blocks = [after(blocks[0], *earlier)] + blocks[1:]
        both = multiply(blocks, at)
        held.append((both, swap(both[:rows], 1)))
        if count == 0:
            acts_low, grads_low = jnp.split(after(low, both), 2, axis=1)
            example_grad = example_gradients(
                acts_low, grads_low, token_example[0], example_group.shape[0]
            )
            every = gather_examples(example_grad, example_group)
        else:
            settle(both)

    near = []
    for at in range(col_parts):
        earlier = pairs[-1:] + arrived[:-1][-1:] + [own[0]]
        term = multiply([after(beside[0], *earlier)], at)
        near.append(swap(term, 1))
        if at == 0:
            settle(term)
    fisher, group_grad = fisher_and_groups(after(every, term), example_grad.shape[1])
    result = jnp.zeros((tokens, cols), bf16)
    for at in range(col_parts):
        earlier = [near[at], term] + ([arrived[-1]] if at == col_parts - 1 else [])
        term = multiply([after(own[0], *earlier)], at)
        for half in range(FAR_PARTS):
            sums = [
                arrived[count] for count, unit in enumerate(units) if unit[1:] == (half, unit[2], at)
            ]
            cut = slice(half * rows, (half + 1) * rows)
            value = add(term[cut], near[at][cut], *sums)
            result = lax.dynamic_update_slice(result, value, (half * rows, at * part))
    return (result, fisher, group_grad)


def solution(mesh):
    return jax.shard_map(
        per_device,
        mesh=mesh,
        in_specs=(
            P(("parts", "dp"), "tensor"),
            P("tensor", None, None, ("parts", "dp")),
            P(None, "dp", None, "tensor"),
            P("tensor", None),
            P("tensor", None, None, None),
            P(("parts", "dp"), None),
            P(("parts", "dp")),
        ),
        out_specs=(
            P(("parts", "dp"), "tensor"),
            P(("parts", "dp"), "tensor"),
            P("parts", "tensor"),
        ),
        check_vma=False,
    )
```

```python
import functools

import jax
import jax.numpy as jnp
from jax import lax
from jax.experimental import pallas as pl
from jax.experimental.layout import Layout, with_layout_constraint
from jax.experimental.pallas import tpu as pltpu
from jax.sharding import PartitionSpec as P

GROUPS = 8
FAR_PARTS = 2
COL_PARTS = 2

highest = lax.Precision.HIGHEST
f32, bf16 = jnp.float32, jnp.bfloat16


def swap(value, step):
    size = lax.axis_size("dp")
    return lax.ppermute(value, "dp", [(d, d ^ step) for d in range(size)])


def after(value, *earlier):
    return lax.optimization_barrier((value,) + earlier)[0]


def across(value, step, places=None):
    size = lax.axis_size("tensor")
    pairs = [(t, t ^ step) for t in range(size) if places is None or t in places]
    return lax.ppermute(value, "tensor", pairs)


def spread(block):
    second = across(block, 2)
    first = across(block, 1)
    middle = across(block, 3, (1, 2))
    ends = across(second, 1, (1, 2))
    return [block, first, second, middle, ends]


def terms_kernel(size, count, first, place_ref, *refs):
    blocks, w_ref, outs = refs[:count], refs[count], refs[count + 1 : -4]
    feats, held, sems, held_sems = refs[-4:]
    width, tile = feats.shape[1] // size, outs[0].shape[1]
    j, steps = pl.program_id(0), pl.num_programs(0)
    slots = held.shape[0]

    def put(value, source, slot):
        at = pl.ds(pl.multiple_of(source * width, width), width)
        return pltpu.make_async_copy(value, feats.at[:, at], sems.at[slot])

    def fetch(step):
        slot = lax.rem(step, slots)
        at = pl.ds(pl.multiple_of(first + step * tile, tile), tile)
        return pltpu.make_async_copy(w_ref.at[:, 0, :, at], held.at[slot], held_sems.at[slot])

    @pl.when(j == 0)
    def _():
        for step in range(slots):

            @pl.when(step < steps)
            def _():
                fetch(step).start()

        if count == 1:
            copies = [put(blocks[0].at[source], source, source) for source in range(size)]
            for copy in copies:
                copy.start()
            for copy in copies:
                copy.wait()
        else:
            place = place_ref[0]
            copies = [put(blocks[step], lax.bitwise_xor(place, step), step) for step in range(3)]
            for copy in copies:
                copy.start()
            inside = jnp.logical_or(place == 1, place == 2)
            for chosen, block in ((inside, blocks[3]), (jnp.logical_not(inside), blocks[4])):

                @pl.when(chosen)
                def _():
                    last = put(block, lax.bitwise_xor(place, 3), 3)
                    last.start()
                    last.wait()

            for copy in copies:
                copy.wait()

    fetch(j).wait()
    weight = held[lax.rem(j, slots)].reshape(size * width, tile)
    total = jnp.dot(feats[...], weight, preferred_element_type=f32).astype(bf16)
    rows = outs[0].shape[0]
    for index, out_ref in enumerate(outs):
        out_ref[...] = total[index * rows : (index + 1) * rows]

    @pl.when(j + slots < steps)
    def _():
        fetch(j + slots).start()


def block_terms(blocks, down_weight, col_start, cols, outs):
    size, _, width, _ = down_weight.shape
    rows = blocks[-1].shape[-2]
    tile = max(n for n in range(128, 513, 128) if cols % n == 0)
    slots = min(4, cols // tile)
    return pl.pallas_call(
        functools.partial(terms_kernel, size, len(blocks), col_start),
        out_shape=[jax.ShapeDtypeStruct((rows // outs, cols), bf16)] * outs,
        grid_spec=pltpu.PrefetchScalarGridSpec(
            num_scalar_prefetch=1,
            grid=(cols // tile,),
            in_specs=[pl.BlockSpec(memory_space=pl.ANY)] * (len(blocks) + 1),
            out_specs=[pl.BlockSpec((rows // outs, tile), lambda j, place: (0, j))] * outs,
            scratch_shapes=[
                pltpu.VMEM((rows, size * width), bf16),
                pltpu.VMEM((slots, size, width, tile), bf16),
                pltpu.SemaphoreType.DMA((size,)),
                pltpu.SemaphoreType.DMA((slots,)),
            ],
        ),
        compiler_params=pltpu.CompilerParams(vmem_limit_bytes=40 << 20),
        cost_estimate=pl.CostEstimate(flops=8 * rows * size * width * cols, bytes_accessed=1000, transcendentals=0),
        name="terms",
    )(lax.axis_index("tensor").reshape(1), *blocks, down_weight)


def gathered_terms(blocks, down_weight, col_start, cols, outs):
    weight = lax.slice_in_dim(down_weight, col_start, col_start + cols, axis=3)
    terms = lax.dot_general(
        blocks[0], weight[:, 0], (((0, 2), (0, 1)), ((), ())), preferred_element_type=f32
    )
    return jnp.split(terms.astype(bf16), outs)


def add(*values):
    total = values[0].astype(f32)
    for value in values[1:]:
        total = total + value.astype(f32)
    return total.astype(bf16)


def far_features(output_grad, parts):
    groups, place = lax.axis_size("dp"), lax.axis_index("dp")
    line = lax.axis_size("tensor") == 4

    def gather(block):
        block = with_layout_constraint(block, Layout(major_to_minor=(0, 1)))
        return [lax.all_gather(block, "tensor", axis=0)]

    turned = jnp.transpose(output_grad[0], (0, 2, 1))
    pieces = [
        lax.dynamic_index_in_dim(turned, place ^ step, 0, keepdims=False) for step in range(groups)
    ]
    rows = pieces[0].shape[0] // FAR_PARTS
    far, beside = [], None
    last = None
    for half in range(FAR_PARTS):
        cut = slice(half * rows, (half + 1) * rows)
        for step in range(2, groups, 2):
            sent = [swap(pieces[step + 1][cut], step + 1), swap(pieces[step][cut], step)]
            block = after(jnp.concatenate(sent), *([parts] if last is None else last))
            far.append((half, step, spread(block) if line else gather(block)))
            last = far[-1][2][1:4] if line else far[-1][2]
            if beside is None:
                beside = swap(after(pieces[1], *last), 1)
                far[0] = far[0][:2] + ([after(far[0][2][0], beside)] + far[0][2][1:],)
    beside = gather(after(beside, far[0][2][-1]))
    own = gather(after(pieces[0], far[0][2][-1]))
    return far, beside, own


def example_gradients(acts_low, grads_low, local_ids, examples):
    onehot = (local_ids[:, None] == jnp.arange(examples, dtype=jnp.int32)[None, :]).astype(f32)
    counts = jnp.sum(onehot, axis=0)
    spread = (onehot[:, :, None] * acts_low[:, None, :]).reshape(onehot.shape[0], -1)
    outer_sum = lax.dot_general(
        spread,
        grads_low,
        (((0,), (0,)), ((), ())),
        precision=highest,
        preferred_element_type=f32,
    )
    basis_rank = acts_low.shape[1]
    outer_sum = outer_sum.reshape(examples, basis_rank * grads_low.shape[1]) / counts[:, None]
    return outer_sum.astype(bf16)


def gather_examples(example_grad, example_group):
    count = example_grad.shape[0]
    groups, place = lax.axis_size("dp"), lax.axis_index("dp")
    group_column = jnp.broadcast_to(example_group.astype(bf16)[:, None], (count, 128))
    held = jnp.concatenate([example_grad, group_column], axis=1)
    values = [held] + [swap(held, step) for step in range(1, groups)]
    ordered = []
    for group in range(groups):
        value = values[0]
        for step in range(1, groups):
            value = jnp.where((place ^ group) == step, values[step], value)
        ordered.append(value)
    return jnp.concatenate(ordered, axis=0)


def fisher_and_groups(every, flat_width):
    row_count = flat_width // lax.axis_size("dp")
    col_count = flat_width // lax.axis_size("tensor")
    col_start = lax.axis_index("tensor") * col_count
    row_start = lax.axis_index("dp") * row_count
    every_group = every[:, flat_width].astype(jnp.int32)
    rows_part = lax.dynamic_slice_in_dim(every, row_start, row_count, 1)
    cols_part = lax.dynamic_slice_in_dim(every, col_start, col_count, 1)
    fisher = lax.dot_general(
        rows_part, cols_part, (((0,), (0,)), ((), ())), preferred_element_type=f32
    )
    member = (every_group[:, None] == jnp.arange(GROUPS, dtype=jnp.int32)[None, :]).astype(bf16)
    group_grad = lax.dot_general(
        member, cols_part, (((0,), (0,)), ((), ())), preferred_element_type=f32
    )
    return fisher, group_grad


def per_device(
    hidden_acts, output_grad, down_weight, input_basis, output_basis, token_example, example_group
):
    tokens, cols = hidden_acts.shape
    col_parts = COL_PARTS if cols % (256 * COL_PARTS) == 0 else 1
    part, rows = cols // col_parts, tokens // FAR_PARTS

    def multiply(blocks, at, outs=2, width=part):
        kernel = block_terms if down_weight.shape[2] % 128 == 0 else gathered_terms
        return kernel(blocks, down_weight, at * part, width, outs)

    acts_part = jnp.dot(hidden_acts, input_basis, preferred_element_type=f32)
    grads_part = lax.dot_general(
        output_grad,
        output_basis,
        (((0, 1, 2), (0, 1, 2)), ((), ())),
        preferred_element_type=f32,
    )
    parts = jnp.concatenate([acts_part, grads_part], axis=1)
    far, beside, own = far_features(output_grad, parts)
    if lax.axis_size("tensor") == 4:
        low = after(parts, far[0][2][-1])
        for step in (1, 2):
            low = low + across(low, step)
    else:
        low = lax.psum(parts, "tensor")

    units = [(blocks, half, step, at) for half, step, blocks in far for at in range(col_parts)]
    held, pairs, arrived = [], [], []

    def settle(latest):
        count = len(pairs)
        pairs.append(add(after(held[count][0], latest), held[count][1]))
        arrived.append(swap(pairs[count], units[count][2]))

    for count, (blocks, half, step, at) in enumerate(units):
        earlier = pairs[-1:] + arrived[:-1][-1:]
        if count == len(units) - 1:
            acts_low, grads_low = jnp.split(after(low, *arrived[:-1][-1:]), 2, axis=1)
            example_grad = example_gradients(
                acts_low, grads_low, token_example[0], example_group.shape[0]
            )
            every = gather_examples(example_grad, example_group)
            earlier += [beside[0], every]
        if earlier:
            blocks = [after(blocks[0], *earlier)] + blocks[1:]
        sent, both = multiply(blocks, at)
        held.append((both, swap(sent, 1)))
        if count:
            settle(both)

    fisher, group_grad = fisher_and_groups(after(every, arrived[-2]), example_grad.shape[1])
    beside = [after(beside[0], pairs[-1], arrived[-2], fisher, group_grad)]
    near = multiply(beside, 0, FAR_PARTS, cols)
    settle(near[0])
    near = [swap(term, 1) for term in near]
    own = [after(own[0], pairs[-1], arrived[-2])]
    mine = multiply(own, 0, FAR_PARTS, cols)
    result = jnp.zeros((tokens, cols), bf16)
    for half in range(FAR_PARTS):
        for at in range(col_parts):
            sums = [
                arrived[count] for count, unit in enumerate(units) if unit[1:] == (half, unit[2], at)
            ]
            cut = slice(at * part, (at + 1) * part)
            value = add(mine[half][:, cut], near[half][:, cut], *sums)
            result = lax.dynamic_update_slice(result, value, (half * rows, at * part))
    return (result, fisher, group_grad)


def solution(mesh):
    return jax.shard_map(
        per_device,
        mesh=mesh,
        in_specs=(
            P(("parts", "dp"), "tensor"),
            P("tensor", None, None, ("parts", "dp")),
            P(None, "dp", None, "tensor"),
            P("tensor", None),
            P("tensor", None, None, None),
            P(("parts", "dp"), None),
            P(("parts", "dp")),
        ),
        out_specs=(
            P(("parts", "dp"), "tensor"),
            P(("parts", "dp"), "tensor"),
            P("parts", "tensor"),
        ),
        check_vma=False,
    )
```

```python
import functools

import jax
import jax.numpy as jnp
from jax import lax
from jax.experimental import pallas as pl
from jax.experimental.layout import Layout, with_layout_constraint
from jax.experimental.pallas import tpu as pltpu
from jax.sharding import PartitionSpec as P

GROUPS = 8
FAR_PARTS = 2

highest = lax.Precision.HIGHEST
f32, bf16 = jnp.float32, jnp.bfloat16


def swap(value, step):
    size = lax.axis_size("dp")
    return lax.ppermute(value, "dp", [(d, d ^ step) for d in range(size)])


def after(value, *earlier):
    return lax.optimization_barrier((value,) + earlier)[0]


def across(value, step, places=None):
    size = lax.axis_size("tensor")
    pairs = [(t, t ^ step) for t in range(size) if places is None or t in places]
    return lax.ppermute(value, "tensor", pairs)


def spread(block, *earlier):
    second = across(block, 2)
    first = across(block, 1)
    middle = across(after(block, second, *earlier), 3, (1, 2))
    ends = across(second, 1, (1, 2))
    return [block, first, second, middle, ends]


def terms_kernel(size, counts, first, lead, split, place_ref, *refs):
    total = sum(counts)
    groups, at = [], 0
    for count in counts:
        groups.append(refs[at : at + count])
        at += count
    w_ref, outs = refs[total], refs[total + 1 : -4]
    feats, held, sems, held_sems = refs[-4:]
    width, tile = feats.shape[1] // size, outs[0].shape[1]
    tall = feats.shape[0] // len(groups)
    j, steps = pl.program_id(0), pl.num_programs(0)
    slots = held.shape[0]

    def put(value, group, source, slot):
        at = pl.ds(pl.multiple_of(source * width, width), width)
        rows = pl.ds(group * tall, tall)
        return pltpu.make_async_copy(value, feats.at[rows, at], sems.at[group * size + slot])

    def fetch(step):
        slot = lax.rem(step, slots)
        at = pl.ds(pl.multiple_of(first + step * tile, tile), tile)
        return pltpu.make_async_copy(w_ref.at[:, 0, :, at], held.at[slot], held_sems.at[slot])

    @pl.when(j == 0)
    def _():
        copies = []
        place = place_ref[0]
        for group, blocks in enumerate(groups):
            if len(blocks) == 1:
                copies += [put(blocks[0].at[k], group, k, k) for k in range(size)]
            else:
                copies += [put(blocks[k], group, lax.bitwise_xor(place, k), k) for k in range(3)]
        for copy in copies:
            copy.start()
        for step in range(slots):
            fetch(step).start()
        inside = jnp.logical_or(place == 1, place == 2)
        for group, blocks in enumerate(groups):
            if len(blocks) == 1:
                continue
            for chosen, block in ((inside, blocks[3]), (jnp.logical_not(inside), blocks[4])):

                @pl.when(chosen)
                def _():
                    last = put(block, group, lax.bitwise_xor(place, 3), 3)
                    last.start()
                    last.wait()

        for copy in copies:
            copy.wait()

    fetch(j).wait()
    weight = held[lax.rem(j, slots)].reshape(size * width, tile)

    def multiply(outs):
        rows = sum(out_ref.shape[0] for out_ref in outs)
        terms = jnp.dot(feats[:rows], weight, preferred_element_type=f32).astype(bf16)
        row = 0
        for out_ref in outs:
            out_ref[...] = terms[row : row + out_ref.shape[0]]
            row += out_ref.shape[0]

    if split is None:
        multiply(outs)
    else:
        pl.when(j < split)(lambda: multiply(outs))
        pl.when(j >= split)(lambda: multiply(outs[:lead]))

    @pl.when(j + slots < steps)
    def _():
        fetch(j + slots).start()


def block_terms(groups, down_weight, col_start, cols, outs, lead=None, lead_cols=None):
    size, _, width, _ = down_weight.shape
    rows = sum(outs)
    wide = [cols if lead is None or k < lead else lead_cols for k in range(len(outs))]
    tile = max(n for n in range(128, 513, 128) if cols % n == 0)
    slots = min(4, cols // tile)
    split = None if lead is None else lead_cols // tile
    blocks = [block for group in groups for block in group]

    def out_at(count):
        return lambda j, place: (0, jnp.minimum(j, count - 1))

    return pl.pallas_call(
        functools.partial(
            terms_kernel, size, [len(group) for group in groups], col_start, lead, split
        ),
        out_shape=[jax.ShapeDtypeStruct((tall, n), bf16) for tall, n in zip(outs, wide)],
        grid_spec=pltpu.PrefetchScalarGridSpec(
            num_scalar_prefetch=1,
            grid=(cols // tile,),
            in_specs=[pl.BlockSpec(memory_space=pl.ANY)] * (len(blocks) + 1),
            out_specs=[pl.BlockSpec((tall, tile), out_at(n // tile)) for tall, n in zip(outs, wide)],
            scratch_shapes=[
                pltpu.VMEM((rows, size * width), bf16),
                pltpu.VMEM((slots, size, width, tile), bf16),
                pltpu.SemaphoreType.DMA((len(groups) * size,)),
                pltpu.SemaphoreType.DMA((slots,)),
            ],
        ),
        compiler_params=pltpu.CompilerParams(vmem_limit_bytes=40 << 20),
        cost_estimate=pl.CostEstimate(
            flops=8 * rows * size * width * cols, bytes_accessed=1000, transcendentals=0
        ),
        name="terms",
    )(lax.axis_index("tensor").reshape(1), *blocks, down_weight)


def gathered_terms(groups, down_weight, col_start, cols, outs, lead=None, lead_cols=None):
    weight = lax.slice_in_dim(down_weight, col_start, col_start + cols, axis=3)
    terms = [
        lax.dot_general(
            blocks[0], weight[:, 0], (((0, 2), (0, 1)), ((), ())), preferred_element_type=f32
        )
        for blocks in groups
    ]
    terms = jnp.concatenate(terms).astype(bf16)
    pieces = jnp.split(terms, [sum(outs[:k]) for k in range(1, len(outs))])
    return [
        piece if lead is None or k < lead else piece[:, :lead_cols]
        for k, piece in enumerate(pieces)
    ]


def add_kernel(kept_ref, first_ref, second_ref, out_ref):
    rows = first_ref.shape[0]
    for index, other in enumerate((first_ref, second_ref)):
        cut = slice(index * rows, (index + 1) * rows)
        out_ref[cut] = (kept_ref[cut].astype(f32) + other[...].astype(f32)).astype(bf16)


def add_halves(kept, first, second):
    rows, cols = kept.shape
    tile = max(n for n in range(128, 1025, 128) if cols % n == 0)

    def spec(tall):
        return pl.BlockSpec((tall, tile), lambda j: (0, j))

    return pl.pallas_call(
        add_kernel,
        out_shape=jax.ShapeDtypeStruct((rows, cols), bf16),
        grid=(cols // tile,),
        in_specs=[spec(rows), spec(rows // 2), spec(rows // 2)],
        out_specs=spec(rows),
        compiler_params=pltpu.CompilerParams(vmem_limit_bytes=16 << 20),
        cost_estimate=pl.CostEstimate(flops=1000, bytes_accessed=1000, transcendentals=0),
        name="pair",
    )(kept, first, second)


def finish_kernel(*refs):
    own_ref, halves, others, out_ref = refs[0], refs[1:3], refs[3:-1], refs[-1]
    rows = halves[0].shape[0]
    for index, half_ref in enumerate(halves):
        cut = slice(index * rows, (index + 1) * rows)
        total = own_ref[cut].astype(f32) + half_ref[...].astype(f32)
        for ref in others:
            total = total + ref[cut].astype(f32)
        out_ref[cut] = total.astype(bf16)


def finish(result, halves, others, row, col):
    rows, cols = others[0].shape
    tile = max(n for n in range(128, 1025, 128) if cols % n == 0)
    part = pl.BlockSpec((rows, tile), lambda j: (row // rows, col // tile + j))

    def spec(tall):
        return pl.BlockSpec((tall, tile), lambda j: (0, j))

    return pl.pallas_call(
        finish_kernel,
        out_shape=jax.ShapeDtypeStruct(result.shape, bf16),
        grid=(cols // tile,),
        in_specs=[part] + [spec(rows // 2)] * 2 + [spec(rows)] * len(others),
        out_specs=part,
        input_output_aliases={0: 0},
        compiler_params=pltpu.CompilerParams(vmem_limit_bytes=16 << 20),
        cost_estimate=pl.CostEstimate(flops=1000, bytes_accessed=1000, transcendentals=0),
        name="finish",
    )(result, *halves, *others)


def features(output_grad, parts):
    groups, place = lax.axis_size("dp"), lax.axis_index("dp")
    line = lax.axis_size("tensor") == 4

    def gather(block):
        block = with_layout_constraint(block, Layout(major_to_minor=(0, 1)))
        return [lax.all_gather(block, "tensor", axis=0)]

    turned = jnp.transpose(output_grad[0], (0, 2, 1))
    pieces = [
        lax.dynamic_index_in_dim(turned, place ^ step, 0, keepdims=False) for step in range(groups)
    ]
    rows = pieces[0].shape[0] // FAR_PARTS
    sent = []
    for half in range(FAR_PARTS):
        cut = slice(half * rows, (half + 1) * rows)
        for step in range(2, groups, 2):
            both = [swap(pieces[step + 1][cut], step + 1), swap(pieces[step][cut], step)]
            sent.append(jnp.concatenate(both))
    beside = swap(pieces[1], 1)
    far, last = [], [parts]
    low = parts + across(parts, 1) if line else lax.psum(parts, "tensor")
    for half in range(FAR_PARTS):
        for step in range(2, groups, 2):
            block = after(sent[len(far)], *last)
            early = [] if far else [low, beside] + sent[1:]
            blocks = spread(block, *early) if line else gather(block)
            far.append((half, step, blocks))
            last = blocks[-2:]
            if line and len(far) == 1:
                low = after(low, *last)
                low = low + across(low, 2)
    beside = after(beside, *last)
    beside = spread(beside) if line else gather(beside)
    own = after(pieces[0], *beside[1:3])
    own = spread(own) if line else gather(own)
    return far, beside, own, low


def example_gradients(acts_low, grads_low, local_ids, examples):
    onehot = (local_ids[:, None] == jnp.arange(examples, dtype=jnp.int32)[None, :]).astype(f32)
    counts = jnp.sum(onehot, axis=0)
    spread = (onehot[:, :, None] * acts_low[:, None, :]).reshape(onehot.shape[0], -1)
    outer_sum = lax.dot_general(
        spread,
        grads_low,
        (((0,), (0,)), ((), ())),
        precision=highest,
        preferred_element_type=f32,
    )
    basis_rank = acts_low.shape[1]
    outer_sum = outer_sum.reshape(examples, basis_rank * grads_low.shape[1]) / counts[:, None]
    return outer_sum.astype(bf16)


def gather_examples(example_grad, example_group):
    count = example_grad.shape[0]
    group_column = jnp.broadcast_to(example_group.astype(bf16)[:, None], (count, 128))
    held = jnp.concatenate([example_grad, group_column], axis=1)
    return [held] + [swap(held, step) for step in range(1, lax.axis_size("dp"))]


def order_examples(values):
    groups, place = lax.axis_size("dp"), lax.axis_index("dp")
    ordered = []
    for group in range(groups):
        value = values[0]
        for step in range(1, groups):
            value = jnp.where((place ^ group) == step, values[step], value)
        ordered.append(value)
    return jnp.concatenate(ordered, axis=0)


def fisher_and_groups(every, flat_width):
    row_count = flat_width // lax.axis_size("dp")
    col_count = flat_width // lax.axis_size("tensor")
    col_start = lax.axis_index("tensor") * col_count
    row_start = lax.axis_index("dp") * row_count
    every_group = every[:, flat_width].astype(jnp.int32)
    rows_part = lax.dynamic_slice_in_dim(every, row_start, row_count, 1)
    cols_part = lax.dynamic_slice_in_dim(every, col_start, col_count, 1)
    fisher = lax.dot_general(
        rows_part, cols_part, (((0,), (0,)), ((), ())), preferred_element_type=f32
    )
    member = (every_group[:, None] == jnp.arange(GROUPS, dtype=jnp.int32)[None, :]).astype(bf16)
    group_grad = lax.dot_general(
        member, cols_part, (((0,), (0,)), ((), ())), preferred_element_type=f32
    )
    return fisher, group_grad


def per_device(
    hidden_acts, output_grad, down_weight, input_basis, output_basis, token_example, example_group
):
    tokens, cols = hidden_acts.shape
    col_parts = 2 if cols % 512 == 0 else 1
    part, rows = cols // col_parts, tokens // FAR_PARTS

    def multiply(blocks, at, outs=2, width=part):
        kernel = block_terms if down_weight.shape[2] % 128 == 0 else gathered_terms
        return kernel(blocks, down_weight, at * part, width, outs)

    acts_part = jnp.dot(hidden_acts, input_basis, preferred_element_type=f32)
    grads_part = lax.dot_general(
        output_grad,
        output_basis,
        (((0, 1, 2), (0, 1, 2)), ((), ())),
        preferred_element_type=f32,
    )
    parts = jnp.concatenate([acts_part, grads_part], axis=1)
    far, beside, own, low = features(output_grad, parts)

    def multiply(groups, at, outs, width=part, *lead):
        kernel = block_terms if down_weight.shape[2] % 128 == 0 else gathered_terms
        return kernel(groups, down_weight, at * part, width, outs, *lead)

    units = [(blocks, half, step, at) for half, step, blocks in far for at in range(col_parts)]
    pairs, arrived, near = [], [], {}
    for count, (blocks, half, step, at) in enumerate(units):
        earlier = pairs[-1:] + arrived[:-1][-1:]
        if count == 1:
            earlier += far[-1][2][1:3]
        if count == 2:
            acts_low, grads_low = jnp.split(after(low, *earlier), 2, axis=1)
            example_grad = example_gradients(
                acts_low, grads_low, token_example[0], example_group.shape[0]
            )
            swapped = gather_examples(example_grad, example_group)
            earlier += [example_grad] + beside[1:3]
        if count == 3:
            every = order_examples(after(swapped, *earlier))
            fisher, group_grad = fisher_and_groups(every, example_grad.shape[1])
            earlier += [fisher, group_grad] + own[1:3]
        groups = [[after(blocks[0], *earlier)] + blocks[1:] if earlier else blocks]
        outs = [rows // 2, rows // 2, rows]
        if count == len(units) - 1:
            groups.append(beside)
            outs += [rows // 2] * (2 * FAR_PARTS)
        first, second, kept, *terms = multiply(groups, at, outs)
        pairs.append(add_halves(kept, swap(first, 1), swap(second, 1)))
        arrived.append(swap(pairs[-1], step))
        near[at] = [swap(after(term, arrived[-2], pairs[-1]), 1) for term in terms]
    own = [after(own[0], pairs[-1], *near[col_parts - 1])] + own[1:]
    if col_parts == 2:
        outs = [tokens] + [rows // 2] * (2 * FAR_PARTS)
        result, *terms = multiply([own, beside], 0, outs, cols, 1, part)
        near[0] = [swap(term, 1) for term in terms]
    else:
        (result,) = multiply([own], 0, [tokens], cols)
    for half in range(FAR_PARTS):
        for at in range(col_parts):
            sums = [
                arrived[count] for count, unit in enumerate(units) if unit[1:] == (half, unit[2], at)
            ]
            result = finish(
                result, near[at][2 * half : 2 * half + 2], sums, half * rows, at * part
            )
    return (result, fisher, group_grad)


def solution(mesh):
    return jax.shard_map(
        per_device,
        mesh=mesh,
        in_specs=(
            P(("parts", "dp"), "tensor"),
            P("tensor", None, None, ("parts", "dp")),
            P(None, "dp", None, "tensor"),
            P("tensor", None),
            P("tensor", None, None, None),
            P(("parts", "dp"), None),
            P(("parts", "dp")),
        ),
        out_specs=(
            P(("parts", "dp"), "tensor"),
            P(("parts", "dp"), "tensor"),
            P("parts", "tensor"),
        ),
        check_vma=False,
    )
```

```python
import functools

import jax
import jax.numpy as jnp
from jax import lax
from jax.experimental import pallas as pl
from jax.experimental.pallas import tpu as pltpu
from jax.sharding import PartitionSpec as P

GROUPS = 8

highest = lax.Precision.HIGHEST
f32, bf16 = jnp.float32, jnp.bfloat16


def swap(value, step):
    size = lax.axis_size("dp")
    return lax.ppermute(value, "dp", [(d, d ^ step) for d in range(size)])


def after(value, *earlier):
    return lax.optimization_barrier((value,) + earlier)[0]


def across(value, step, places=None):
    size = lax.axis_size("tensor")
    pairs = [(t, t ^ step) for t in range(size) if places is None or t in places]
    return lax.ppermute(value, "tensor", pairs)


def spread_first(block):
    second = across(block, 2)
    return [block, across(block, 1), second]


def spread_last(blocks, *earlier):
    block, _, second = blocks
    middle = across(after(block, second, *earlier), 3, (1, 2))
    ends = across(after(second, *earlier), 1, (1, 2))
    return blocks + [middle, ends]


def terms_kernel(size, count, first, adds, per_part, place_ref, *refs):
    total = 5 * count
    groups = [refs[5 * group : 5 * group + 5] for group in range(count)]
    w_ref, add_refs, outs = refs[total], refs[total + 1 :][: len(adds)], refs[total + 1 + len(adds) : -4]
    feats, held, sems, held_sems = refs[-4:]
    width, tile = feats.shape[1] // size, outs[0].shape[1]
    tall = feats.shape[0] // len(groups)
    j, steps = pl.program_id(0), pl.num_programs(0)
    slots = held.shape[0]

    def put(value, group, source, slot):
        at = pl.ds(pl.multiple_of(source * width, width), width)
        rows = pl.ds(group * tall, tall)
        return pltpu.make_async_copy(value, feats.at[rows, at], sems.at[group * size + slot])

    def fetch(step):
        slot = lax.rem(step, slots)
        at = pl.ds(pl.multiple_of(first + step * tile, tile), tile)
        return pltpu.make_async_copy(w_ref.at[:, 0, :, at], held.at[slot], held_sems.at[slot])

    @pl.when(j == 0)
    def _():
        copies = []
        place = place_ref[0]
        for group, blocks in enumerate(groups):
            copies += [put(blocks[k], group, lax.bitwise_xor(place, k), k) for k in range(3)]
        for copy in copies:
            copy.start()
        for step in range(slots):
            fetch(step).start()
        inside = jnp.logical_or(place == 1, place == 2)
        for group, blocks in enumerate(groups):
            for chosen, block in ((inside, blocks[3]), (jnp.logical_not(inside), blocks[4])):

                @pl.when(chosen)
                def _():
                    last = put(block, group, lax.bitwise_xor(place, 3), 3)
                    last.start()
                    last.wait()

        for copy in copies:
            copy.wait()

    fetch(j).wait()
    weight = held[lax.rem(j, slots)].reshape(size * width, tile)
    terms = jnp.dot(feats[...], weight, preferred_element_type=f32)
    row = 0
    for out_ref in outs:
        if not adds:
            out_ref[...] = terms[row : row + out_ref.shape[0]].astype(bf16)
        row += out_ref.shape[0]

    def add_part(part):
        here = [(ref, at) for ref, (at, of) in zip(add_refs, adds) if of == part]
        cut = min(ref.shape[0] for ref, _ in here)
        for row in range(0, feats.shape[0], cut):
            total = terms[row : row + cut]
            for ref, at in here:
                if at <= row < at + ref.shape[0]:
                    total = total + ref[row - at : row - at + cut].astype(f32)
            outs[0][row : row + cut] = total.astype(bf16)

    for part in sorted({of for _, of in adds}):
        pl.when(j // per_part == part)(functools.partial(add_part, part))

    @pl.when(j + slots < steps)
    def _():
        fetch(j + slots).start()


def block_terms(groups, down_weight, col_start, cols, outs, adds=()):
    size, _, width, _ = down_weight.shape
    rows = sum(outs)
    tile = max(n for n in range(128, 513, 128) if cols % n == 0)
    slots = min(4, cols // tile)
    blocks = [block for group in groups for block in group]
    per_part = adds[0][0].shape[1] // tile if adds else 1

    def add_spec(value, part):
        return pl.BlockSpec(
            (value.shape[0], tile),
            lambda j, place: (0, jnp.clip(j - part * per_part, 0, per_part - 1)),
        )

    return pl.pallas_call(
        functools.partial(
            terms_kernel,
            size,
            len(groups),
            col_start,
            [add[1:] for add in adds],
            per_part,
        ),
        out_shape=[jax.ShapeDtypeStruct((tall, cols), bf16) for tall in outs],
        grid_spec=pltpu.PrefetchScalarGridSpec(
            num_scalar_prefetch=1,
            grid=(cols // tile,),
            in_specs=[pl.BlockSpec(memory_space=pl.ANY)] * (len(blocks) + 1)
            + [add_spec(value, part) for value, _, part in adds],
            out_specs=[pl.BlockSpec((tall, tile), lambda j, place: (0, j)) for tall in outs],
            scratch_shapes=[
                pltpu.VMEM((rows, size * width), bf16),
                pltpu.VMEM((slots, size, width, tile), bf16),
                pltpu.SemaphoreType.DMA((len(groups) * size,)),
                pltpu.SemaphoreType.DMA((slots,)),
            ],
        ),
        compiler_params=pltpu.CompilerParams(vmem_limit_bytes=40 << 20),
        cost_estimate=pl.CostEstimate(
            flops=8 * rows * size * width * cols, bytes_accessed=1000, transcendentals=0
        ),
        name="terms",
    )(
        lax.axis_index("tensor").reshape(1),
        *blocks,
        down_weight,
        *[value for value, _, _ in adds],
    )


def add_kernel(kept_ref, first_ref, second_ref, out_ref):
    rows = first_ref.shape[0]
    for index, other in enumerate((first_ref, second_ref)):
        cut = slice(index * rows, (index + 1) * rows)
        out_ref[cut] = (kept_ref[cut].astype(f32) + other[...].astype(f32)).astype(bf16)


def add_halves(kept, first, second):
    rows, cols = kept.shape
    tile = max(n for n in range(128, 1025, 128) if cols % n == 0)

    def spec(tall):
        return pl.BlockSpec((tall, tile), lambda j: (0, j))

    return pl.pallas_call(
        add_kernel,
        out_shape=jax.ShapeDtypeStruct((rows, cols), bf16),
        grid=(cols // tile,),
        in_specs=[spec(rows), spec(rows // 2), spec(rows // 2)],
        out_specs=spec(rows),
        compiler_params=pltpu.CompilerParams(vmem_limit_bytes=16 << 20),
        cost_estimate=pl.CostEstimate(flops=1000, bytes_accessed=1000, transcendentals=0),
        name="pair",
    )(kept, first, second)


def finish_kernel(own_ref, other_ref, out_ref):
    out_ref[...] = (own_ref[...].astype(f32) + other_ref[...].astype(f32)).astype(bf16)


def finish(result, other, row, col):
    rows, cols = other.shape
    tile = max(n for n in range(128, 2049, 128) if cols % n == 0)
    part = pl.BlockSpec((rows, tile), lambda j: (row // rows, col // tile + j))
    return pl.pallas_call(
        finish_kernel,
        out_shape=jax.ShapeDtypeStruct(result.shape, bf16),
        grid=(cols // tile,),
        in_specs=[part, pl.BlockSpec((rows, tile), lambda j: (0, j))],
        out_specs=part,
        input_output_aliases={0: 0},
        compiler_params=pltpu.CompilerParams(vmem_limit_bytes=16 << 20),
        cost_estimate=pl.CostEstimate(flops=1000, bytes_accessed=1000, transcendentals=0),
        name="finish",
    )(result, other)


def example_gradients(acts_low, grads_low, local_ids, examples):
    onehot = (local_ids[:, None] == jnp.arange(examples, dtype=jnp.int32)[None, :]).astype(f32)
    counts = jnp.sum(onehot, axis=0)
    spread = (onehot[:, :, None] * acts_low[:, None, :]).reshape(onehot.shape[0], -1)
    outer_sum = lax.dot_general(
        spread,
        grads_low,
        (((0,), (0,)), ((), ())),
        precision=highest,
        preferred_element_type=f32,
    )
    basis_rank = acts_low.shape[1]
    outer_sum = outer_sum.reshape(examples, basis_rank * grads_low.shape[1]) / counts[:, None]
    return outer_sum.astype(bf16)


def gather_examples(example_grad, example_group):
    count = example_grad.shape[0]
    group_column = jnp.broadcast_to(example_group.astype(bf16)[:, None], (count, 128))
    held = jnp.concatenate([example_grad, group_column], axis=1)
    return [held] + [swap(held, step) for step in range(1, lax.axis_size("dp"))]


def order_examples(values):
    groups, place = lax.axis_size("dp"), lax.axis_index("dp")
    ordered = []
    for group in range(groups):
        value = values[0]
        for step in range(1, groups):
            value = jnp.where((place ^ group) == step, values[step], value)
        ordered.append(value)
    return jnp.concatenate(ordered, axis=0)


def fisher_and_groups(every, flat_width):
    row_count = flat_width // lax.axis_size("dp")
    col_count = flat_width // lax.axis_size("tensor")
    col_start = lax.axis_index("tensor") * col_count
    row_start = lax.axis_index("dp") * row_count
    every_group = every[:, flat_width].astype(jnp.int32)
    rows_part = lax.dynamic_slice_in_dim(every, row_start, row_count, 1)
    cols_part = lax.dynamic_slice_in_dim(every, col_start, col_count, 1)
    fisher = lax.dot_general(
        rows_part, cols_part, (((0,), (0,)), ((), ())), preferred_element_type=f32
    )
    member = (every_group[:, None] == jnp.arange(GROUPS, dtype=jnp.int32)[None, :]).astype(bf16)
    group_grad = lax.dot_general(
        member, cols_part, (((0,), (0,)), ((), ())), preferred_element_type=f32
    )
    return fisher, group_grad


def small_sums(hidden_acts, output_grad, input_basis, output_basis):
    acts_part = jnp.dot(hidden_acts, input_basis, preferred_element_type=f32)
    grads_part = lax.dot_general(
        output_grad,
        output_basis,
        (((0, 1, 2), (0, 1, 2)), ((), ())),
        preferred_element_type=f32,
    )
    return jnp.concatenate([acts_part, grads_part], axis=1)


def any_mesh(
    hidden_acts, output_grad, down_weight, input_basis, output_basis, token_example, example_group
):
    pieces = lax.all_to_all(output_grad, "dp", split_axis=1, concat_axis=3, tiled=True)
    columns = lax.all_gather(pieces, "tensor", axis=0, tiled=True)
    parts = small_sums(hidden_acts, output_grad, input_basis, output_basis)
    terms = lax.dot_general(
        columns, down_weight, (((0, 1, 2), (0, 1, 2)), ((), ())), preferred_element_type=f32
    )
    hidden_grad = lax.psum_scatter(terms.astype(bf16), "dp", scatter_dimension=0, tiled=True)
    acts_low, grads_low = jnp.split(lax.psum(parts, "tensor"), 2, axis=1)
    example_grad = example_gradients(
        acts_low, grads_low, token_example[0], example_group.shape[0]
    )
    every = order_examples(gather_examples(example_grad, example_group))
    fisher, group_grad = fisher_and_groups(every, example_grad.shape[1])
    return (hidden_grad, fisher, group_grad)


def line_of_four(
    hidden_acts, output_grad, down_weight, input_basis, output_basis, token_example, example_group
):
    tokens, cols = hidden_acts.shape
    part, rows = cols // 2, tokens // 2
    place = lax.axis_index("dp")
    turned = jnp.transpose(output_grad[0], (0, 2, 1))
    pieces = [lax.dynamic_index_in_dim(turned, place ^ k, 0, keepdims=False) for k in range(4)]
    far = []
    for half in range(2):
        cut = slice(half * rows, (half + 1) * rows)
        far.append(jnp.concatenate([swap(pieces[3][cut], 3), swap(pieces[2][cut], 2)]))
    beside, own = swap(pieces[1], 1), pieces[0]
    parts = small_sums(hidden_acts, output_grad, input_basis, output_basis)
    low = parts + across(parts, 1)

    blocks = spread_first(after(far[0], parts))
    later = spread_first(after(far[1], blocks[2]))
    blocks = spread_last(blocks, low, beside, far[1])
    low = after(low, blocks[4])

    def far_terms(chunks, at, *earlier):
        chunks = [[after(chunks[0][0], *earlier)] + chunks[0][1:]] + chunks[1:]
        outs = [rows // 2, rows // 2, rows] + [rows // 2] * 4 * (len(chunks) - 1)
        return block_terms(chunks, down_weight, at * part, part, outs)

    def pair_sum(first, last, kept, *earlier):
        pair = add_halves(kept, swap(after(first, *earlier), 1), swap(after(last, *earlier), 1))
        return pair, swap(pair, 2)

    first, last, kept = far_terms([blocks], 0, *later)
    pair0, sum0 = pair_sum(first, last, kept)

    low = low + across(after(low, pair0), 2)
    later = spread_last(later, pair0)
    beside = spread_first(after(beside, pair0))
    first, last, kept = far_terms([blocks], 1, pair0)
    pair1, sum1 = pair_sum(first, last, kept, *later, *beside)

    beside = spread_last(beside, pair1)
    own = spread_first(after(own, pair1))
    acts_low, grads_low = jnp.split(after(low, pair1, sum0), 2, axis=1)
    example_grad = example_gradients(
        acts_low, grads_low, token_example[0], example_group.shape[0]
    )
    gathered = gather_examples(example_grad, example_group)
    first, last, kept, *near0 = far_terms([later, beside], 0, pair1, example_grad)
    pair2, sum2 = pair_sum(first, last, kept, *own)

    own = spread_last(own, pair2)
    near0 = [swap(after(term, sum1, pair2), 1) for term in near0]
    every = order_examples(after(gathered, sum1, pair2))
    fisher, group_grad = fisher_and_groups(every, example_grad.shape[1])
    first, last, kept, *near1 = far_terms([later, beside], 1, fisher, group_grad, *near0)
    pair3, sum3 = pair_sum(first, last, kept, *own)

    near1 = [swap(after(term, sum2, pair3), 1) for term in near1]
    adds = [(term, row * (rows // 2), 0) for row, term in enumerate(near0)]
    adds += [(term, row * (rows // 2), 1) for row, term in enumerate(near1)]
    adds += [(sum0, 0, 0), (sum1, 0, 1), (sum2, rows, 0)]
    (result,) = block_terms([own], down_weight, 0, cols, [tokens], adds)
    return (finish(result, sum3, rows, part), fisher, group_grad)


def per_device(hidden_acts, output_grad, down_weight, *rest):
    fits = lax.axis_size("tensor") == 4 and lax.axis_size("dp") == 4
    fits = fits and down_weight.shape[2] % 128 == 0 and down_weight.shape[3] % 1024 == 0
    fits = fits and hidden_acts.shape[0] % 64 == 0
    return (line_of_four if fits else any_mesh)(hidden_acts, output_grad, down_weight, *rest)


def solution(mesh):
    return jax.shard_map(
        per_device,
        mesh=mesh,
        in_specs=(
            P(("parts", "dp"), "tensor"),
            P("tensor", None, None, ("parts", "dp")),
            P(None, "dp", None, "tensor"),
            P("tensor", None),
            P("tensor", None, None, None),
            P(("parts", "dp"), None),
            P(("parts", "dp")),
        ),
        out_specs=(
            P(("parts", "dp"), "tensor"),
            P(("parts", "dp"), "tensor"),
            P("parts", "tensor"),
        ),
        check_vma=False,
    )
```

```python
import functools

import jax
import jax.numpy as jnp
from jax import lax
from jax.experimental import pallas as pl
from jax.experimental.pallas import tpu as pltpu
from jax.sharding import PartitionSpec as P

GROUPS = 8

highest = lax.Precision.HIGHEST
f32, bf16 = jnp.float32, jnp.bfloat16


def swap(value, step):
    size = lax.axis_size("dp")
    return lax.ppermute(value, "dp", [(d, d ^ step) for d in range(size)])


def after(value, *earlier):
    return lax.optimization_barrier((value,) + earlier)[0]


def across(value, step, places=None):
    size = lax.axis_size("tensor")
    pairs = [(t, t ^ step) for t in range(size) if places is None or t in places]
    return lax.ppermute(value, "tensor", pairs)


def spread_first(block):
    second = across(block, 2)
    return [block, across(block, 1), second]


def spread_last(blocks, *earlier):
    block, _, second = blocks
    middle = across(after(block, second, *earlier), 3, (1, 2))
    ends = across(after(second, *earlier), 1, (1, 2))
    return blocks + [middle, ends]


def terms_kernel(size, count, first, adds, per_part, place_ref, *refs):
    total = 5 * count
    groups = [refs[5 * group : 5 * group + 5] for group in range(count)]
    w_ref, add_refs, outs = refs[total], refs[total + 1 :][: len(adds)], refs[total + 1 + len(adds) : -4]
    feats, held, sems, held_sems = refs[-4:]
    width, tile = feats.shape[1] // size, outs[0].shape[1]
    tall = feats.shape[0] // len(groups)
    j, steps = pl.program_id(0), pl.num_programs(0)
    slots = held.shape[0]

    def put(value, group, source, slot):
        at = pl.ds(pl.multiple_of(source * width, width), width)
        rows = pl.ds(group * tall, tall)
        return pltpu.make_async_copy(value, feats.at[rows, at], sems.at[group * size + slot])

    def fetch(step):
        slot = lax.rem(step, slots)
        at = pl.ds(pl.multiple_of(first + step * tile, tile), tile)
        return pltpu.make_async_copy(w_ref.at[:, 0, :, at], held.at[slot], held_sems.at[slot])

    @pl.when(j == 0)
    def _():
        copies = []
        place = place_ref[0]
        for group, blocks in enumerate(groups):
            copies += [put(blocks[k], group, lax.bitwise_xor(place, k), k) for k in range(3)]
        for copy in copies:
            copy.start()
        for step in range(slots):
            fetch(step).start()
        inside = jnp.logical_or(place == 1, place == 2)
        for group, blocks in enumerate(groups):
            for chosen, block in ((inside, blocks[3]), (jnp.logical_not(inside), blocks[4])):

                @pl.when(chosen)
                def _():
                    last = put(block, group, lax.bitwise_xor(place, 3), 3)
                    last.start()
                    last.wait()

        for copy in copies:
            copy.wait()

    fetch(j).wait()
    weight = held[lax.rem(j, slots)].reshape(size * width, tile)
    terms = jnp.dot(feats[...], weight, preferred_element_type=f32)
    row = 0
    for out_ref in outs:
        if not adds:
            out_ref[...] = terms[row : row + out_ref.shape[0]].astype(bf16)
        row += out_ref.shape[0]

    def add_part(part):
        here = [(ref, at) for ref, (at, of) in zip(add_refs, adds) if of == part]
        cut = min(ref.shape[0] for ref, _ in here)
        cols = pl.ds(pl.multiple_of((j - part * per_part) * tile, tile), tile)
        for row in range(0, feats.shape[0], cut):
            total = terms[row : row + cut]
            for ref, at in here:
                if at <= row < at + ref.shape[0]:
                    total = total + ref[row - at : row - at + cut, cols].astype(f32)
            outs[0][row : row + cut] = total.astype(bf16)

    for part in sorted({of for _, of in adds}):
        pl.when(j // per_part == part)(functools.partial(add_part, part))

    @pl.when(j + slots < steps)
    def _():
        fetch(j + slots).start()


def block_terms(groups, down_weight, col_start, cols, outs, adds=()):
    size, _, width, _ = down_weight.shape
    rows = sum(outs)
    tile = max(n for n in range(128, 513, 128) if cols % n == 0)
    slots = min(4, cols // tile)
    blocks = [block for group in groups for block in group]
    per_part = adds[0][0].shape[1] // tile if adds else 1

    return pl.pallas_call(
        functools.partial(
            terms_kernel,
            size,
            len(groups),
            col_start,
            [add[1:] for add in adds],
            per_part,
        ),
        out_shape=[jax.ShapeDtypeStruct((tall, cols), bf16) for tall in outs],
        grid_spec=pltpu.PrefetchScalarGridSpec(
            num_scalar_prefetch=1,
            grid=(cols // tile,),
            in_specs=[pl.BlockSpec(memory_space=pl.ANY)] * len(blocks)
            + [pl.BlockSpec(memory_space=pltpu.HBM)]
            + [pl.BlockSpec(memory_space=pltpu.VMEM)] * len(adds),
            out_specs=[pl.BlockSpec((tall, tile), lambda j, place: (0, j)) for tall in outs],
            scratch_shapes=[
                pltpu.VMEM((rows, size * width), bf16),
                pltpu.VMEM((slots, size, width, tile), bf16),
                pltpu.SemaphoreType.DMA((len(groups) * size,)),
                pltpu.SemaphoreType.DMA((slots,)),
            ],
        ),
        compiler_params=pltpu.CompilerParams(vmem_limit_bytes=24 << 20),
        cost_estimate=pl.CostEstimate(
            flops=8 * rows * size * width * cols, bytes_accessed=1000, transcendentals=0
        ),
        name="terms",
    )(
        lax.axis_index("tensor").reshape(1),
        *blocks,
        down_weight,
        *[value for value, _, _ in adds],
    )


def add_kernel(kept_ref, first_ref, second_ref, out_ref):
    rows = first_ref.shape[0]
    for index, other in enumerate((first_ref, second_ref)):
        cut = slice(index * rows, (index + 1) * rows)
        out_ref[cut] = (kept_ref[cut].astype(f32) + other[...].astype(f32)).astype(bf16)


def add_halves(kept, first, second):
    rows, cols = kept.shape
    tile = max(n for n in range(128, 1025, 128) if cols % n == 0)

    def spec(tall):
        return pl.BlockSpec((tall, tile), lambda j: (0, j))

    return pl.pallas_call(
        add_kernel,
        out_shape=jax.ShapeDtypeStruct((rows, cols), bf16),
        grid=(cols // tile,),
        in_specs=[spec(rows), spec(rows // 2), spec(rows // 2)],
        out_specs=spec(rows),
        compiler_params=pltpu.CompilerParams(vmem_limit_bytes=16 << 20),
        cost_estimate=pl.CostEstimate(flops=1000, bytes_accessed=1000, transcendentals=0),
        name="pair",
    )(kept, first, second)


def finish_kernel(own_ref, other_ref, out_ref):
    out_ref[...] = (own_ref[...].astype(f32) + other_ref[...].astype(f32)).astype(bf16)


def finish(result, other, row, col):
    rows, cols = other.shape
    tile = max(n for n in range(128, 2049, 128) if cols % n == 0)
    part = pl.BlockSpec((rows, tile), lambda j: (row // rows, col // tile + j))
    return pl.pallas_call(
        finish_kernel,
        out_shape=jax.ShapeDtypeStruct(result.shape, bf16),
        grid=(cols // tile,),
        in_specs=[part, pl.BlockSpec((rows, tile), lambda j: (0, j))],
        out_specs=part,
        input_output_aliases={0: 0},
        compiler_params=pltpu.CompilerParams(vmem_limit_bytes=16 << 20),
        cost_estimate=pl.CostEstimate(flops=1000, bytes_accessed=1000, transcendentals=0),
        name="finish",
    )(result, other)


def example_gradients(acts_low, grads_low, local_ids, examples):
    onehot = (local_ids[:, None] == jnp.arange(examples, dtype=jnp.int32)[None, :]).astype(f32)
    counts = jnp.sum(onehot, axis=0)
    spread = (onehot[:, :, None] * acts_low[:, None, :]).reshape(onehot.shape[0], -1)
    outer_sum = lax.dot_general(
        spread,
        grads_low,
        (((0,), (0,)), ((), ())),
        precision=highest,
        preferred_element_type=f32,
    )
    basis_rank = acts_low.shape[1]
    outer_sum = outer_sum.reshape(examples, basis_rank * grads_low.shape[1]) / counts[:, None]
    return outer_sum.astype(bf16)


def gather_examples(example_grad, example_group):
    count = example_grad.shape[0]
    group_column = jnp.broadcast_to(example_group.astype(bf16)[:, None], (count, 128))
    held = jnp.concatenate([example_grad, group_column], axis=1)
    return [held] + [swap(held, step) for step in range(1, lax.axis_size("dp"))]


def order_examples(values):
    groups, place = lax.axis_size("dp"), lax.axis_index("dp")
    ordered = []
    for group in range(groups):
        value = values[0]
        for step in range(1, groups):
            value = jnp.where((place ^ group) == step, values[step], value)
        ordered.append(value)
    return jnp.concatenate(ordered, axis=0)


def fisher_and_groups(every, flat_width):
    row_count = flat_width // lax.axis_size("dp")
    col_count = flat_width // lax.axis_size("tensor")
    col_start = lax.axis_index("tensor") * col_count
    row_start = lax.axis_index("dp") * row_count
    every_group = every[:, flat_width].astype(jnp.int32)
    rows_part = lax.dynamic_slice_in_dim(every, row_start, row_count, 1)
    cols_part = lax.dynamic_slice_in_dim(every, col_start, col_count, 1)
    fisher = lax.dot_general(
        rows_part, cols_part, (((0,), (0,)), ((), ())), preferred_element_type=f32
    )
    member = (every_group[:, None] == jnp.arange(GROUPS, dtype=jnp.int32)[None, :]).astype(bf16)
    group_grad = lax.dot_general(
        member, cols_part, (((0,), (0,)), ((), ())), preferred_element_type=f32
    )
    return fisher, group_grad


def small_sums(hidden_acts, output_grad, input_basis, output_basis):
    acts_part = jnp.dot(hidden_acts, input_basis, preferred_element_type=f32)
    grads_part = lax.dot_general(
        output_grad,
        output_basis,
        (((0, 1, 2), (0, 1, 2)), ((), ())),
        preferred_element_type=f32,
    )
    return jnp.concatenate([acts_part, grads_part], axis=1)


def any_mesh(
    hidden_acts, output_grad, down_weight, input_basis, output_basis, token_example, example_group
):
    pieces = lax.all_to_all(output_grad, "dp", split_axis=1, concat_axis=3, tiled=True)
    columns = lax.all_gather(pieces, "tensor", axis=0, tiled=True)
    parts = small_sums(hidden_acts, output_grad, input_basis, output_basis)
    terms = lax.dot_general(
        columns, down_weight, (((0, 1, 2), (0, 1, 2)), ((), ())), preferred_element_type=f32
    )
    hidden_grad = lax.psum_scatter(terms.astype(bf16), "dp", scatter_dimension=0, tiled=True)
    acts_low, grads_low = jnp.split(lax.psum(parts, "tensor"), 2, axis=1)
    example_grad = example_gradients(
        acts_low, grads_low, token_example[0], example_group.shape[0]
    )
    every = order_examples(gather_examples(example_grad, example_group))
    fisher, group_grad = fisher_and_groups(every, example_grad.shape[1])
    return (hidden_grad, fisher, group_grad)


def line_of_four(
    hidden_acts, output_grad, down_weight, input_basis, output_basis, token_example, example_group
):
    tokens, cols = hidden_acts.shape
    part, rows = cols // 2, tokens // 2
    place = lax.axis_index("dp")
    turned = jnp.transpose(output_grad[0], (0, 2, 1))
    pieces = [lax.dynamic_index_in_dim(turned, place ^ k, 0, keepdims=False) for k in range(4)]
    far = []
    for half in range(2):
        cut = slice(half * rows, (half + 1) * rows)
        far.append(jnp.concatenate([swap(pieces[3][cut], 3), swap(pieces[2][cut], 2)]))
    beside, own = swap(pieces[1], 1), pieces[0]
    parts = small_sums(hidden_acts, output_grad, input_basis, output_basis)
    low = parts + across(parts, 1)

    blocks = spread_first(after(far[0], parts))
    later = spread_first(after(far[1], blocks[2]))
    blocks = spread_last(blocks, low, beside, far[1])
    low = after(low, blocks[4])

    def far_terms(chunks, at, *earlier):
        chunks = [[after(chunks[0][0], *earlier)] + chunks[0][1:]] + chunks[1:]
        outs = [rows // 2, rows // 2, rows] + [rows // 2] * 4 * (len(chunks) - 1)
        return block_terms(chunks, down_weight, at * part, part, outs)

    def pair_sum(first, last, kept, *earlier):
        pair = add_halves(kept, swap(after(first, *earlier), 1), swap(after(last, *earlier), 1))
        return pair, swap(pair, 2)

    first, last, kept = far_terms([blocks], 0, *later)
    pair0, sum0 = pair_sum(first, last, kept)

    low = low + across(after(low, pair0), 2)
    later = spread_last(later, pair0)
    beside = spread_first(after(beside, pair0))
    first, last, kept = far_terms([blocks], 1, pair0)
    pair1, sum1 = pair_sum(first, last, kept, *later, *beside)

    beside = spread_last(beside, pair1)
    own = spread_first(after(own, pair1))
    first, last, kept, *near0 = far_terms([later, beside], 0, pair1, sum0)
    pair2, sum2 = pair_sum(first, last, kept, *own)

    own = spread_last(own, pair2)
    near0 = [swap(after(term, sum1, pair2), 1) for term in near0]
    acts_low, grads_low = jnp.split(after(low, pair2, sum1), 2, axis=1)
    example_grad = example_gradients(
        acts_low, grads_low, token_example[0], example_group.shape[0]
    )
    gathered = gather_examples(example_grad, example_group)
    first, last, kept, *near1 = far_terms([later, beside], 1, example_grad, *near0)
    pair3, sum3 = pair_sum(first, last, kept, *own)

    near1 = [swap(after(term, sum2, pair3), 1) for term in near1]
    every = order_examples(after(gathered, sum2, pair3))
    fisher, group_grad = fisher_and_groups(every, example_grad.shape[1])
    own = [after(own[0], fisher, group_grad)] + own[1:]
    adds = [(term, row * (rows // 2), 0) for row, term in enumerate(near0)]
    adds += [(term, row * (rows // 2), 1) for row, term in enumerate(near1)]
    adds += [(sum0, 0, 0), (sum1, 0, 1), (sum2, rows, 0)]
    (result,) = block_terms([own], down_weight, 0, cols, [tokens], adds)
    return (finish(result, sum3, rows, part), fisher, group_grad)


def per_device(hidden_acts, output_grad, down_weight, *rest):
    fits = lax.axis_size("tensor") == 4 and lax.axis_size("dp") == 4
    fits = fits and down_weight.shape[2] % 128 == 0 and down_weight.shape[3] % 1024 == 0
    fits = fits and hidden_acts.shape[0] % 64 == 0
    return (line_of_four if fits else any_mesh)(hidden_acts, output_grad, down_weight, *rest)


def solution(mesh):
    return jax.shard_map(
        per_device,
        mesh=mesh,
        in_specs=(
            P(("parts", "dp"), "tensor"),
            P("tensor", None, None, ("parts", "dp")),
            P(None, "dp", None, "tensor"),
            P("tensor", None),
            P("tensor", None, None, None),
            P(("parts", "dp"), None),
            P(("parts", "dp")),
        ),
        out_specs=(
            P(("parts", "dp"), "tensor"),
            P(("parts", "dp"), "tensor"),
            P("parts", "tensor"),
        ),
        check_vma=False,
    )
```

```python
import functools

import jax
import jax.numpy as jnp
from jax import lax
from jax.experimental import pallas as pl
from jax.experimental.pallas import tpu as pltpu
from jax.sharding import PartitionSpec as P

GROUPS = 8

highest = lax.Precision.HIGHEST
f32, bf16 = jnp.float32, jnp.bfloat16


def swap(value, step):
    size = lax.axis_size("dp")
    return lax.ppermute(value, "dp", [(d, d ^ step) for d in range(size)])


def after(value, *earlier):
    return lax.optimization_barrier((value,) + earlier)[0]


def across(value, step, places=None):
    size = lax.axis_size("tensor")
    pairs = [(t, t ^ step) for t in range(size) if places is None or t in places]
    return lax.ppermute(value, "tensor", pairs)


def spread_first(block):
    second = across(block, 2)
    return [block, across(block, 1), second]


def spread_last(blocks, *earlier):
    block, _, second = blocks
    middle = across(after(block, second, *earlier), 3, (1, 2))
    ends = across(after(second, *earlier), 1, (1, 2))
    return blocks + [middle, ends]


def terms_kernel(size, count, first, adds, per_part, place_ref, *refs):
    total = 5 * count
    groups = [refs[5 * group : 5 * group + 5] for group in range(count)]
    w_ref, add_refs, outs = refs[total], refs[total + 1 :][: len(adds)], refs[total + 1 + len(adds) : -4]
    feats, held, sems, held_sems = refs[-4:]
    width, tile = feats.shape[1] // size, outs[0].shape[1]
    tall = feats.shape[0] // len(groups)
    j, steps = pl.program_id(0), pl.num_programs(0)
    slots = held.shape[0]

    def put(value, group, source, slot):
        at = pl.ds(pl.multiple_of(source * width, width), width)
        rows = pl.ds(group * tall, tall)
        return pltpu.make_async_copy(value, feats.at[rows, at], sems.at[group * size + slot])

    def fetch(step):
        slot = lax.rem(step, slots)
        at = pl.ds(pl.multiple_of(first + step * tile, tile), tile)
        return pltpu.make_async_copy(w_ref.at[:, 0, :, at], held.at[slot], held_sems.at[slot])

    @pl.when(j == 0)
    def _():
        copies = []
        place = place_ref[0]
        for group, blocks in enumerate(groups):
            copies += [put(blocks[k], group, lax.bitwise_xor(place, k), k) for k in range(3)]
        for copy in copies:
            copy.start()
        for step in range(slots):
            fetch(step).start()
        inside = jnp.logical_or(place == 1, place == 2)
        for group, blocks in enumerate(groups):
            for chosen, block in ((inside, blocks[3]), (jnp.logical_not(inside), blocks[4])):

                @pl.when(chosen)
                def _():
                    last = put(block, group, lax.bitwise_xor(place, 3), 3)
                    last.start()
                    last.wait()

        for copy in copies:
            copy.wait()

    fetch(j).wait()
    weight = held[lax.rem(j, slots)].reshape(size * width, tile)
    terms = jnp.dot(feats[...], weight, preferred_element_type=f32)
    row = 0
    for out_ref in outs:
        if not adds:
            out_ref[...] = terms[row : row + out_ref.shape[0]].astype(bf16)
        row += out_ref.shape[0]

    def add_part(part):
        here = [(ref, at) for ref, (at, of) in zip(add_refs, adds) if of == part]
        cut = min(ref.shape[0] for ref, _ in here)
        cols = pl.ds(pl.multiple_of((j - part * per_part) * tile, tile), tile)
        for row in range(0, feats.shape[0], cut):
            total = terms[row : row + cut]
            for ref, at in here:
                if at <= row < at + ref.shape[0]:
                    total = total + ref[row - at : row - at + cut, cols].astype(f32)
            outs[0][row : row + cut] = total.astype(bf16)

    for part in sorted({of for _, of in adds}):
        pl.when(j // per_part == part)(functools.partial(add_part, part))

    @pl.when(j + slots < steps)
    def _():
        fetch(j + slots).start()


def block_terms(groups, down_weight, col_start, cols, outs, adds=()):
    size, _, width, _ = down_weight.shape
    rows = sum(outs)
    tile = max(n for n in range(128, 513, 128) if cols % n == 0)
    slots = min(4, cols // tile)
    blocks = [block for group in groups for block in group]
    per_part = adds[0][0].shape[1] // tile if adds else 1

    return pl.pallas_call(
        functools.partial(
            terms_kernel,
            size,
            len(groups),
            col_start,
            [add[1:] for add in adds],
            per_part,
        ),
        out_shape=[jax.ShapeDtypeStruct((tall, cols), bf16) for tall in outs],
        grid_spec=pltpu.PrefetchScalarGridSpec(
            num_scalar_prefetch=1,
            grid=(cols // tile,),
            in_specs=[pl.BlockSpec(memory_space=pltpu.HBM)] * (len(blocks) + 1)
            + [pl.BlockSpec(memory_space=pltpu.VMEM)] * len(adds),
            out_specs=[pl.BlockSpec((tall, tile), lambda j, place: (0, j)) for tall in outs],
            scratch_shapes=[
                pltpu.VMEM((rows, size * width), bf16),
                pltpu.VMEM((slots, size, width, tile), bf16),
                pltpu.SemaphoreType.DMA((len(groups) * size,)),
                pltpu.SemaphoreType.DMA((slots,)),
            ],
        ),
        compiler_params=pltpu.CompilerParams(vmem_limit_bytes=24 << 20),
        cost_estimate=pl.CostEstimate(
            flops=rows * size * width * cols // 4, bytes_accessed=1000, transcendentals=0
        ),
        name="terms",
    )(
        lax.axis_index("tensor").reshape(1),
        *blocks,
        down_weight,
        *[value for value, _, _ in adds],
    )


def add_kernel(kept_ref, first_ref, second_ref, out_ref):
    rows = first_ref.shape[0]
    for index, other in enumerate((first_ref, second_ref)):
        cut = slice(index * rows, (index + 1) * rows)
        out_ref[cut] = (kept_ref[cut].astype(f32) + other[...].astype(f32)).astype(bf16)


def add_halves(kept, first, second):
    rows, cols = kept.shape
    tile = max(n for n in range(128, 1025, 128) if cols % n == 0)

    def spec(tall):
        return pl.BlockSpec((tall, tile), lambda j: (0, j))

    return pl.pallas_call(
        add_kernel,
        out_shape=jax.ShapeDtypeStruct((rows, cols), bf16),
        grid=(cols // tile,),
        in_specs=[spec(rows), spec(rows // 2), spec(rows // 2)],
        out_specs=spec(rows),
        compiler_params=pltpu.CompilerParams(vmem_limit_bytes=16 << 20),
        cost_estimate=pl.CostEstimate(flops=1000, bytes_accessed=1000, transcendentals=0),
        name="pair",
    )(kept, first, second)


def finish_kernel(own_ref, other_ref, out_ref):
    out_ref[...] = (own_ref[...].astype(f32) + other_ref[...].astype(f32)).astype(bf16)


def finish(result, other, row, col):
    rows, cols = other.shape
    tile = max(n for n in range(128, 2049, 128) if cols % n == 0)
    part = pl.BlockSpec((rows, tile), lambda j: (row // rows, col // tile + j))
    return pl.pallas_call(
        finish_kernel,
        out_shape=jax.ShapeDtypeStruct(result.shape, bf16),
        grid=(cols // tile,),
        in_specs=[part, pl.BlockSpec((rows, tile), lambda j: (0, j))],
        out_specs=part,
        input_output_aliases={0: 0},
        compiler_params=pltpu.CompilerParams(vmem_limit_bytes=16 << 20),
        cost_estimate=pl.CostEstimate(flops=1000, bytes_accessed=1000, transcendentals=0),
        name="finish",
    )(result, other)


def example_gradients(acts_low, grads_low, local_ids, examples):
    onehot = (local_ids[:, None] == jnp.arange(examples, dtype=jnp.int32)[None, :]).astype(f32)
    counts = jnp.sum(onehot, axis=0)
    spread = (onehot[:, :, None] * acts_low[:, None, :]).reshape(onehot.shape[0], -1)
    outer_sum = lax.dot_general(
        spread,
        grads_low,
        (((0,), (0,)), ((), ())),
        precision=highest,
        preferred_element_type=f32,
    )
    basis_rank = acts_low.shape[1]
    outer_sum = outer_sum.reshape(examples, basis_rank * grads_low.shape[1]) / counts[:, None]
    return outer_sum.astype(bf16)


def gather_examples(example_grad, example_group):
    count = example_grad.shape[0]
    group_column = jnp.broadcast_to(example_group.astype(bf16)[:, None], (count, 128))
    held = jnp.concatenate([example_grad, group_column], axis=1)
    return [held] + [swap(held, step) for step in range(1, lax.axis_size("dp"))]


def order_examples(values):
    groups, place = lax.axis_size("dp"), lax.axis_index("dp")
    ordered = []
    for group in range(groups):
        value = values[0]
        for step in range(1, groups):
            value = jnp.where((place ^ group) == step, values[step], value)
        ordered.append(value)
    return jnp.concatenate(ordered, axis=0)


def fisher_and_groups(every, flat_width):
    row_count = flat_width // lax.axis_size("dp")
    col_count = flat_width // lax.axis_size("tensor")
    col_start = lax.axis_index("tensor") * col_count
    row_start = lax.axis_index("dp") * row_count
    every_group = every[:, flat_width].astype(jnp.int32)
    rows_part = lax.dynamic_slice_in_dim(every, row_start, row_count, 1)
    cols_part = lax.dynamic_slice_in_dim(every, col_start, col_count, 1)
    fisher = lax.dot_general(
        rows_part, cols_part, (((0,), (0,)), ((), ())), preferred_element_type=f32
    )
    member = (every_group[:, None] == jnp.arange(GROUPS, dtype=jnp.int32)[None, :]).astype(bf16)
    group_grad = lax.dot_general(
        member, cols_part, (((0,), (0,)), ((), ())), preferred_element_type=f32
    )
    return fisher, group_grad


def small_sums(hidden_acts, output_grad, input_basis, output_basis):
    acts_part = jnp.dot(hidden_acts, input_basis, preferred_element_type=f32)
    grads_part = lax.dot_general(
        output_grad,
        output_basis,
        (((0, 1, 2), (0, 1, 2)), ((), ())),
        preferred_element_type=f32,
    )
    return jnp.concatenate([acts_part, grads_part], axis=1)


def any_mesh(
    hidden_acts, output_grad, down_weight, input_basis, output_basis, token_example, example_group
):
    pieces = lax.all_to_all(output_grad, "dp", split_axis=1, concat_axis=3, tiled=True)
    columns = lax.all_gather(pieces, "tensor", axis=0, tiled=True)
    parts = small_sums(hidden_acts, output_grad, input_basis, output_basis)
    terms = lax.dot_general(
        columns, down_weight, (((0, 1, 2), (0, 1, 2)), ((), ())), preferred_element_type=f32
    )
    hidden_grad = lax.psum_scatter(terms.astype(bf16), "dp", scatter_dimension=0, tiled=True)
    acts_low, grads_low = jnp.split(lax.psum(parts, "tensor"), 2, axis=1)
    example_grad = example_gradients(
        acts_low, grads_low, token_example[0], example_group.shape[0]
    )
    every = order_examples(gather_examples(example_grad, example_group))
    fisher, group_grad = fisher_and_groups(every, example_grad.shape[1])
    return (hidden_grad, fisher, group_grad)


def line_of_four(
    hidden_acts, output_grad, down_weight, input_basis, output_basis, token_example, example_group
):
    tokens, cols = hidden_acts.shape
    part, rows = cols // 2, tokens // 2
    place = lax.axis_index("dp")
    turned = jnp.transpose(output_grad[0], (0, 2, 1))
    pieces = [lax.dynamic_index_in_dim(turned, place ^ k, 0, keepdims=False) for k in range(4)]
    far = []
    for half in range(2):
        cut = slice(half * rows, (half + 1) * rows)
        far.append(jnp.concatenate([swap(pieces[3][cut], 3), swap(pieces[2][cut], 2)]))
    beside, own = swap(pieces[1], 1), pieces[0]
    parts = small_sums(hidden_acts, output_grad, input_basis, output_basis)
    low = parts + across(parts, 1)

    blocks = spread_first(after(far[0], parts))
    later = spread_first(after(far[1], blocks[2]))
    blocks = spread_last(blocks, low, beside, far[1])
    low = after(low, blocks[4])

    def far_terms(chunks, at, *earlier):
        chunks = [[after(chunks[0][0], *earlier)] + chunks[0][1:]] + chunks[1:]
        outs = [rows // 2, rows // 2, rows] + [rows // 2] * 4 * (len(chunks) - 1)
        return block_terms(chunks, down_weight, at * part, part, outs)

    def pair_sum(first, last, kept, *earlier):
        pair = add_halves(kept, swap(after(first, *earlier), 1), swap(after(last, *earlier), 1))
        return pair, swap(pair, 2)

    first, last, kept = far_terms([blocks], 0, *later)
    pair0, sum0 = pair_sum(first, last, kept)

    later = spread_last(later, pair0)
    beside = spread_first(after(beside, pair0))
    first, last, kept = far_terms([blocks], 1, pair0)
    pair1, sum1 = pair_sum(first, last, kept, *later, *beside)

    beside = spread_last(beside, pair1)
    own = spread_first(after(own, pair1))
    first, last, kept, *near0 = far_terms([later, beside], 0, pair1, sum0)
    pair2, sum2 = pair_sum(first, last, kept, *own)

    own = spread_last(own, pair2)
    near0 = [swap(after(term, sum1, pair2), 1) for term in near0]
    partner = across(after(low, pair0), 2)
    acts_low, grads_low = jnp.split(after(low, pair2, sum1) + partner, 2, axis=1)
    example_grad = example_gradients(
        acts_low, grads_low, token_example[0], example_group.shape[0]
    )
    gathered = gather_examples(example_grad, example_group)
    first, last, kept, *near1 = far_terms([later, beside], 1, example_grad, *near0)
    pair3, sum3 = pair_sum(first, last, kept, *own)

    near1 = [swap(after(term, sum2, pair3), 1) for term in near1]
    every = order_examples(after(gathered, sum2, pair3))
    fisher, group_grad = fisher_and_groups(every, example_grad.shape[1])
    own = [after(own[0], fisher, group_grad)] + own[1:]
    adds = [(term, row * (rows // 2), 0) for row, term in enumerate(near0)]
    adds += [(term, row * (rows // 2), 1) for row, term in enumerate(near1)]
    adds += [(sum0, 0, 0), (sum1, 0, 1), (sum2, rows, 0)]
    (result,) = block_terms([own], down_weight, 0, cols, [tokens], adds)
    return (finish(result, sum3, rows, part), fisher, group_grad)


def per_device(hidden_acts, output_grad, down_weight, *rest):
    fits = lax.axis_size("tensor") == 4 and lax.axis_size("dp") == 4
    fits = fits and down_weight.shape[2] % 128 == 0 and down_weight.shape[3] % 1024 == 0
    fits = fits and hidden_acts.shape[0] % 64 == 0
    return (line_of_four if fits else any_mesh)(hidden_acts, output_grad, down_weight, *rest)


def solution(mesh):
    return jax.shard_map(
        per_device,
        mesh=mesh,
        in_specs=(
            P(("parts", "dp"), "tensor"),
            P("tensor", None, None, ("parts", "dp")),
            P(None, "dp", None, "tensor"),
            P("tensor", None),
            P("tensor", None, None, None),
            P(("parts", "dp"), None),
            P(("parts", "dp")),
        ),
        out_specs=(
            P(("parts", "dp"), "tensor"),
            P(("parts", "dp"), "tensor"),
            P("parts", "tensor"),
        ),
        check_vma=False,
    )
```

```python
import functools

import jax
import jax.numpy as jnp
from jax import lax
from jax.experimental import pallas as pl
from jax.experimental.pallas import tpu as pltpu
from jax.sharding import PartitionSpec as P

GROUPS = 8

highest = lax.Precision.HIGHEST
f32, bf16 = jnp.float32, jnp.bfloat16


def swap(value, step):
    size = lax.axis_size("dp")
    return lax.ppermute(value, "dp", [(d, d ^ step) for d in range(size)])


def after(value, *earlier):
    return lax.optimization_barrier((value,) + earlier)[0]


def across(value, step, places=None):
    size = lax.axis_size("tensor")
    pairs = [(t, t ^ step) for t in range(size) if places is None or t in places]
    return lax.ppermute(value, "tensor", pairs)


def spread_first(block):
    second = across(block, 2)
    return [block, across(block, 1), second]


def spread_direct(block):
    second, third = across(block, 2), across(block, 3)
    return [block, across(block, 1), second, third]


def spread_last(blocks, *earlier):
    block, _, second = blocks
    middle = across(after(block, second, *earlier), 3, (1, 2))
    ends = across(after(second, *earlier), 1, (1, 2))
    return blocks + [middle, ends]


def terms_kernel(size, per_group, count, first, adds, per_part, parts, place_ref, *refs):
    total = per_group * count
    groups = [refs[per_group * group :][:per_group] for group in range(count)]
    w_ref, add_refs, outs = refs[total], refs[total + 1 :][:adds], refs[total + 1 + adds : -4]
    feats, held, sems, held_sems = refs[-4:]
    width, tile = feats.shape[1] // size, outs[0].shape[1]
    tall = feats.shape[0] // len(groups)
    j, steps = pl.program_id(0), pl.num_programs(0)
    slots = held.shape[0]

    def put(value, group, source, slot):
        at = pl.ds(pl.multiple_of(source * width, width), width)
        rows = pl.ds(group * tall, tall)
        return pltpu.make_async_copy(value, feats.at[rows, at], sems.at[group * size + slot])

    def fetch(step):
        slot = lax.rem(step, slots)
        at = pl.ds(pl.multiple_of(first + step * tile, tile), tile)
        return pltpu.make_async_copy(w_ref.at[:, 0, :, at], held.at[slot], held_sems.at[slot])

    @pl.when(j == 0)
    def _():
        copies = []
        place = place_ref[0]
        for group, blocks in enumerate(groups):
            straight = 3 if per_group == 5 else 4
            copies += [
                put(blocks[k], group, lax.bitwise_xor(place, k), k) for k in range(straight)
            ]
        for copy in copies:
            copy.start()
        for step in range(slots):
            fetch(step).start()
        inside = jnp.logical_or(place == 1, place == 2)
        for group, blocks in enumerate(groups if per_group == 5 else ()):
            for chosen, block in ((inside, blocks[3]), (jnp.logical_not(inside), blocks[4])):

                @pl.when(chosen)
                def _():
                    last = put(block, group, lax.bitwise_xor(place, 3), 3)
                    last.start()
                    last.wait()

        for copy in copies:
            copy.wait()

    fetch(j).wait()
    weight = held[lax.rem(j, slots)].reshape(size * width, tile)
    terms = jnp.dot(feats[...], weight, preferred_element_type=f32)
    if adds:
        wide_refs, low_refs = add_refs[:-2], add_refs[-2:]
        tall = low_refs[0].shape[0]
        top = feats.shape[0] - 2 * tall
        for part, ref in enumerate(wide_refs):

            @pl.when(j // per_part == part)
            def _():
                total = terms + ref[...].astype(f32)
                if part == len(wide_refs) - 1:
                    outs[0][:top] = total[:top].astype(bf16)
                    for row, low_ref in zip((top, top + tall), low_refs):
                        low = total[row : row + tall] + low_ref[...].astype(f32)
                        outs[0][row : row + tall] = low.astype(bf16)
                else:
                    outs[0][...] = total.astype(bf16)


    def write(some):
        row = 0
        for out_ref in some:
            out_ref[...] = terms[row : row + out_ref.shape[0]].astype(bf16)
            row += out_ref.shape[0]

    each = len(outs) // parts
    if parts == 1 and not adds:
        write(outs)
    for part in range(parts if parts > 1 else 0):
        pl.when(j // per_part == part)(
            functools.partial(write, outs[part * each : (part + 1) * each])
        )

    @pl.when(j + slots < steps)
    def _():
        fetch(j + slots).start()


def block_terms(groups, down_weight, col_start, cols, outs, adds=(), low_adds=(), parts=1):
    size, _, width, _ = down_weight.shape
    rows = sum(outs)
    tile = max(n for n in range(128, 897, 128) if cols % n == 0)
    slots = min(3, cols // tile)
    blocks = [block for group in groups for block in group]
    per_part = adds[0].shape[1] // tile if adds else cols // parts // tile

    def add_spec(part, tall=rows):
        if parts == 1 and not adds or part is None:
            return pl.BlockSpec((tall, tile), lambda j, place: (0, j))
        return pl.BlockSpec(
            (tall, tile), lambda j, place: (0, jnp.clip(j - part * per_part, 0, per_part - 1))
        )

    add_specs = [add_spec(part) for part in range(len(adds))]
    if adds:
        add_specs += [add_spec(len(adds) - 1, value.shape[0]) for value in low_adds]
        adds = [*adds, *low_adds]

    return pl.pallas_call(
        functools.partial(
            terms_kernel,
            size,
            len(groups[0]),
            len(groups),
            col_start,
            len(adds),
            per_part,
            parts,
        ),
        out_shape=[jax.ShapeDtypeStruct((tall, cols // parts), bf16) for tall in outs] * parts,
        grid_spec=pltpu.PrefetchScalarGridSpec(
            num_scalar_prefetch=1,
            grid=(cols // tile,),
            in_specs=[pl.BlockSpec(memory_space=pltpu.HBM)] * (len(blocks) + 1)
            + add_specs,
            out_specs=[
                add_spec(None if parts == 1 else part, tall)
                for part in range(parts)
                for tall in outs
            ],
            scratch_shapes=[
                pltpu.VMEM((rows, size * width), bf16),
                pltpu.VMEM((slots, size, width, tile), bf16),
                pltpu.SemaphoreType.DMA((len(groups) * size,)),
                pltpu.SemaphoreType.DMA((slots,)),
            ],
        ),
        compiler_params=pltpu.CompilerParams(vmem_limit_bytes=24 << 20),
        cost_estimate=pl.CostEstimate(
            flops=rows * size * width * cols // 4, bytes_accessed=1000, transcendentals=0
        ),
        name="terms",
    )(
        lax.axis_index("tensor").reshape(1),
        *blocks,
        down_weight,
        *adds,
    )


def add_kernel(kept_ref, first_ref, second_ref, *outs):
    rows, tall = first_ref.shape[0], outs[0].shape[0]
    for index, other in enumerate((first_ref, second_ref)):
        total = kept_ref[index * rows : (index + 1) * rows].astype(f32) + other[...].astype(f32)
        at = index * rows % tall
        outs[index * rows // tall][at : at + rows] = total.astype(bf16)


def add_halves(kept, first, second, outs=1):
    rows, cols = kept.shape
    tile = max(n for n in range(128, 1025, 128) if cols % n == 0)

    def spec(tall):
        return pl.BlockSpec((tall, tile), lambda j: (0, j))

    return pl.pallas_call(
        add_kernel,
        out_shape=[jax.ShapeDtypeStruct((rows // outs, cols), bf16)] * outs,
        grid=(cols // tile,),
        in_specs=[spec(rows), spec(rows // 2), spec(rows // 2)],
        out_specs=[spec(rows // outs)] * outs,
        compiler_params=pltpu.CompilerParams(vmem_limit_bytes=16 << 20),
        cost_estimate=pl.CostEstimate(flops=1000, bytes_accessed=1000, transcendentals=0),
        name="pair",
    )(kept, first, second)


def gather_sums_kernel(*refs):
    quarters, sums, out_ref = refs[:4], refs[4:-1], refs[-1]
    rows = quarters[0].shape[0]
    for index, ref in enumerate(quarters):
        value = ref[...]
        if index // 2 < len(sums):
            at = (index % 2) * rows
            other = sums[index // 2][at : at + rows]
            value = (value.astype(f32) + other.astype(f32)).astype(bf16)
        out_ref[index * rows : (index + 1) * rows] = value


def gather_sums(quarters, sums):
    rows, cols = quarters[0].shape
    tile = max(n for n in range(128, 2049, 128) if cols % n == 0)

    def spec(tall):
        return pl.BlockSpec((tall, tile), lambda j: (0, j))

    return pl.pallas_call(
        gather_sums_kernel,
        out_shape=jax.ShapeDtypeStruct((4 * rows, cols), bf16),
        grid=(cols // tile,),
        in_specs=[spec(rows)] * 4 + [spec(2 * rows)] * len(sums),
        out_specs=spec(4 * rows),
        compiler_params=pltpu.CompilerParams(vmem_limit_bytes=24 << 20),
        cost_estimate=pl.CostEstimate(flops=1000, bytes_accessed=1000, transcendentals=0),
        name="sums",
    )(*quarters, *sums)


def example_gradients(acts_low, grads_low, local_ids, examples):
    onehot = (local_ids[:, None] == jnp.arange(examples, dtype=jnp.int32)[None, :]).astype(f32)
    counts = jnp.sum(onehot, axis=0)
    spread = (onehot[:, :, None] * acts_low[:, None, :]).reshape(onehot.shape[0], -1)
    outer_sum = lax.dot_general(
        spread,
        grads_low,
        (((0,), (0,)), ((), ())),
        precision=highest,
        preferred_element_type=f32,
    )
    basis_rank = acts_low.shape[1]
    outer_sum = outer_sum.reshape(examples, basis_rank * grads_low.shape[1]) / counts[:, None]
    return outer_sum.astype(bf16)


def gather_examples(example_grad, example_group):
    count = example_grad.shape[0]
    group_column = jnp.broadcast_to(example_group.astype(bf16)[:, None], (count, 128))
    held = jnp.concatenate([example_grad, group_column], axis=1)
    return [held] + [swap(held, step) for step in range(1, lax.axis_size("dp"))]


def order_examples(values):
    groups, place = lax.axis_size("dp"), lax.axis_index("dp")
    ordered = []
    for group in range(groups):
        value = values[0]
        for step in range(1, groups):
            value = jnp.where((place ^ group) == step, values[step], value)
        ordered.append(value)
    return jnp.concatenate(ordered, axis=0)


def fisher_and_groups(every, flat_width):
    row_count = flat_width // lax.axis_size("dp")
    col_count = flat_width // lax.axis_size("tensor")
    col_start = lax.axis_index("tensor") * col_count
    row_start = lax.axis_index("dp") * row_count
    every_group = every[:, flat_width].astype(jnp.int32)
    rows_part = lax.dynamic_slice_in_dim(every, row_start, row_count, 1)
    cols_part = lax.dynamic_slice_in_dim(every, col_start, col_count, 1)
    fisher = lax.dot_general(
        rows_part, cols_part, (((0,), (0,)), ((), ())), preferred_element_type=f32
    )
    member = (every_group[:, None] == jnp.arange(GROUPS, dtype=jnp.int32)[None, :]).astype(bf16)
    group_grad = lax.dot_general(
        member, cols_part, (((0,), (0,)), ((), ())), preferred_element_type=f32
    )
    return fisher, group_grad


def small_sums(hidden_acts, output_grad, input_basis, output_basis):
    acts_part = jnp.dot(hidden_acts, input_basis, preferred_element_type=f32)
    grads_part = lax.dot_general(
        output_grad,
        output_basis,
        (((0, 1, 2), (0, 1, 2)), ((), ())),
        preferred_element_type=f32,
    )
    return jnp.concatenate([acts_part, grads_part], axis=1)


def any_mesh(
    hidden_acts, output_grad, down_weight, input_basis, output_basis, token_example, example_group
):
    pieces = lax.all_to_all(output_grad, "dp", split_axis=1, concat_axis=3, tiled=True)
    columns = lax.all_gather(pieces, "tensor", axis=0, tiled=True)
    parts = small_sums(hidden_acts, output_grad, input_basis, output_basis)
    terms = lax.dot_general(
        columns, down_weight, (((0, 1, 2), (0, 1, 2)), ((), ())), preferred_element_type=f32
    )
    hidden_grad = lax.psum_scatter(terms.astype(bf16), "dp", scatter_dimension=0, tiled=True)
    acts_low, grads_low = jnp.split(lax.psum(parts, "tensor"), 2, axis=1)
    example_grad = example_gradients(
        acts_low, grads_low, token_example[0], example_group.shape[0]
    )
    every = order_examples(gather_examples(example_grad, example_group))
    fisher, group_grad = fisher_and_groups(every, example_grad.shape[1])
    return (hidden_grad, fisher, group_grad)


def line_of_four(
    hidden_acts, output_grad, down_weight, input_basis, output_basis, token_example, example_group
):
    tokens, cols = hidden_acts.shape
    part, rows = cols // 2, tokens // 2
    place = lax.axis_index("dp")
    turned = jnp.transpose(output_grad[0], (0, 2, 1))
    pieces = [lax.dynamic_index_in_dim(turned, place ^ k, 0, keepdims=False) for k in range(4)]
    far = []
    for half in range(2):
        cut = slice(half * rows, (half + 1) * rows)
        far.append(jnp.concatenate([swap(pieces[3][cut], 3), swap(pieces[2][cut], 2)]))
    beside, own = swap(pieces[1], 1), pieces[0]
    parts = small_sums(hidden_acts, output_grad, input_basis, output_basis)
    low = parts + across(parts, 1)

    blocks = spread_direct(after(far[0], parts))
    low = after(low, *blocks[1:])
    partner = across(low, 2)
    far[1] = after(far[1], *blocks[1:])
    later_first = across(far[1], 1)

    def far_terms(chunk, at, *earlier):
        chunk = [after(chunk[0], *earlier)] + chunk[1:] if earlier else chunk
        return block_terms([chunk], down_weight, at * part, part, [rows // 2, rows // 2, rows])

    def pair_sum(first, last, kept, *earlier):
        (pair,) = add_halves(kept, swap(after(first, *earlier), 1), swap(after(last, *earlier), 1))
        return pair, swap(pair, 2)

    first, last, kept = far_terms(blocks, 0)
    pair0, sum0 = pair_sum(first, last, kept, partner, later_first)

    later = [far[1], later_first, across(after(far[1], pair0), 2)]
    first, last, kept = far_terms(blocks, 1, pair0)
    pair1, sum1 = pair_sum(first, last, kept, later[2])

    later = spread_last(later, pair1)
    beside = spread_first(after(beside, pair1, *later[3:]))
    acts_low, grads_low = jnp.split(after(low, pair1, sum0) + partner, 2, axis=1)
    example_grad = example_gradients(
        acts_low, grads_low, token_example[0], example_group.shape[0]
    )
    gathered = gather_examples(example_grad, example_group)
    first, last, kept = far_terms(later, 0, example_grad)
    pair2, sum2 = pair_sum(first, last, kept, *beside)

    beside = spread_last(beside, pair2)
    own = after(own, pair2)
    own_first = across(own, 1)
    every = order_examples(after(gathered, pair2, sum1))
    fisher, group_grad = fisher_and_groups(every, example_grad.shape[1])
    first, last, kept = far_terms(later, 1, fisher, group_grad)
    first, last = (swap(after(term, own_first, *beside), 1) for term in (first, last))
    pair3 = add_halves(kept, first, last, 2)
    sum3 = [swap(term, 2) for term in pair3]

    own = [own, own_first, across(after(own, pair3[0]), 2)]
    beside = [after(beside[0], pair3[0], sum2)] + beside[1:]
    near = block_terms([beside], down_weight, 0, cols, [rows // 2] * 4, parts=2)
    near = [swap(after(term, own[2], sum3[0]), 1) for term in near]
    own = spread_last(own, *near[:1])
    adds = [gather_sums(near[:4], [sum0, sum2]), gather_sums(near[4:], [sum1])]
    (result,) = block_terms([own], down_weight, 0, cols, [tokens], adds, sum3)
    return (result, fisher, group_grad)


def per_device(hidden_acts, output_grad, down_weight, *rest):
    fits = lax.axis_size("tensor") == 4 and lax.axis_size("dp") == 4
    fits = fits and down_weight.shape[2] % 128 == 0 and down_weight.shape[3] % 1024 == 0
    fits = fits and hidden_acts.shape[0] % 64 == 0
    return (line_of_four if fits else any_mesh)(hidden_acts, output_grad, down_weight, *rest)


def solution(mesh):
    return jax.shard_map(
        per_device,
        mesh=mesh,
        in_specs=(
            P(("parts", "dp"), "tensor"),
            P("tensor", None, None, ("parts", "dp")),
            P(None, "dp", None, "tensor"),
            P("tensor", None),
            P("tensor", None, None, None),
            P(("parts", "dp"), None),
            P(("parts", "dp")),
        ),
        out_specs=(
            P(("parts", "dp"), "tensor"),
            P(("parts", "dp"), "tensor"),
            P("parts", "tensor"),
        ),
        check_vma=False,
    )
```

```python
import functools

import jax
import jax.numpy as jnp
from jax import lax
from jax.experimental import pallas as pl
from jax.experimental.pallas import tpu as pltpu
from jax.sharding import PartitionSpec as P

GROUPS = 8

highest = lax.Precision.HIGHEST
f32, bf16 = jnp.float32, jnp.bfloat16


def swap(value, step):
    size = lax.axis_size("dp")
    return lax.ppermute(value, "dp", [(d, d ^ step) for d in range(size)])


def after(value, *earlier):
    return lax.optimization_barrier((value,) + earlier)[0]


def across(value, step, places=None):
    size = lax.axis_size("tensor")
    pairs = [(t, t ^ step) for t in range(size) if places is None or t in places]
    return lax.ppermute(value, "tensor", pairs)


def spread_first(block):
    second = across(block, 2)
    return [block, across(block, 1), second]


def spread_direct(block):
    second, third = across(block, 2), across(block, 3)
    return [block, across(block, 1), second, third]


def spread_last(blocks, *earlier):
    block, _, second = blocks
    middle = across(after(block, second, *earlier), 3, (1, 2))
    ends = across(after(second, *earlier), 1, (1, 2))
    return blocks + [middle, ends]


def terms_kernel(size, count, first, lows, place_ref, *refs):
    blocks, w_ref = refs[:count], refs[count]
    feats, held, sems, held_sems = refs[-4:]
    outs = refs[count + 1 : -4]
    add_refs = []
    if lows is not None:
        add_refs, outs = outs[: 1 + lows], outs[-1:]
    width, tile = feats.shape[1] // size, outs[0].shape[1]
    j, steps = pl.program_id(0), pl.num_programs(0)
    slots = held.shape[0]

    def put(value, source, slot):
        at = pl.ds(pl.multiple_of(source * width, width), width)
        return pltpu.make_async_copy(value, feats.at[:, at], sems.at[slot])

    def fetch(step):
        slot = lax.rem(step, slots)
        at = pl.ds(pl.multiple_of(first + step * tile, tile), tile)
        return pltpu.make_async_copy(w_ref.at[:, 0, :, at], held.at[slot], held_sems.at[slot])

    @pl.when(j == 0)
    def _():
        place = place_ref[0]
        straight = 3 if count == 5 else 4
        copies = [put(blocks[k], lax.bitwise_xor(place, k), k) for k in range(straight)]
        for copy in copies:
            copy.start()
        for step in range(slots):
            fetch(step).start()
        inside = jnp.logical_or(place == 1, place == 2)
        relayed = ((inside, 3), (jnp.logical_not(inside), 4)) if count == 5 else ()
        for chosen, k in relayed:

            @pl.when(chosen)
            def _():
                last = put(blocks[k], lax.bitwise_xor(place, 3), 3)
                last.start()
                last.wait()

        for copy in copies:
            copy.wait()

    fetch(j).wait()
    weight = held[lax.rem(j, slots)].reshape(size * width, tile)
    terms = jnp.dot(feats[...], weight, preferred_element_type=f32)
    if add_refs:
        terms = terms + add_refs[0][...].astype(f32)
    row = 0
    for low_ref in reversed(add_refs[1:]):
        row += low_ref.shape[0]
        cut = slice(feats.shape[0] - row, feats.shape[0] - row + low_ref.shape[0])
        outs[0][cut] = (terms[cut] + low_ref[...].astype(f32)).astype(bf16)
    if add_refs:
        outs[0][: feats.shape[0] - row] = terms[: feats.shape[0] - row].astype(bf16)
    else:
        for out_ref in outs:
            out_ref[...] = terms[row : row + out_ref.shape[0]].astype(bf16)
            row += out_ref.shape[0]

    @pl.when(j + slots < steps)
    def _():
        fetch(j + slots).start()


def block_terms(blocks, down_weight, part, parts, outs, adds=None, into=None):
    size, _, width, every = down_weight.shape
    rows, cols = sum(outs), every // parts
    tile = max(n for n in range(128, 513, 128) if cols % n == 0)
    slots = min(4, cols // tile)

    def spec(tall, first=0):
        return pl.BlockSpec((tall, tile), lambda j, place: (0, first + j))

    operands = [*blocks, down_weight]
    in_specs = [pl.BlockSpec(memory_space=pltpu.HBM)] * len(operands)
    out_shape = [jax.ShapeDtypeStruct((tall, cols), bf16) for tall in outs]
    out_specs = [spec(tall) for tall in outs]
    aliases = {}
    if adds is not None:
        operands += adds
        in_specs += [spec(value.shape[0]) for value in adds]
        out_shape = [jax.ShapeDtypeStruct((rows, every), bf16)]
        out_specs = [spec(rows, part * (cols // tile))]
    if into is not None:
        operands.append(into)
        in_specs.append(pl.BlockSpec(memory_space=pltpu.HBM))
        aliases = {len(operands): 0}
    return pl.pallas_call(
        functools.partial(
            terms_kernel,
            size,
            len(blocks),
            part * cols,
            None if adds is None else len(adds) - 1,
        ),
        out_shape=out_shape,
        grid_spec=pltpu.PrefetchScalarGridSpec(
            num_scalar_prefetch=1,
            grid=(cols // tile,),
            in_specs=in_specs,
            out_specs=out_specs,
            scratch_shapes=[
                pltpu.VMEM((rows, size * width), bf16),
                pltpu.VMEM((slots, size, width, tile), bf16),
                pltpu.SemaphoreType.DMA((size,)),
                pltpu.SemaphoreType.DMA((slots,)),
            ],
        ),
        input_output_aliases=aliases,
        compiler_params=pltpu.CompilerParams(vmem_limit_bytes=24 << 20),
        cost_estimate=pl.CostEstimate(
            flops=rows * size * width * cols // 4, bytes_accessed=1000, transcendentals=0
        ),
        name="terms",
    )(lax.axis_index("tensor").reshape(1), *operands)


def add_kernel(count, kept_ref, *refs):
    pieces, outs = refs[:count], refs[count:]
    rows, tall = pieces[0].shape[0], outs[0].shape[0]
    for index, piece in enumerate(pieces):
        row = index * rows
        total = kept_ref[row : row + rows].astype(f32) + piece[...].astype(f32)
        outs[row // tall][row % tall : row % tall + rows] = total.astype(bf16)


def add_pieces(kept, pieces, outs=1):
    rows, cols = kept.shape
    tile = max(n for n in range(128, 1025, 128) if cols % n == 0)

    def spec(tall):
        return pl.BlockSpec((tall, tile), lambda j: (0, j))

    return pl.pallas_call(
        functools.partial(add_kernel, len(pieces)),
        out_shape=[jax.ShapeDtypeStruct((rows // outs, cols), bf16)] * outs,
        grid=(cols // tile,),
        in_specs=[spec(rows)] + [spec(rows // len(pieces))] * len(pieces),
        out_specs=[spec(rows // outs)] * outs,
        compiler_params=pltpu.CompilerParams(vmem_limit_bytes=16 << 20),
        cost_estimate=pl.CostEstimate(flops=1000, bytes_accessed=1000, transcendentals=0),
        name="pair",
    )(kept, *pieces)


def gather_sums_kernel(*refs):
    quarters, sums, out_ref = refs[:4], refs[4:-1], refs[-1]
    rows = quarters[0].shape[0]
    for index, ref in enumerate(quarters):
        value = ref[...]
        if index // 2 < len(sums):
            at = (index % 2) * rows
            other = sums[index // 2][at : at + rows]
            value = (value.astype(f32) + other.astype(f32)).astype(bf16)
        out_ref[index * rows : (index + 1) * rows] = value


def gather_sums(quarters, sums):
    rows, cols = quarters[0].shape
    tile = max(n for n in range(128, 2049, 128) if cols % n == 0)

    def spec(tall):
        return pl.BlockSpec((tall, tile), lambda j: (0, j))

    return pl.pallas_call(
        gather_sums_kernel,
        out_shape=jax.ShapeDtypeStruct((4 * rows, cols), bf16),
        grid=(cols // tile,),
        in_specs=[spec(rows)] * 4 + [spec(2 * rows)] * len(sums),
        out_specs=spec(4 * rows),
        compiler_params=pltpu.CompilerParams(vmem_limit_bytes=24 << 20),
        cost_estimate=pl.CostEstimate(flops=1000, bytes_accessed=1000, transcendentals=0),
        name="sums",
    )(*quarters, *sums)


def example_gradients(acts_low, grads_low, local_ids, examples):
    onehot = (local_ids[:, None] == jnp.arange(examples, dtype=jnp.int32)[None, :]).astype(f32)
    counts = jnp.sum(onehot, axis=0)
    spread = (onehot[:, :, None] * acts_low[:, None, :]).reshape(onehot.shape[0], -1)
    outer_sum = lax.dot_general(
        spread,
        grads_low,
        (((0,), (0,)), ((), ())),
        precision=highest,
        preferred_element_type=f32,
    )
    basis_rank = acts_low.shape[1]
    outer_sum = outer_sum.reshape(examples, basis_rank * grads_low.shape[1]) / counts[:, None]
    return outer_sum.astype(bf16)


def gather_examples(example_grad, example_group):
    count = example_grad.shape[0]
    group_column = jnp.broadcast_to(example_group.astype(bf16)[:, None], (count, 128))
    held = jnp.concatenate([example_grad, group_column], axis=1)
    return [held] + [swap(held, step) for step in range(1, lax.axis_size("dp"))]


def order_examples(values):
    groups, place = lax.axis_size("dp"), lax.axis_index("dp")
    ordered = []
    for group in range(groups):
        value = values[0]
        for step in range(1, groups):
            value = jnp.where((place ^ group) == step, values[step], value)
        ordered.append(value)
    return jnp.concatenate(ordered, axis=0)


def fisher_and_groups(every, flat_width):
    row_count = flat_width // lax.axis_size("dp")
    col_count = flat_width // lax.axis_size("tensor")
    col_start = lax.axis_index("tensor") * col_count
    row_start = lax.axis_index("dp") * row_count
    every_group = every[:, flat_width].astype(jnp.int32)
    rows_part = lax.dynamic_slice_in_dim(every, row_start, row_count, 1)
    cols_part = lax.dynamic_slice_in_dim(every, col_start, col_count, 1)
    fisher = lax.dot_general(
        rows_part, cols_part, (((0,), (0,)), ((), ())), preferred_element_type=f32
    )
    member = (every_group[:, None] == jnp.arange(GROUPS, dtype=jnp.int32)[None, :]).astype(bf16)
    group_grad = lax.dot_general(
        member, cols_part, (((0,), (0,)), ((), ())), preferred_element_type=f32
    )
    return fisher, group_grad


def small_sums(hidden_acts, output_grad, input_basis, output_basis):
    acts_part = jnp.dot(hidden_acts, input_basis, preferred_element_type=f32)
    grads_part = lax.dot_general(
        output_grad,
        output_basis,
        (((0, 1, 2), (0, 1, 2)), ((), ())),
        preferred_element_type=f32,
    )
    return jnp.concatenate([acts_part, grads_part], axis=1)


def any_mesh(
    hidden_acts, output_grad, down_weight, input_basis, output_basis, token_example, example_group
):
    pieces = lax.all_to_all(output_grad, "dp", split_axis=1, concat_axis=3, tiled=True)
    columns = lax.all_gather(pieces, "tensor", axis=0, tiled=True)
    parts = small_sums(hidden_acts, output_grad, input_basis, output_basis)
    terms = lax.dot_general(
        columns, down_weight, (((0, 1, 2), (0, 1, 2)), ((), ())), preferred_element_type=f32
    )
    hidden_grad = lax.psum_scatter(terms.astype(bf16), "dp", scatter_dimension=0, tiled=True)
    acts_low, grads_low = jnp.split(lax.psum(parts, "tensor"), 2, axis=1)
    example_grad = example_gradients(
        acts_low, grads_low, token_example[0], example_group.shape[0]
    )
    every = order_examples(gather_examples(example_grad, example_group))
    fisher, group_grad = fisher_and_groups(every, example_grad.shape[1])
    return (hidden_grad, fisher, group_grad)


def line_of_four(
    hidden_acts, output_grad, down_weight, input_basis, output_basis, token_example, example_group
):
    tokens = hidden_acts.shape[0]
    rows = tokens // 2
    place = lax.axis_index("dp")
    turned = jnp.transpose(output_grad[0], (0, 2, 1))
    pieces = [lax.dynamic_index_in_dim(turned, place ^ k, 0, keepdims=False) for k in range(4)]
    far = []
    for half in range(2):
        cut = slice(half * rows, (half + 1) * rows)
        far.append(jnp.concatenate([swap(pieces[3][cut], 3), swap(pieces[2][cut], 2)]))
    beside, own = swap(pieces[1], 1), pieces[0]
    parts = small_sums(hidden_acts, output_grad, input_basis, output_basis)
    low = parts + across(parts, 1)

    blocks = spread_direct(after(far[0], parts))
    low = after(low, *blocks[1:])
    partner = across(low, 2)
    far[1] = after(far[1], *blocks[1:])
    later_first = across(far[1], 1)

    def far_terms(chunk, at, pieces, *earlier):
        chunk = [after(chunk[0], *earlier)] + chunk[1:] if earlier else chunk
        outs = [rows // pieces] * pieces + [rows]
        *sent, kept = block_terms(chunk, down_weight, at, 2, outs)
        return sent, kept

    def pair_sum(sent, kept, *earlier, outs=1):
        pair = add_pieces(kept, [swap(after(term, *earlier), 1) for term in sent], outs)
        return pair[0], [swap(term, 2) for term in pair]

    sent, kept = far_terms(blocks, 0, 2, beside)
    pair0, sum0 = pair_sum(sent, kept, partner, later_first)

    later = after(far[1], pair0)
    later = [far[1], later_first, across(later, 2), across(later, 3)]
    sent, kept = far_terms(blocks, 1, 2, pair0)
    pair1, sum1 = pair_sum(sent, kept, *later[2:])

    beside = spread_first(after(beside, pair1))
    sent, kept = far_terms(later, 0, 2, pair1, *sum0)
    pair2, sum2 = pair_sum(sent, kept, *beside[1:])

    beside = spread_last(beside, pair2)
    own = after(own, pair2)
    own_first = across(own, 1)
    acts_low, grads_low = jnp.split(after(low, pair2, *sum1) + partner, 2, axis=1)
    example_grad = example_gradients(
        acts_low, grads_low, token_example[0], example_group.shape[0]
    )
    gathered = gather_examples(example_grad, example_group)
    sent, kept = far_terms(later, 1, 2, example_grad)
    pair3, sum3 = pair_sum(sent, kept, own_first, *beside, outs=2)

    own = [own, own_first, across(after(own, pair3), 2)]
    every = order_examples(after(gathered, pair3, *sum2))
    fisher, group_grad = fisher_and_groups(every, example_grad.shape[1])
    beside = [after(beside[0], fisher, group_grad)] + beside[1:]
    near0 = block_terms(beside, down_weight, 0, 2, [rows // 2] * 4)
    near0 = [swap(after(term, own[2], sum3[0]), 1) for term in near0]
    own = spread_last(own, *near0[:1])
    beside = [after(beside[0], *near0[:1])] + beside[1:]
    near1 = block_terms(beside, down_weight, 1, 2, [rows // 2] * 4)
    near1 = [swap(after(term, sum3[1]), 1) for term in near1]
    adds = [gather_sums(near0, sum0 + sum2)]
    (result,) = block_terms(own, down_weight, 0, 2, [tokens], adds)
    adds = [gather_sums(near1, sum1)] + sum3
    (result,) = block_terms(own, down_weight, 1, 2, [tokens], adds, result)
    return (result, fisher, group_grad)


def per_device(hidden_acts, output_grad, down_weight, *rest):
    fits = lax.axis_size("tensor") == 4 and lax.axis_size("dp") == 4
    fits = fits and down_weight.shape[2] % 128 == 0 and down_weight.shape[3] % 1024 == 0
    fits = fits and hidden_acts.shape[0] % 64 == 0
    return (line_of_four if fits else any_mesh)(hidden_acts, output_grad, down_weight, *rest)


def solution(mesh):
    return jax.shard_map(
        per_device,
        mesh=mesh,
        in_specs=(
            P(("parts", "dp"), "tensor"),
            P("tensor", None, None, ("parts", "dp")),
            P(None, "dp", None, "tensor"),
            P("tensor", None),
            P("tensor", None, None, None),
            P(("parts", "dp"), None),
            P(("parts", "dp")),
        ),
        out_specs=(
            P(("parts", "dp"), "tensor"),
            P(("parts", "dp"), "tensor"),
            P("parts", "tensor"),
        ),
        check_vma=False,
    )
```

```python
import functools

import jax
import jax.numpy as jnp
from jax import lax
from jax.experimental import pallas as pl
from jax.experimental.pallas import tpu as pltpu
from jax.sharding import PartitionSpec as P

GROUPS = 8

highest = lax.Precision.HIGHEST
f32, bf16 = jnp.float32, jnp.bfloat16


def swap(value, step):
    size = lax.axis_size("dp")
    return lax.ppermute(value, "dp", [(d, d ^ step) for d in range(size)])


def after(value, *earlier):
    return lax.optimization_barrier((value,) + earlier)[0]


def across(value, step, places=None):
    size = lax.axis_size("tensor")
    pairs = [(t, t ^ step) for t in range(size) if places is None or t in places]
    return lax.ppermute(value, "tensor", pairs)


def spread_first(block):
    second = across(block, 2)
    return [block, across(block, 1), second]


def spread_direct(block):
    second, third = across(block, 2), across(block, 3)
    return [block, across(block, 1), second, third]


def spread_last(blocks, *earlier):
    block, _, second = blocks
    middle = across(after(block, second, *earlier), 3, (1, 2))
    ends = across(after(second, *earlier), 1, (1, 2))
    return blocks + [middle, ends]


def terms_kernel(size, count, first, lows, place_ref, *refs):
    blocks, w_ref = refs[:count], refs[count]
    feats, held, sems, held_sems = refs[-4:]
    outs = refs[count + 1 : -4]
    add_refs = []
    if lows is not None:
        add_refs, outs = outs[: 1 + lows], outs[-1:]
    width, tile = feats.shape[1] // size, outs[0].shape[1]
    j, steps = pl.program_id(0), pl.num_programs(0)
    slots = held.shape[0]

    def put(value, source, slot):
        at = pl.ds(pl.multiple_of(source * width, width), width)
        return pltpu.make_async_copy(value, feats.at[:, at], sems.at[slot])

    def fetch(step):
        slot = lax.rem(step, slots)
        at = pl.ds(pl.multiple_of(first + step * tile, tile), tile)
        return pltpu.make_async_copy(w_ref.at[:, 0, :, at], held.at[slot], held_sems.at[slot])

    @pl.when(j == 0)
    def _():
        place = place_ref[0]
        straight = 3 if count == 5 else 4
        copies = [put(blocks[k], lax.bitwise_xor(place, k), k) for k in range(straight)]
        for copy in copies:
            copy.start()
        for step in range(slots):
            fetch(step).start()
        inside = jnp.logical_or(place == 1, place == 2)
        relayed = ((inside, 3), (jnp.logical_not(inside), 4)) if count == 5 else ()
        for chosen, k in relayed:

            @pl.when(chosen)
            def _():
                last = put(blocks[k], lax.bitwise_xor(place, 3), 3)
                last.start()
                last.wait()

        for copy in copies:
            copy.wait()

    fetch(j).wait()
    weight = held[lax.rem(j, slots)].reshape(size * width, tile)
    terms = jnp.dot(feats[...], weight, preferred_element_type=f32)
    if add_refs:
        terms = terms + add_refs[0][...].astype(f32)
    row = 0
    for low_ref in reversed(add_refs[1:]):
        row += low_ref.shape[0]
        cut = slice(feats.shape[0] - row, feats.shape[0] - row + low_ref.shape[0])
        outs[0][cut] = (terms[cut] + low_ref[...].astype(f32)).astype(bf16)
    if add_refs:
        outs[0][: feats.shape[0] - row] = terms[: feats.shape[0] - row].astype(bf16)
    else:
        for out_ref in outs:
            out_ref[...] = terms[row : row + out_ref.shape[0]].astype(bf16)
            row += out_ref.shape[0]

    @pl.when(j + slots < steps)
    def _():
        fetch(j + slots).start()


def block_terms(blocks, down_weight, part, parts, outs, adds=None, into=None):
    size, _, width, every = down_weight.shape
    rows, cols = sum(outs), every // parts
    tile = max(n for n in range(128, 513, 128) if cols % n == 0)
    slots = min(4, cols // tile)

    def spec(tall, first=0):
        return pl.BlockSpec((tall, tile), lambda j, place: (0, first + j))

    operands = [*blocks, down_weight]
    in_specs = [pl.BlockSpec(memory_space=pltpu.HBM)] * len(operands)
    out_shape = [jax.ShapeDtypeStruct((tall, cols), bf16) for tall in outs]
    out_specs = [spec(tall) for tall in outs]
    aliases = {}
    if adds is not None:
        operands += adds
        in_specs += [spec(value.shape[0]) for value in adds]
        out_shape = [jax.ShapeDtypeStruct((rows, every), bf16)]
        out_specs = [spec(rows, part * (cols // tile))]
    if into is not None:
        operands.append(into)
        in_specs.append(pl.BlockSpec(memory_space=pltpu.HBM))
        aliases = {len(operands): 0}
    return pl.pallas_call(
        functools.partial(
            terms_kernel,
            size,
            len(blocks),
            part * cols,
            None if adds is None else len(adds) - 1,
        ),
        out_shape=out_shape,
        grid_spec=pltpu.PrefetchScalarGridSpec(
            num_scalar_prefetch=1,
            grid=(cols // tile,),
            in_specs=in_specs,
            out_specs=out_specs,
            scratch_shapes=[
                pltpu.VMEM((rows, size * width), bf16),
                pltpu.VMEM((slots, size, width, tile), bf16),
                pltpu.SemaphoreType.DMA((size,)),
                pltpu.SemaphoreType.DMA((slots,)),
            ],
        ),
        input_output_aliases=aliases,
        compiler_params=pltpu.CompilerParams(vmem_limit_bytes=24 << 20),
        cost_estimate=pl.CostEstimate(
            flops=rows * size * width * cols // 4, bytes_accessed=1000, transcendentals=0
        ),
        name="terms",
    )(lax.axis_index("tensor").reshape(1), *operands)


def add_kernel(count, kept_ref, *refs):
    pieces, outs = refs[:count], refs[count:]
    rows, tall = pieces[0].shape[0], outs[0].shape[0]
    for index, piece in enumerate(pieces):
        row = index * rows
        total = kept_ref[row : row + rows].astype(f32) + piece[...].astype(f32)
        outs[row // tall][row % tall : row % tall + rows] = total.astype(bf16)


def add_pieces(kept, pieces, outs=1):
    rows, cols = kept.shape
    tile = max(n for n in range(128, 1025, 128) if cols % n == 0)

    def spec(tall):
        return pl.BlockSpec((tall, tile), lambda j: (0, j))

    return pl.pallas_call(
        functools.partial(add_kernel, len(pieces)),
        out_shape=[jax.ShapeDtypeStruct((rows // outs, cols), bf16)] * outs,
        grid=(cols // tile,),
        in_specs=[spec(rows)] + [spec(rows // len(pieces))] * len(pieces),
        out_specs=[spec(rows // outs)] * outs,
        compiler_params=pltpu.CompilerParams(vmem_limit_bytes=16 << 20),
        cost_estimate=pl.CostEstimate(flops=1000, bytes_accessed=1000, transcendentals=0),
        name="pair",
    )(kept, *pieces)


def gather_sums_kernel(*refs):
    quarters, sums, out_ref = refs[:4], refs[4:-1], refs[-1]
    rows = quarters[0].shape[0]
    for index, ref in enumerate(quarters):
        value = ref[...]
        if index // 2 < len(sums):
            at = (index % 2) * rows
            other = sums[index // 2][at : at + rows]
            value = (value.astype(f32) + other.astype(f32)).astype(bf16)
        out_ref[index * rows : (index + 1) * rows] = value


def gather_sums(quarters, sums):
    rows, cols = quarters[0].shape
    tile = max(n for n in range(128, 2049, 128) if cols % n == 0)

    def spec(tall):
        return pl.BlockSpec((tall, tile), lambda j: (0, j))

    return pl.pallas_call(
        gather_sums_kernel,
        out_shape=jax.ShapeDtypeStruct((4 * rows, cols), bf16),
        grid=(cols // tile,),
        in_specs=[spec(rows)] * 4 + [spec(2 * rows)] * len(sums),
        out_specs=spec(4 * rows),
        compiler_params=pltpu.CompilerParams(vmem_limit_bytes=24 << 20),
        cost_estimate=pl.CostEstimate(flops=1000, bytes_accessed=1000, transcendentals=0),
        name="sums",
    )(*quarters, *sums)


def example_gradients(acts_low, grads_low, local_ids, examples):
    onehot = (local_ids[:, None] == jnp.arange(examples, dtype=jnp.int32)[None, :]).astype(f32)
    counts = jnp.sum(onehot, axis=0)
    spread = (onehot[:, :, None] * acts_low[:, None, :]).reshape(onehot.shape[0], -1)
    outer_sum = lax.dot_general(
        spread,
        grads_low,
        (((0,), (0,)), ((), ())),
        precision=highest,
        preferred_element_type=f32,
    )
    basis_rank = acts_low.shape[1]
    outer_sum = outer_sum.reshape(examples, basis_rank * grads_low.shape[1]) / counts[:, None]
    return outer_sum.astype(bf16)


def gather_examples(example_grad, example_group):
    count = example_grad.shape[0]
    group_column = jnp.broadcast_to(example_group.astype(bf16)[:, None], (count, 128))
    held = jnp.concatenate([example_grad, group_column], axis=1)
    return [held] + [swap(held, step) for step in range(1, lax.axis_size("dp"))]


def order_examples(values):
    groups, place = lax.axis_size("dp"), lax.axis_index("dp")
    ordered = []
    for group in range(groups):
        value = values[0]
        for step in range(1, groups):
            value = jnp.where((place ^ group) == step, values[step], value)
        ordered.append(value)
    return jnp.concatenate(ordered, axis=0)


def fisher_and_groups(every, flat_width):
    row_count = flat_width // lax.axis_size("dp")
    col_count = flat_width // lax.axis_size("tensor")
    col_start = lax.axis_index("tensor") * col_count
    row_start = lax.axis_index("dp") * row_count
    every_group = every[:, flat_width].astype(jnp.int32)
    rows_part = lax.dynamic_slice_in_dim(every, row_start, row_count, 1)
    cols_part = lax.dynamic_slice_in_dim(every, col_start, col_count, 1)
    fisher = lax.dot_general(
        rows_part, cols_part, (((0,), (0,)), ((), ())), preferred_element_type=f32
    )
    member = (every_group[:, None] == jnp.arange(GROUPS, dtype=jnp.int32)[None, :]).astype(bf16)
    group_grad = lax.dot_general(
        member, cols_part, (((0,), (0,)), ((), ())), preferred_element_type=f32
    )
    return fisher, group_grad


def small_sums(hidden_acts, output_grad, input_basis, output_basis):
    acts_part = jnp.dot(hidden_acts, input_basis, preferred_element_type=f32)
    grads_part = lax.dot_general(
        output_grad,
        output_basis,
        (((0, 1, 2), (0, 1, 2)), ((), ())),
        preferred_element_type=f32,
    )
    return jnp.concatenate([acts_part, grads_part], axis=1)


def any_mesh(
    hidden_acts, output_grad, down_weight, input_basis, output_basis, token_example, example_group
):
    pieces = lax.all_to_all(output_grad, "dp", split_axis=1, concat_axis=3, tiled=True)
    columns = lax.all_gather(pieces, "tensor", axis=0, tiled=True)
    parts = small_sums(hidden_acts, output_grad, input_basis, output_basis)
    terms = lax.dot_general(
        columns, down_weight, (((0, 1, 2), (0, 1, 2)), ((), ())), preferred_element_type=f32
    )
    hidden_grad = lax.psum_scatter(terms.astype(bf16), "dp", scatter_dimension=0, tiled=True)
    acts_low, grads_low = jnp.split(lax.psum(parts, "tensor"), 2, axis=1)
    example_grad = example_gradients(
        acts_low, grads_low, token_example[0], example_group.shape[0]
    )
    every = order_examples(gather_examples(example_grad, example_group))
    fisher, group_grad = fisher_and_groups(every, example_grad.shape[1])
    return (hidden_grad, fisher, group_grad)


def line_of_four(
    hidden_acts, output_grad, down_weight, input_basis, output_basis, token_example, example_group
):
    tokens = hidden_acts.shape[0]
    rows = tokens // 2
    place = lax.axis_index("dp")
    turned = jnp.transpose(output_grad[0], (0, 2, 1))
    pieces = [lax.dynamic_index_in_dim(turned, place ^ k, 0, keepdims=False) for k in range(4)]
    far = []
    for half in range(2):
        cut = slice(half * rows, (half + 1) * rows)
        far.append(jnp.concatenate([swap(pieces[3][cut], 3), swap(pieces[2][cut], 2)]))
    beside, own = swap(pieces[1], 1), pieces[0]
    parts = small_sums(hidden_acts, output_grad, input_basis, output_basis)
    low = parts + across(parts, 1)

    blocks = spread_direct(after(far[0], parts))
    low = after(low, *blocks[1:])
    partner = across(low, 2)
    far[1] = after(far[1], *blocks[1:])
    later_first = across(far[1], 1)

    def far_terms(chunk, at, pieces, *earlier):
        chunk = [after(chunk[0], *earlier)] + chunk[1:] if earlier else chunk
        outs = [rows // pieces] * pieces + [rows]
        *sent, kept = block_terms(chunk, down_weight, at, 2, outs)
        return sent, kept

    def pair_sum(sent, kept, *earlier, outs=1):
        pair = add_pieces(kept, [swap(after(term, *earlier), 1) for term in sent], outs)
        return pair[0], [swap(term, 2) for term in pair]

    sent, kept = far_terms(blocks, 0, 2, beside)
    pair0, sum0 = pair_sum(sent, kept, partner, later_first)

    later = after(far[1], pair0)
    later = [far[1], later_first, across(later, 2), across(later, 3)]
    sent, kept = far_terms(blocks, 1, 2, pair0)
    pair1, sum1 = pair_sum(sent, kept, *later[2:])

    beside = spread_first(after(beside, pair1))
    sent, kept = far_terms(later, 0, 2, pair1, *sum0)
    pair2, sum2 = pair_sum(sent, kept, *beside[1:])

    beside = spread_last(beside, pair2)
    own = after(own, pair2)
    own_first = across(own, 1)
    acts_low, grads_low = jnp.split(after(low, pair2, *sum1) + partner, 2, axis=1)
    example_grad = example_gradients(
        acts_low, grads_low, token_example[0], example_group.shape[0]
    )
    gathered = gather_examples(example_grad, example_group)
    sent, kept = far_terms(later, 1, 4, example_grad)
    own = [own, own_first, across(own, 2)]
    pair3, sum3 = pair_sum(sent, after(kept, own[2]), own_first, *beside, outs=2)

    own = spread_last(own, pair3)
    beside = [after(beside[0], pair3, *sum2)] + beside[1:]
    near0 = block_terms(beside, down_weight, 0, 2, [rows // 2] * 4)
    near0 = [swap(after(term, sum3[0]), 1) for term in near0]
    beside = [after(beside[0], *near0[:1])] + beside[1:]
    near1 = block_terms(beside, down_weight, 1, 2, [rows // 2] * 4)
    every = order_examples(after(gathered, near1[0]))
    fisher, group_grad = fisher_and_groups(every, example_grad.shape[1])
    own = [after(own[0], near1[0])] + own[1:]
    near1 = [swap(after(term, sum3[1], *own[3:]), 1) for term in near1]
    adds = [gather_sums(near0, sum0 + sum2)]
    (result,) = block_terms(own, down_weight, 0, 2, [tokens], adds)
    adds = [gather_sums(near1, sum1)] + sum3
    own = [after(own[0], fisher, group_grad, result)] + own[1:]
    (result,) = block_terms(own, down_weight, 1, 2, [tokens], adds, result)
    return (result, fisher, group_grad)


def per_device(hidden_acts, output_grad, down_weight, *rest):
    fits = lax.axis_size("tensor") == 4 and lax.axis_size("dp") == 4
    fits = fits and down_weight.shape[2] % 128 == 0 and down_weight.shape[3] % 1024 == 0
    fits = fits and hidden_acts.shape[0] % 64 == 0
    return (line_of_four if fits else any_mesh)(hidden_acts, output_grad, down_weight, *rest)


def solution(mesh):
    return jax.shard_map(
        per_device,
        mesh=mesh,
        in_specs=(
            P(("parts", "dp"), "tensor"),
            P("tensor", None, None, ("parts", "dp")),
            P(None, "dp", None, "tensor"),
            P("tensor", None),
            P("tensor", None, None, None),
            P(("parts", "dp"), None),
            P(("parts", "dp")),
        ),
        out_specs=(
            P(("parts", "dp"), "tensor"),
            P(("parts", "dp"), "tensor"),
            P("parts", "tensor"),
        ),
        check_vma=False,
    )
```

```python
import functools

import jax
import jax.numpy as jnp
from jax import lax
from jax.experimental import pallas as pl
from jax.experimental.pallas import tpu as pltpu
from jax.sharding import PartitionSpec as P

GROUPS = 8

highest = lax.Precision.HIGHEST
f32, bf16 = jnp.float32, jnp.bfloat16


def swap(value, step):
    size = lax.axis_size("dp")
    return lax.ppermute(value, "dp", [(d, d ^ step) for d in range(size)])


def after(value, *earlier):
    return lax.optimization_barrier((value,) + earlier)[0]


def across(value, step, places=None):
    size = lax.axis_size("tensor")
    pairs = [(t, t ^ step) for t in range(size) if places is None or t in places]
    return lax.ppermute(value, "tensor", pairs)


def spread_first(block):
    second = across(block, 2)
    return [block, across(block, 1), second]


def spread_direct(block):
    second, third = across(block, 2), across(block, 3)
    return [block, across(block, 1), second, third]


def spread_last(blocks, *earlier):
    block, _, second = blocks
    middle = across(after(block, second, *earlier), 3, (1, 2))
    ends = across(after(second, *earlier), 1, (1, 2))
    return blocks + [middle, ends]


def terms_kernel(size, count, first, lows, place_ref, *refs):
    blocks, w_ref = refs[:count], refs[count]
    feats, held, sems, held_sems = refs[-4:]
    outs = refs[count + 1 : -4]
    add_refs = []
    if lows is not None:
        add_refs, outs = outs[: 1 + lows], outs[-1:]
    width, tile = feats.shape[1] // size, outs[0].shape[1]
    j, steps = pl.program_id(0), pl.num_programs(0)
    slots = held.shape[0]

    def put(value, source, slot):
        at = pl.ds(pl.multiple_of(source * width, width), width)
        return pltpu.make_async_copy(value, feats.at[:, at], sems.at[slot])

    def fetch(step):
        slot = lax.rem(step, slots)
        at = pl.ds(pl.multiple_of(first + step * tile, tile), tile)
        return pltpu.make_async_copy(w_ref.at[:, 0, :, at], held.at[slot], held_sems.at[slot])

    @pl.when(j == 0)
    def _():
        place = place_ref[0]
        straight = 3 if count == 5 else 4
        copies = [put(blocks[k], lax.bitwise_xor(place, k), k) for k in range(straight)]
        for copy in copies:
            copy.start()
        for step in range(slots):
            fetch(step).start()
        inside = jnp.logical_or(place == 1, place == 2)
        relayed = ((inside, 3), (jnp.logical_not(inside), 4)) if count == 5 else ()
        for chosen, k in relayed:

            @pl.when(chosen)
            def _():
                last = put(blocks[k], lax.bitwise_xor(place, 3), 3)
                last.start()
                last.wait()

        for copy in copies:
            copy.wait()

    fetch(j).wait()
    weight = held[lax.rem(j, slots)].reshape(size * width, tile)
    terms = jnp.dot(feats[...], weight, preferred_element_type=f32)
    if add_refs:
        terms = terms + add_refs[0][...].astype(f32)
    row = 0
    for low_ref in reversed(add_refs[1:]):
        row += low_ref.shape[0]
        cut = slice(feats.shape[0] - row, feats.shape[0] - row + low_ref.shape[0])
        outs[0][cut] = (terms[cut] + low_ref[...].astype(f32)).astype(bf16)
    if add_refs:
        outs[0][: feats.shape[0] - row] = terms[: feats.shape[0] - row].astype(bf16)
    else:
        for out_ref in outs:
            out_ref[...] = terms[row : row + out_ref.shape[0]].astype(bf16)
            row += out_ref.shape[0]

    @pl.when(j + slots < steps)
    def _():
        fetch(j + slots).start()


def block_terms(blocks, down_weight, part, parts, outs, adds=None, into=None):
    size, _, width, every = down_weight.shape
    rows, cols = sum(outs), every // parts
    tile = max(n for n in range(128, 513, 128) if cols % n == 0)
    slots = min(4, cols // tile)

    def spec(tall, first=0):
        return pl.BlockSpec((tall, tile), lambda j, place: (0, first + j))

    operands = [*blocks, down_weight]
    in_specs = [pl.BlockSpec(memory_space=pltpu.HBM)] * len(operands)
    out_shape = [jax.ShapeDtypeStruct((tall, cols), bf16) for tall in outs]
    out_specs = [spec(tall) for tall in outs]
    aliases = {}
    if adds is not None:
        operands += adds
        in_specs += [spec(value.shape[0]) for value in adds]
        out_shape = [jax.ShapeDtypeStruct((rows, every), bf16)]
        out_specs = [spec(rows, part * (cols // tile))]
    if into is not None:
        operands.append(into)
        in_specs.append(pl.BlockSpec(memory_space=pltpu.HBM))
        aliases = {len(operands): 0}
    return pl.pallas_call(
        functools.partial(
            terms_kernel,
            size,
            len(blocks),
            part * cols,
            None if adds is None else len(adds) - 1,
        ),
        out_shape=out_shape,
        grid_spec=pltpu.PrefetchScalarGridSpec(
            num_scalar_prefetch=1,
            grid=(cols // tile,),
            in_specs=in_specs,
            out_specs=out_specs,
            scratch_shapes=[
                pltpu.VMEM((rows, size * width), bf16),
                pltpu.VMEM((slots, size, width, tile), bf16),
                pltpu.SemaphoreType.DMA((size,)),
                pltpu.SemaphoreType.DMA((slots,)),
            ],
        ),
        input_output_aliases=aliases,
        compiler_params=pltpu.CompilerParams(vmem_limit_bytes=24 << 20),
        cost_estimate=pl.CostEstimate(
            flops=rows * size * width * cols // 4, bytes_accessed=1000, transcendentals=0
        ),
        name="terms",
    )(lax.axis_index("tensor").reshape(1), *operands)


def add_kernel(count, kept_ref, *refs):
    pieces, outs = refs[:count], refs[count:]
    rows, tall = pieces[0].shape[0], outs[0].shape[0]
    for index, piece in enumerate(pieces):
        row = index * rows
        total = kept_ref[row : row + rows].astype(f32) + piece[...].astype(f32)
        outs[row // tall][row % tall : row % tall + rows] = total.astype(bf16)


def add_pieces(kept, pieces, outs=1):
    rows, cols = kept.shape
    tile = max(n for n in range(128, 1025, 128) if cols % n == 0)

    def spec(tall):
        return pl.BlockSpec((tall, tile), lambda j: (0, j))

    return pl.pallas_call(
        functools.partial(add_kernel, len(pieces)),
        out_shape=[jax.ShapeDtypeStruct((rows // outs, cols), bf16)] * outs,
        grid=(cols // tile,),
        in_specs=[spec(rows)] + [spec(rows // len(pieces))] * len(pieces),
        out_specs=[spec(rows // outs)] * outs,
        compiler_params=pltpu.CompilerParams(vmem_limit_bytes=16 << 20),
        cost_estimate=pl.CostEstimate(flops=1000, bytes_accessed=1000, transcendentals=0),
        name="pair",
    )(kept, *pieces)


def gather_sums_kernel(*refs):
    quarters, sums, out_ref = refs[:4], refs[4:-1], refs[-1]
    rows = quarters[0].shape[0]
    for index, ref in enumerate(quarters):
        value = ref[...]
        if index // 2 < len(sums):
            at = (index % 2) * rows
            other = sums[index // 2][at : at + rows]
            value = (value.astype(f32) + other.astype(f32)).astype(bf16)
        out_ref[index * rows : (index + 1) * rows] = value


def gather_sums(quarters, sums):
    rows, cols = quarters[0].shape
    tile = max(n for n in range(128, 2049, 128) if cols % n == 0)

    def spec(tall):
        return pl.BlockSpec((tall, tile), lambda j: (0, j))

    return pl.pallas_call(
        gather_sums_kernel,
        out_shape=jax.ShapeDtypeStruct((4 * rows, cols), bf16),
        grid=(cols // tile,),
        in_specs=[spec(rows)] * 4 + [spec(2 * rows)] * len(sums),
        out_specs=spec(4 * rows),
        compiler_params=pltpu.CompilerParams(vmem_limit_bytes=24 << 20),
        cost_estimate=pl.CostEstimate(flops=1000, bytes_accessed=1000, transcendentals=0),
        name="sums",
    )(*quarters, *sums)


def example_gradients(acts_low, grads_low, local_ids, examples):
    onehot = (local_ids[:, None] == jnp.arange(examples, dtype=jnp.int32)[None, :]).astype(f32)
    counts = jnp.sum(onehot, axis=0)
    spread = (onehot[:, :, None] * acts_low[:, None, :]).reshape(onehot.shape[0], -1)
    outer_sum = lax.dot_general(
        spread,
        grads_low,
        (((0,), (0,)), ((), ())),
        precision=highest,
        preferred_element_type=f32,
    )
    basis_rank = acts_low.shape[1]
    outer_sum = outer_sum.reshape(examples, basis_rank * grads_low.shape[1]) / counts[:, None]
    return outer_sum.astype(bf16)


def gather_examples(example_grad, example_group):
    count = example_grad.shape[0]
    group_column = jnp.broadcast_to(example_group.astype(bf16)[:, None], (count, 128))
    held = jnp.concatenate([example_grad, group_column], axis=1)
    return [held] + [swap(held, step) for step in range(1, lax.axis_size("dp"))]


def order_examples(values):
    groups, place = lax.axis_size("dp"), lax.axis_index("dp")
    ordered = []
    for group in range(groups):
        value = values[0]
        for step in range(1, groups):
            value = jnp.where((place ^ group) == step, values[step], value)
        ordered.append(value)
    return jnp.concatenate(ordered, axis=0)


def fisher_and_groups(every, flat_width):
    row_count = flat_width // lax.axis_size("dp")
    col_count = flat_width // lax.axis_size("tensor")
    col_start = lax.axis_index("tensor") * col_count
    row_start = lax.axis_index("dp") * row_count
    every_group = every[:, flat_width].astype(jnp.int32)
    rows_part = lax.dynamic_slice_in_dim(every, row_start, row_count, 1)
    cols_part = lax.dynamic_slice_in_dim(every, col_start, col_count, 1)
    fisher = lax.dot_general(
        rows_part, cols_part, (((0,), (0,)), ((), ())), preferred_element_type=f32
    )
    member = (every_group[:, None] == jnp.arange(GROUPS, dtype=jnp.int32)[None, :]).astype(bf16)
    group_grad = lax.dot_general(
        member, cols_part, (((0,), (0,)), ((), ())), preferred_element_type=f32
    )
    return fisher, group_grad


def small_sums(hidden_acts, output_grad, input_basis, output_basis):
    acts_part = jnp.dot(hidden_acts, input_basis, preferred_element_type=f32)
    grads_part = lax.dot_general(
        output_grad,
        output_basis,
        (((0, 1, 2), (0, 1, 2)), ((), ())),
        preferred_element_type=f32,
    )
    return jnp.concatenate([acts_part, grads_part], axis=1)


def any_mesh(
    hidden_acts, output_grad, down_weight, input_basis, output_basis, token_example, example_group
):
    pieces = lax.all_to_all(output_grad, "dp", split_axis=1, concat_axis=3, tiled=True)
    columns = lax.all_gather(pieces, "tensor", axis=0, tiled=True)
    parts = small_sums(hidden_acts, output_grad, input_basis, output_basis)
    terms = lax.dot_general(
        columns, down_weight, (((0, 1, 2), (0, 1, 2)), ((), ())), preferred_element_type=f32
    )
    hidden_grad = lax.psum_scatter(terms.astype(bf16), "dp", scatter_dimension=0, tiled=True)
    acts_low, grads_low = jnp.split(lax.psum(parts, "tensor"), 2, axis=1)
    example_grad = example_gradients(
        acts_low, grads_low, token_example[0], example_group.shape[0]
    )
    every = order_examples(gather_examples(example_grad, example_group))
    fisher, group_grad = fisher_and_groups(every, example_grad.shape[1])
    return (hidden_grad, fisher, group_grad)


def line_of_four(
    hidden_acts, output_grad, down_weight, input_basis, output_basis, token_example, example_group
):
    tokens = hidden_acts.shape[0]
    rows = tokens // 2
    place = lax.axis_index("dp")
    turned = jnp.transpose(output_grad[0], (0, 2, 1))
    pieces = [lax.dynamic_index_in_dim(turned, place ^ k, 0, keepdims=False) for k in range(4)]
    far = []
    for half in range(2):
        cut = slice(half * rows, (half + 1) * rows)
        far.append(jnp.concatenate([swap(pieces[3][cut], 3), swap(pieces[2][cut], 2)]))
    beside, own = swap(pieces[1], 1), pieces[0]
    parts = small_sums(hidden_acts, output_grad, input_basis, output_basis)
    low = parts + across(parts, 1)

    blocks = spread_direct(after(far[0], parts))
    low = after(low, *blocks[1:])
    partner = across(low, 2)
    far[1] = after(far[1], *blocks[1:])
    later = spread_direct(far[1])

    def far_terms(chunk, at, pieces, *earlier):
        chunk = [after(chunk[0], *earlier)] + chunk[1:] if earlier else chunk
        outs = [rows // pieces] * pieces + [rows]
        *sent, kept = block_terms(chunk, down_weight, at, 2, outs)
        return sent, kept

    def pair_sum(sent, kept, *earlier, outs=1):
        pair = add_pieces(kept, [swap(after(term, *earlier), 1) for term in sent], outs)
        return pair[0], [swap(term, 2) for term in pair]

    sent0, kept0 = far_terms(blocks, 0, 2, beside)
    sent1, kept1 = far_terms(blocks, 1, 2, sent0[0])
    pair0, sum0 = pair_sum(sent0, kept0, partner, *later[1:], sent1[0])
    pair1, sum1 = pair_sum(sent1, kept1, *later[1:])

    beside = spread_first(after(beside, pair1))
    sent, kept = far_terms(later, 0, 2, pair0, pair1)
    pair2, sum2 = pair_sum(sent, kept, *beside[1:])

    beside = spread_last(beside, pair2)
    own = after(own, pair2)
    own_first = across(own, 1)
    acts_low, grads_low = jnp.split(after(low, pair2, *sum0) + partner, 2, axis=1)
    example_grad = example_gradients(
        acts_low, grads_low, token_example[0], example_group.shape[0]
    )
    gathered = gather_examples(example_grad, example_group)
    sent, kept = far_terms(later, 1, 2, example_grad)
    pair3, sum3 = pair_sum(sent, kept, own_first, *beside, outs=2)

    own = [own, own_first, across(after(own, pair3), 2)]
    beside = [after(beside[0], pair3, *sum1)] + beside[1:]
    near0 = block_terms(beside, down_weight, 0, 2, [rows // 2] * 4)
    near0 = [swap(after(term, own[2]), 1) for term in near0]
    own = spread_last(own, *near0[:1])
    beside = [after(beside[0], *near0[:1], *sum2)] + beside[1:]
    near1 = block_terms(beside, down_weight, 1, 2, [rows // 2] * 4)
    near1 = [swap(after(term, *own[3:]), 1) for term in near1]
    every = order_examples(after(gathered, near1[0]))
    fisher, group_grad = fisher_and_groups(every, example_grad.shape[1])
    near0 = [after(near0[0], near1[0])] + near0[1:]
    adds = [gather_sums(near0, sum0 + sum2)]
    own = [after(own[0], sum3[0])] + own[1:]
    (result,) = block_terms(own, down_weight, 0, 2, [tokens], adds)
    adds = [gather_sums(near1, sum1)] + sum3
    own = [after(own[0], fisher, group_grad, result)] + own[1:]
    (result,) = block_terms(own, down_weight, 1, 2, [tokens], adds, result)
    return (result, fisher, group_grad)


def per_device(hidden_acts, output_grad, down_weight, *rest):
    fits = lax.axis_size("tensor") == 4 and lax.axis_size("dp") == 4
    fits = fits and down_weight.shape[2] % 128 == 0 and down_weight.shape[3] % 1024 == 0
    fits = fits and hidden_acts.shape[0] % 64 == 0
    return (line_of_four if fits else any_mesh)(hidden_acts, output_grad, down_weight, *rest)


def solution(mesh):
    return jax.shard_map(
        per_device,
        mesh=mesh,
        in_specs=(
            P(("parts", "dp"), "tensor"),
            P("tensor", None, None, ("parts", "dp")),
            P(None, "dp", None, "tensor"),
            P("tensor", None),
            P("tensor", None, None, None),
            P(("parts", "dp"), None),
            P(("parts", "dp")),
        ),
        out_specs=(
            P(("parts", "dp"), "tensor"),
            P(("parts", "dp"), "tensor"),
            P("parts", "tensor"),
        ),
        check_vma=False,
    )
```

```python
import functools

import jax
import jax.numpy as jnp
from jax import lax
from jax.experimental import pallas as pl
from jax.experimental.pallas import tpu as pltpu
from jax.sharding import PartitionSpec as P

GROUPS = 8

highest = lax.Precision.HIGHEST
f32, bf16 = jnp.float32, jnp.bfloat16


def swap(value, step):
    size = lax.axis_size("dp")
    return lax.ppermute(value, "dp", [(d, d ^ step) for d in range(size)])


def after(value, *earlier):
    return lax.optimization_barrier((value,) + earlier)[0]


def across(value, step, places=None):
    size = lax.axis_size("tensor")
    pairs = [(t, t ^ step) for t in range(size) if places is None or t in places]
    return lax.ppermute(value, "tensor", pairs)


def spread_first(block):
    second = across(block, 2)
    return [block, across(block, 1), second]


def spread_direct(block):
    second, third = across(block, 2), across(block, 3)
    return [block, across(block, 1), second, third]


def spread_last(blocks, *earlier):
    block, _, second = blocks
    middle = across(after(block, second, *earlier), 3, (1, 2))
    ends = across(after(second, *earlier), 1, (1, 2))
    return blocks + [middle, ends]


def terms_kernel(size, count, first, lows, place_ref, *refs):
    blocks, w_ref = refs[:count], refs[count]
    feats, held, sems, held_sems = refs[-4:]
    outs = refs[count + 1 : -4]
    add_refs = []
    if lows is not None:
        add_refs, outs = outs[: 1 + lows], outs[-1:]
    width, tile = feats.shape[1] // size, outs[0].shape[1]
    j, steps = pl.program_id(0), pl.num_programs(0)
    slots = held.shape[0]

    def put(value, source, slot):
        at = pl.ds(pl.multiple_of(source * width, width), width)
        return pltpu.make_async_copy(value, feats.at[:, at], sems.at[slot])

    def fetch(step):
        slot = lax.rem(step, slots)
        at = pl.ds(pl.multiple_of(first + step * tile, tile), tile)
        return pltpu.make_async_copy(w_ref.at[:, 0, :, at], held.at[slot], held_sems.at[slot])

    @pl.when(j == 0)
    def _():
        place = place_ref[0]
        straight = 3 if count == 5 else 4
        copies = [put(blocks[k], lax.bitwise_xor(place, k), k) for k in range(straight)]
        for copy in copies:
            copy.start()
        for step in range(slots):
            fetch(step).start()
        inside = jnp.logical_or(place == 1, place == 2)
        relayed = ((inside, 3), (jnp.logical_not(inside), 4)) if count == 5 else ()
        for chosen, k in relayed:

            @pl.when(chosen)
            def _():
                last = put(blocks[k], lax.bitwise_xor(place, 3), 3)
                last.start()
                last.wait()

        for copy in copies:
            copy.wait()

    fetch(j).wait()
    weight = held[lax.rem(j, slots)].reshape(size * width, tile)
    terms = jnp.dot(feats[...], weight, preferred_element_type=f32)
    if add_refs:
        terms = terms + add_refs[0][...].astype(f32)
    row = 0
    for low_ref in reversed(add_refs[1:]):
        row += low_ref.shape[0]
        cut = slice(feats.shape[0] - row, feats.shape[0] - row + low_ref.shape[0])
        outs[0][cut] = (terms[cut] + low_ref[...].astype(f32)).astype(bf16)
    if add_refs:
        outs[0][: feats.shape[0] - row] = terms[: feats.shape[0] - row].astype(bf16)
    else:
        for out_ref in outs:
            out_ref[...] = terms[row : row + out_ref.shape[0]].astype(bf16)
            row += out_ref.shape[0]

    @pl.when(j + slots < steps)
    def _():
        fetch(j + slots).start()


def block_terms(blocks, down_weight, part, parts, outs, adds=None, into=None):
    size, _, width, every = down_weight.shape
    rows, cols = sum(outs), every // parts
    tile = max(n for n in range(128, 513, 128) if cols % n == 0)
    slots = min(4, cols // tile)

    def spec(tall, first=0):
        return pl.BlockSpec((tall, tile), lambda j, place: (0, first + j))

    operands = [*blocks, down_weight]
    in_specs = [pl.BlockSpec(memory_space=pltpu.HBM)] * len(operands)
    out_shape = [jax.ShapeDtypeStruct((tall, cols), bf16) for tall in outs]
    out_specs = [spec(tall) for tall in outs]
    aliases = {}
    if adds is not None:
        operands += adds
        in_specs += [spec(value.shape[0]) for value in adds]
        out_shape = [jax.ShapeDtypeStruct((rows, every), bf16)]
        out_specs = [spec(rows, part * (cols // tile))]
    if into is not None:
        operands.append(into)
        in_specs.append(pl.BlockSpec(memory_space=pltpu.HBM))
        aliases = {len(operands): 0}
    return pl.pallas_call(
        functools.partial(
            terms_kernel,
            size,
            len(blocks),
            part * cols,
            None if adds is None else len(adds) - 1,
        ),
        out_shape=out_shape,
        grid_spec=pltpu.PrefetchScalarGridSpec(
            num_scalar_prefetch=1,
            grid=(cols // tile,),
            in_specs=in_specs,
            out_specs=out_specs,
            scratch_shapes=[
                pltpu.VMEM((rows, size * width), bf16),
                pltpu.VMEM((slots, size, width, tile), bf16),
                pltpu.SemaphoreType.DMA((size,)),
                pltpu.SemaphoreType.DMA((slots,)),
            ],
        ),
        input_output_aliases=aliases,
        compiler_params=pltpu.CompilerParams(vmem_limit_bytes=24 << 20),
        cost_estimate=pl.CostEstimate(
            flops=rows * size * width * cols // 4, bytes_accessed=1000, transcendentals=0
        ),
        name="terms",
    )(lax.axis_index("tensor").reshape(1), *operands)


def add_kernel(count, kept_ref, *refs):
    pieces, outs = refs[:count], refs[count:]
    rows, tall = pieces[0].shape[0], outs[0].shape[0]
    for index, piece in enumerate(pieces):
        row = index * rows
        total = kept_ref[row : row + rows].astype(f32) + piece[...].astype(f32)
        outs[row // tall][row % tall : row % tall + rows] = total.astype(bf16)


def add_pieces(kept, pieces, outs=1):
    rows, cols = kept.shape
    tile = max(n for n in range(128, 1025, 128) if cols % n == 0)

    def spec(tall):
        return pl.BlockSpec((tall, tile), lambda j: (0, j))

    return pl.pallas_call(
        functools.partial(add_kernel, len(pieces)),
        out_shape=[jax.ShapeDtypeStruct((rows // outs, cols), bf16)] * outs,
        grid=(cols // tile,),
        in_specs=[spec(rows)] + [spec(rows // len(pieces))] * len(pieces),
        out_specs=[spec(rows // outs)] * outs,
        compiler_params=pltpu.CompilerParams(vmem_limit_bytes=16 << 20),
        cost_estimate=pl.CostEstimate(flops=1000, bytes_accessed=1000, transcendentals=0),
        name="pair",
    )(kept, *pieces)


def gather_sums_kernel(places, *refs):
    quarters, sums, out_ref = refs[:4], refs[4:-1], refs[-1]
    rows = quarters[0].shape[0]
    for index, ref in enumerate(quarters):
        value = ref[...].astype(f32)
        for place, other in zip(places, sums):
            at = (index - place) * rows
            if 0 <= at < other.shape[0]:
                value = value + other[at : at + rows].astype(f32)
        out_ref[index * rows : (index + 1) * rows] = value.astype(bf16)


def gather_sums(quarters, sums):
    rows, cols = quarters[0].shape
    tile = max(n for n in range(128, 2049, 128) if cols % n == 0)
    places = [sum(value.shape[0] for value in sums[:k]) // rows for k in range(len(sums))]

    def spec(tall):
        return pl.BlockSpec((tall, tile), lambda j: (0, j))

    return pl.pallas_call(
        functools.partial(gather_sums_kernel, places),
        out_shape=jax.ShapeDtypeStruct((4 * rows, cols), bf16),
        grid=(cols // tile,),
        in_specs=[spec(rows)] * 4 + [spec(value.shape[0]) for value in sums],
        out_specs=spec(4 * rows),
        compiler_params=pltpu.CompilerParams(vmem_limit_bytes=24 << 20),
        cost_estimate=pl.CostEstimate(flops=1000, bytes_accessed=1000, transcendentals=0),
        name="sums",
    )(*quarters, *sums)


def example_gradients(acts_low, grads_low, local_ids, examples):
    onehot = (local_ids[:, None] == jnp.arange(examples, dtype=jnp.int32)[None, :]).astype(f32)
    counts = jnp.sum(onehot, axis=0)
    spread = (onehot[:, :, None] * acts_low[:, None, :]).reshape(onehot.shape[0], -1)
    outer_sum = lax.dot_general(
        spread,
        grads_low,
        (((0,), (0,)), ((), ())),
        precision=highest,
        preferred_element_type=f32,
    )
    basis_rank = acts_low.shape[1]
    outer_sum = outer_sum.reshape(examples, basis_rank * grads_low.shape[1]) / counts[:, None]
    return outer_sum.astype(bf16)


def gather_examples(example_grad, example_group):
    count = example_grad.shape[0]
    group_column = jnp.broadcast_to(example_group.astype(bf16)[:, None], (count, 128))
    held = jnp.concatenate([example_grad, group_column], axis=1)
    return [held] + [swap(held, step) for step in range(1, lax.axis_size("dp"))]


def order_examples(values):
    groups, place = lax.axis_size("dp"), lax.axis_index("dp")
    ordered = []
    for group in range(groups):
        value = values[0]
        for step in range(1, groups):
            value = jnp.where((place ^ group) == step, values[step], value)
        ordered.append(value)
    return jnp.concatenate(ordered, axis=0)


def fisher_and_groups(every, flat_width):
    row_count = flat_width // lax.axis_size("dp")
    col_count = flat_width // lax.axis_size("tensor")
    col_start = lax.axis_index("tensor") * col_count
    row_start = lax.axis_index("dp") * row_count
    every_group = every[:, flat_width].astype(jnp.int32)
    rows_part = lax.dynamic_slice_in_dim(every, row_start, row_count, 1)
    cols_part = lax.dynamic_slice_in_dim(every, col_start, col_count, 1)
    fisher = lax.dot_general(
        rows_part, cols_part, (((0,), (0,)), ((), ())), preferred_element_type=f32
    )
    member = (every_group[:, None] == jnp.arange(GROUPS, dtype=jnp.int32)[None, :]).astype(bf16)
    group_grad = lax.dot_general(
        member, cols_part, (((0,), (0,)), ((), ())), preferred_element_type=f32
    )
    return fisher, group_grad


def small_sums(hidden_acts, output_grad, input_basis, output_basis):
    acts_part = jnp.dot(hidden_acts, input_basis, preferred_element_type=f32)
    grads_part = lax.dot_general(
        output_grad,
        output_basis,
        (((0, 1, 2), (0, 1, 2)), ((), ())),
        preferred_element_type=f32,
    )
    return jnp.concatenate([acts_part, grads_part], axis=1)


def any_mesh(
    hidden_acts, output_grad, down_weight, input_basis, output_basis, token_example, example_group
):
    pieces = lax.all_to_all(output_grad, "dp", split_axis=1, concat_axis=3, tiled=True)
    columns = lax.all_gather(pieces, "tensor", axis=0, tiled=True)
    parts = small_sums(hidden_acts, output_grad, input_basis, output_basis)
    terms = lax.dot_general(
        columns, down_weight, (((0, 1, 2), (0, 1, 2)), ((), ())), preferred_element_type=f32
    )
    hidden_grad = lax.psum_scatter(terms.astype(bf16), "dp", scatter_dimension=0, tiled=True)
    acts_low, grads_low = jnp.split(lax.psum(parts, "tensor"), 2, axis=1)
    example_grad = example_gradients(
        acts_low, grads_low, token_example[0], example_group.shape[0]
    )
    every = order_examples(gather_examples(example_grad, example_group))
    fisher, group_grad = fisher_and_groups(every, example_grad.shape[1])
    return (hidden_grad, fisher, group_grad)


def line_of_four(
    hidden_acts, output_grad, down_weight, input_basis, output_basis, token_example, example_group
):
    tokens = hidden_acts.shape[0]
    rows = tokens // 2
    place = lax.axis_index("dp")
    turned = jnp.transpose(output_grad[0], (0, 2, 1))
    pieces = [lax.dynamic_index_in_dim(turned, place ^ k, 0, keepdims=False) for k in range(4)]
    far = []
    for half in range(2):
        cut = slice(half * rows, (half + 1) * rows)
        far.append(jnp.concatenate([swap(pieces[3][cut], 3), swap(pieces[2][cut], 2)]))
    beside, own = swap(pieces[1], 1), pieces[0]
    parts = small_sums(hidden_acts, output_grad, input_basis, output_basis)
    low = parts + across(parts, 1)

    blocks = spread_direct(after(far[0], parts))
    low = after(low, *blocks[1:])
    partner = across(low, 2)
    far[1] = after(far[1], *blocks[1:])
    later = spread_direct(far[1])

    def far_terms(chunk, at, pieces, *earlier):
        chunk = [after(chunk[0], *earlier)] + chunk[1:] if earlier else chunk
        outs = [rows // pieces] * pieces + [rows]
        *sent, kept = block_terms(chunk, down_weight, at, 2, outs)
        return sent, kept

    def pair_sum(sent, kept, *earlier, outs=1):
        pair = add_pieces(kept, [swap(after(term, *earlier), 1) for term in sent], outs)
        return pair[0], [swap(term, 2) for term in pair]

    sent0, kept0 = far_terms(blocks, 0, 2, beside)
    sent1, kept1 = far_terms(blocks, 1, 2, sent0[0])
    pair0, sum0 = pair_sum(sent0, kept0, partner, *later[1:], sent1[0])
    pair1, sum1 = pair_sum(sent1, kept1, *later[1:])

    beside = spread_first(after(beside, pair1))
    sent, kept = far_terms(later, 0, 2, pair0, pair1)
    pair2, sum2 = pair_sum(sent, kept, *beside[1:], outs=2)

    beside = spread_last(beside, pair2)
    own = after(own, pair2)
    own_first = across(own, 1)
    own = [own, own_first, across(own, 2)]
    acts_low, grads_low = jnp.split(after(low, pair2, *sum0) + partner, 2, axis=1)
    example_grad = example_gradients(
        acts_low, grads_low, token_example[0], example_group.shape[0]
    )
    gathered = gather_examples(example_grad, example_group)
    sent, kept = far_terms(later, 1, 4, example_grad)
    pair3, sum3 = pair_sum(sent, after(kept, own[2]), own_first, *beside, outs=2)

    own = spread_last(own, pair3)
    beside = [after(beside[0], pair3, *sum1)] + beside[1:]
    near0 = block_terms(beside, down_weight, 0, 2, [rows // 2] * 4)
    near0 = [swap(term, 1) for term in near0]
    beside = [after(beside[0], near0[0], sum2[0])] + beside[1:]
    near1 = block_terms(beside, down_weight, 1, 2, [rows // 2] * 4)
    every = order_examples(after(gathered, near1[0]))
    fisher, group_grad = fisher_and_groups(every, example_grad.shape[1])
    own = [after(own[0], near1[0], sum3[0])] + own[1:]
    near1 = [swap(after(term, *own[3:]), 1) for term in near1]
    adds = [gather_sums(near0, sum0 + sum2)]
    (result,) = block_terms(own, down_weight, 0, 2, [tokens], adds)
    adds = [gather_sums(near1, sum1)] + sum3
    own = [after(own[0], fisher, group_grad, result)] + own[1:]
    (result,) = block_terms(own, down_weight, 1, 2, [tokens], adds, result)
    return (result, fisher, group_grad)


def per_device(hidden_acts, output_grad, down_weight, *rest):
    fits = lax.axis_size("tensor") == 4 and lax.axis_size("dp") == 4
    fits = fits and down_weight.shape[2] % 128 == 0 and down_weight.shape[3] % 1024 == 0
    fits = fits and hidden_acts.shape[0] % 64 == 0
    return (line_of_four if fits else any_mesh)(hidden_acts, output_grad, down_weight, *rest)


def solution(mesh):
    return jax.shard_map(
        per_device,
        mesh=mesh,
        in_specs=(
            P(("parts", "dp"), "tensor"),
            P("tensor", None, None, ("parts", "dp")),
            P(None, "dp", None, "tensor"),
            P("tensor", None),
            P("tensor", None, None, None),
            P(("parts", "dp"), None),
            P(("parts", "dp")),
        ),
        out_specs=(
            P(("parts", "dp"), "tensor"),
            P(("parts", "dp"), "tensor"),
            P("parts", "tensor"),
        ),
        check_vma=False,
    )
```

```python
import functools

import jax
import jax.numpy as jnp
from jax import lax
from jax.experimental import pallas as pl
from jax.experimental.pallas import tpu as pltpu
from jax.sharding import PartitionSpec as P

GROUPS = 8

highest = lax.Precision.HIGHEST
f32, bf16 = jnp.float32, jnp.bfloat16


def swap(value, step):
    size = lax.axis_size("dp")
    return lax.ppermute(value, "dp", [(d, d ^ step) for d in range(size)])


def after(value, *earlier):
    return lax.optimization_barrier((value,) + earlier)[0]


def across(value, step, places=None):
    size = lax.axis_size("tensor")
    pairs = [(t, t ^ step) for t in range(size) if places is None or t in places]
    return lax.ppermute(value, "tensor", pairs)


def spread_first(block):
    second = across(block, 2)
    return [block, across(block, 1), second]


def spread_direct(block):
    second, third = across(block, 2), across(block, 3)
    return [block, across(block, 1), second, third]


def spread_last(blocks, *earlier):
    block, _, second = blocks
    middle = across(after(block, second, *earlier), 3, (1, 2))
    ends = across(after(second, *earlier), 1, (1, 2))
    return blocks + [middle, ends]


def terms_kernel(size, count, first, lows, place_ref, *refs):
    blocks, w_ref = refs[:count], refs[count]
    feats, held, sems, held_sems = refs[-4:]
    outs = refs[count + 1 : -4]
    add_refs = []
    if lows is not None:
        add_refs, outs = outs[: 1 + lows], outs[-1:]
    width, tile = feats.shape[1] // size, outs[0].shape[1]
    j, steps = pl.program_id(0), pl.num_programs(0)
    slots = held.shape[0]

    def put(value, source, slot):
        at = pl.ds(pl.multiple_of(source * width, width), width)
        return pltpu.make_async_copy(value, feats.at[:, at], sems.at[slot])

    def fetch(step):
        slot = lax.rem(step, slots)
        at = pl.ds(pl.multiple_of(first + step * tile, tile), tile)
        return pltpu.make_async_copy(w_ref.at[:, 0, :, at], held.at[slot], held_sems.at[slot])

    @pl.when(j == 0)
    def _():
        place = place_ref[0]
        straight = 3 if count == 5 else 4
        copies = [put(blocks[k], lax.bitwise_xor(place, k), k) for k in range(straight)]
        for copy in copies:
            copy.start()
        for step in range(slots):
            fetch(step).start()
        inside = jnp.logical_or(place == 1, place == 2)
        relayed = ((inside, 3), (jnp.logical_not(inside), 4)) if count == 5 else ()
        for chosen, k in relayed:

            @pl.when(chosen)
            def _():
                last = put(blocks[k], lax.bitwise_xor(place, 3), 3)
                last.start()
                last.wait()

        for copy in copies:
            copy.wait()

    fetch(j).wait()
    weight = held[lax.rem(j, slots)].reshape(size * width, tile)
    terms = jnp.dot(feats[...], weight, preferred_element_type=f32)
    if add_refs:
        terms = terms + add_refs[0][...].astype(f32)
    row = 0
    for low_ref in reversed(add_refs[1:]):
        row += low_ref.shape[0]
        cut = slice(feats.shape[0] - row, feats.shape[0] - row + low_ref.shape[0])
        outs[0][cut] = (terms[cut] + low_ref[...].astype(f32)).astype(bf16)
    if add_refs:
        outs[0][: feats.shape[0] - row] = terms[: feats.shape[0] - row].astype(bf16)
    else:
        for out_ref in outs:
            out_ref[...] = terms[row : row + out_ref.shape[0]].astype(bf16)
            row += out_ref.shape[0]

    @pl.when(j + slots < steps)
    def _():
        fetch(j + slots).start()


def block_terms(blocks, down_weight, part, parts, outs, adds=None, into=None):
    size, _, width, every = down_weight.shape
    rows, cols = sum(outs), every // parts
    tile = max(n for n in range(128, 513, 128) if cols % n == 0)
    slots = min(4, cols // tile)

    def spec(tall, first=0):
        return pl.BlockSpec((tall, tile), lambda j, place: (0, first + j))

    operands = [*blocks, down_weight]
    in_specs = [pl.BlockSpec(memory_space=pltpu.HBM)] * len(operands)
    out_shape = [jax.ShapeDtypeStruct((tall, cols), bf16) for tall in outs]
    out_specs = [spec(tall) for tall in outs]
    aliases = {}
    if adds is not None:
        operands += adds
        in_specs += [spec(value.shape[0]) for value in adds]
        out_shape = [jax.ShapeDtypeStruct((rows, every), bf16)]
        out_specs = [spec(rows, part * (cols // tile))]
    if into is not None:
        operands.append(into)
        in_specs.append(pl.BlockSpec(memory_space=pltpu.HBM))
        aliases = {len(operands): 0}
    return pl.pallas_call(
        functools.partial(
            terms_kernel,
            size,
            len(blocks),
            part * cols,
            None if adds is None else len(adds) - 1,
        ),
        out_shape=out_shape,
        grid_spec=pltpu.PrefetchScalarGridSpec(
            num_scalar_prefetch=1,
            grid=(cols // tile,),
            in_specs=in_specs,
            out_specs=out_specs,
            scratch_shapes=[
                pltpu.VMEM((rows, size * width), bf16),
                pltpu.VMEM((slots, size, width, tile), bf16),
                pltpu.SemaphoreType.DMA((size,)),
                pltpu.SemaphoreType.DMA((slots,)),
            ],
        ),
        input_output_aliases=aliases,
        compiler_params=pltpu.CompilerParams(vmem_limit_bytes=24 << 20),
        cost_estimate=pl.CostEstimate(
            flops=rows * size * width * cols // 4, bytes_accessed=1000, transcendentals=0
        ),
        name="terms",
    )(lax.axis_index("tensor").reshape(1), *operands)


def add_kernel(count, kept_ref, *refs):
    pieces, outs = refs[:count], refs[count:]
    rows, tall = pieces[0].shape[0], outs[0].shape[0]
    for index, piece in enumerate(pieces):
        row = index * rows
        total = kept_ref[row : row + rows].astype(f32) + piece[...].astype(f32)
        outs[row // tall][row % tall : row % tall + rows] = total.astype(bf16)


def add_pieces(kept, pieces, outs=1):
    rows, cols = kept.shape
    tile = max(n for n in range(128, 1025, 128) if cols % n == 0)

    def spec(tall):
        return pl.BlockSpec((tall, tile), lambda j: (0, j))

    return pl.pallas_call(
        functools.partial(add_kernel, len(pieces)),
        out_shape=[jax.ShapeDtypeStruct((rows // outs, cols), bf16)] * outs,
        grid=(cols // tile,),
        in_specs=[spec(rows)] + [spec(rows // len(pieces))] * len(pieces),
        out_specs=[spec(rows // outs)] * outs,
        compiler_params=pltpu.CompilerParams(vmem_limit_bytes=16 << 20),
        cost_estimate=pl.CostEstimate(flops=1000, bytes_accessed=1000, transcendentals=0),
        name="pair",
    )(kept, *pieces)


def gather_sums_kernel(places, *refs):
    quarters, sums, out_ref = refs[:4], refs[4:-1], refs[-1]
    rows = quarters[0].shape[0]
    for index, ref in enumerate(quarters):
        value = ref[...].astype(f32)
        for place, other in zip(places, sums):
            at = (index - place) * rows
            if 0 <= at < other.shape[0]:
                value = value + other[at : at + rows].astype(f32)
        out_ref[index * rows : (index + 1) * rows] = value.astype(bf16)


def gather_sums(quarters, sums):
    rows, cols = quarters[0].shape
    tile = max(n for n in range(128, 2049, 128) if cols % n == 0)
    places = [sum(value.shape[0] for value in sums[:k]) // rows for k in range(len(sums))]

    def spec(tall):
        return pl.BlockSpec((tall, tile), lambda j: (0, j))

    return pl.pallas_call(
        functools.partial(gather_sums_kernel, places),
        out_shape=jax.ShapeDtypeStruct((4 * rows, cols), bf16),
        grid=(cols // tile,),
        in_specs=[spec(rows)] * 4 + [spec(value.shape[0]) for value in sums],
        out_specs=spec(4 * rows),
        compiler_params=pltpu.CompilerParams(vmem_limit_bytes=24 << 20),
        cost_estimate=pl.CostEstimate(flops=1000, bytes_accessed=1000, transcendentals=0),
        name="sums",
    )(*quarters, *sums)


def example_gradients(acts_low, grads_low, local_ids, examples):
    onehot = (local_ids[:, None] == jnp.arange(examples, dtype=jnp.int32)[None, :]).astype(f32)
    counts = jnp.sum(onehot, axis=0)
    spread = (onehot[:, :, None] * acts_low[:, None, :]).reshape(onehot.shape[0], -1)
    outer_sum = lax.dot_general(
        spread,
        grads_low,
        (((0,), (0,)), ((), ())),
        precision=highest,
        preferred_element_type=f32,
    )
    basis_rank = acts_low.shape[1]
    outer_sum = outer_sum.reshape(examples, basis_rank * grads_low.shape[1]) / counts[:, None]
    return outer_sum.astype(bf16)


def gather_examples(example_grad, example_group):
    count = example_grad.shape[0]
    group_column = jnp.broadcast_to(example_group.astype(bf16)[:, None], (count, 128))
    held = jnp.concatenate([example_grad, group_column], axis=1)
    return [held] + [swap(held, step) for step in range(1, lax.axis_size("dp"))]


def order_examples(values):
    groups, place = lax.axis_size("dp"), lax.axis_index("dp")
    ordered = []
    for group in range(groups):
        value = values[0]
        for step in range(1, groups):
            value = jnp.where((place ^ group) == step, values[step], value)
        ordered.append(value)
    return jnp.concatenate(ordered, axis=0)


def fisher_and_groups(every, flat_width):
    row_count = flat_width // lax.axis_size("dp")
    col_count = flat_width // lax.axis_size("tensor")
    col_start = lax.axis_index("tensor") * col_count
    row_start = lax.axis_index("dp") * row_count
    every_group = every[:, flat_width].astype(jnp.int32)
    rows_part = lax.dynamic_slice_in_dim(every, row_start, row_count, 1)
    cols_part = lax.dynamic_slice_in_dim(every, col_start, col_count, 1)
    fisher = lax.dot_general(
        rows_part, cols_part, (((0,), (0,)), ((), ())), preferred_element_type=f32
    )
    member = (every_group[:, None] == jnp.arange(GROUPS, dtype=jnp.int32)[None, :]).astype(bf16)
    group_grad = lax.dot_general(
        member, cols_part, (((0,), (0,)), ((), ())), preferred_element_type=f32
    )
    return fisher, group_grad


def small_sums(hidden_acts, output_grad, input_basis, output_basis):
    acts_part = jnp.dot(hidden_acts, input_basis, preferred_element_type=f32)
    grads_part = lax.dot_general(
        output_grad,
        output_basis,
        (((0, 1, 2), (0, 1, 2)), ((), ())),
        preferred_element_type=f32,
    )
    return jnp.concatenate([acts_part, grads_part], axis=1)


def any_mesh(
    hidden_acts, output_grad, down_weight, input_basis, output_basis, token_example, example_group
):
    pieces = lax.all_to_all(output_grad, "dp", split_axis=1, concat_axis=3, tiled=True)
    columns = lax.all_gather(pieces, "tensor", axis=0, tiled=True)
    parts = small_sums(hidden_acts, output_grad, input_basis, output_basis)
    terms = lax.dot_general(
        columns, down_weight, (((0, 1, 2), (0, 1, 2)), ((), ())), preferred_element_type=f32
    )
    hidden_grad = lax.psum_scatter(terms.astype(bf16), "dp", scatter_dimension=0, tiled=True)
    acts_low, grads_low = jnp.split(lax.psum(parts, "tensor"), 2, axis=1)
    example_grad = example_gradients(
        acts_low, grads_low, token_example[0], example_group.shape[0]
    )
    every = order_examples(gather_examples(example_grad, example_group))
    fisher, group_grad = fisher_and_groups(every, example_grad.shape[1])
    return (hidden_grad, fisher, group_grad)


def line_of_four(
    hidden_acts, output_grad, down_weight, input_basis, output_basis, token_example, example_group
):
    tokens = hidden_acts.shape[0]
    rows = tokens // 2
    place = lax.axis_index("dp")
    turned = jnp.transpose(output_grad[0], (0, 2, 1))
    pieces = [lax.dynamic_index_in_dim(turned, place ^ k, 0, keepdims=False) for k in range(4)]
    far = []
    for half in range(2):
        cut = slice(half * rows, (half + 1) * rows)
        far.append(jnp.concatenate([swap(pieces[3][cut], 3), swap(pieces[2][cut], 2)]))
    beside, own = swap(pieces[1], 1), pieces[0]
    parts = small_sums(hidden_acts, output_grad, input_basis, output_basis)
    low = parts + across(parts, 1)

    blocks = spread_direct(after(far[0], parts))
    low = after(low, *blocks[1:])
    partner = across(low, 2)
    far[1] = after(far[1], *blocks[1:])
    later = spread_direct(far[1])

    def far_terms(chunk, at, pieces, *earlier):
        chunk = [after(chunk[0], *earlier)] + chunk[1:] if earlier else chunk
        outs = [rows // pieces] * pieces + [rows]
        *sent, kept = block_terms(chunk, down_weight, at, 2, outs)
        return sent, kept

    def pair_sum(sent, kept, *earlier, outs=1):
        pair = add_pieces(kept, [swap(after(term, *earlier), 1) for term in sent], outs)
        return pair[0], [swap(term, 2) for term in pair]

    sent0, kept0 = far_terms(blocks, 0, 2, beside)
    sent1, kept1 = far_terms(blocks, 1, 2, sent0[0])
    pair0, sum0 = pair_sum(sent0, kept0, partner, *later[1:], sent1[0])
    pair1, sum1 = pair_sum(sent1, kept1, *later[1:])

    beside = spread_first(after(beside, pair1))
    sent, kept = far_terms(later, 0, 2, pair0, pair1)
    pair2, sum2 = pair_sum(sent, kept, *beside[1:], outs=2)

    beside = spread_last(beside, pair2)
    own = spread_first(after(own, pair2))
    acts_low, grads_low = jnp.split(after(low, pair2, *sum0) + partner, 2, axis=1)
    example_grad = example_gradients(
        acts_low, grads_low, token_example[0], example_group.shape[0]
    )
    gathered = gather_examples(example_grad, example_group)
    sent, kept = far_terms(later, 1, 2, example_grad)
    pair3, sum3 = pair_sum(sent, kept, *own, *beside, outs=2)

    own = spread_last(own, pair3)
    beside = [after(beside[0], pair3, *sum1)] + beside[1:]
    near0 = block_terms(beside, down_weight, 0, 2, [rows // 2] * 4)
    near0 = [swap(after(term, sum2[0], *own[3:]), 1) for term in near0]
    adds0 = gather_sums(near0, sum0 + sum2)
    every = order_examples(after(gathered, near0[0]))
    fisher, group_grad = fisher_and_groups(every, example_grad.shape[1])
    beside = [after(beside[0], near0[0], fisher, group_grad)] + beside[1:]
    near1 = block_terms(beside, down_weight, 1, 2, [rows // 2] * 4)

    near1 = [swap(after(term, sum3[0]), 1) for term in near1]
    adds1 = gather_sums(near1, sum1)
    own = [after(own[0], adds1)] + own[1:]
    (result,) = block_terms(own, down_weight, 0, 2, [tokens], [adds0])
    own = [after(own[0], result)] + own[1:]
    (result,) = block_terms(own, down_weight, 1, 2, [tokens], [adds1] + sum3, result)
    return (result, fisher, group_grad)


def per_device(hidden_acts, output_grad, down_weight, *rest):
    fits = lax.axis_size("tensor") == 4 and lax.axis_size("dp") == 4
    fits = fits and down_weight.shape[2] % 128 == 0 and down_weight.shape[3] % 1024 == 0
    fits = fits and hidden_acts.shape[0] % 64 == 0
    return (line_of_four if fits else any_mesh)(hidden_acts, output_grad, down_weight, *rest)


def solution(mesh):
    return jax.shard_map(
        per_device,
        mesh=mesh,
        in_specs=(
            P(("parts", "dp"), "tensor"),
            P("tensor", None, None, ("parts", "dp")),
            P(None, "dp", None, "tensor"),
            P("tensor", None),
            P("tensor", None, None, None),
            P(("parts", "dp"), None),
            P(("parts", "dp")),
        ),
        out_specs=(
            P(("parts", "dp"), "tensor"),
            P(("parts", "dp"), "tensor"),
            P("parts", "tensor"),
        ),
        check_vma=False,
    )
```

```python
import functools

import jax
import jax.numpy as jnp
from jax import lax
from jax.experimental import pallas as pl
from jax.experimental.pallas import tpu as pltpu
from jax.sharding import PartitionSpec as P

GROUPS = 8

highest = lax.Precision.HIGHEST
f32, bf16 = jnp.float32, jnp.bfloat16


def swap(value, step):
    size = lax.axis_size("dp")
    return lax.ppermute(value, "dp", [(d, d ^ step) for d in range(size)])


def after(value, *earlier):
    return lax.optimization_barrier((value,) + earlier)[0]


def across(value, step, places=None):
    size = lax.axis_size("tensor")
    pairs = [(t, t ^ step) for t in range(size) if places is None or t in places]
    return lax.ppermute(value, "tensor", pairs)


def spread_first(block):
    second = across(block, 2)
    return [block, across(block, 1), second]


def spread_direct(block):
    second, third = across(block, 2), across(block, 3)
    return [block, across(block, 1), second, third]


def spread_last(blocks, *earlier):
    block, _, second = blocks
    middle = across(after(block, second, *earlier), 3, (1, 2))
    ends = across(after(second, *earlier), 1, (1, 2))
    return blocks + [middle, ends]


def terms_kernel(size, count, first, lows, place_ref, *refs):
    blocks, w_ref = refs[:count], refs[count]
    feats, held, sems, held_sems = refs[-4:]
    outs = refs[count + 1 : -4]
    add_refs = []
    if lows is not None:
        add_refs, outs = outs[: 1 + lows], outs[-1:]
    width, tile = feats.shape[1] // size, outs[0].shape[1]
    j, steps = pl.program_id(0), pl.num_programs(0)
    slots = held.shape[0]

    def put(value, source, slot):
        at = pl.ds(pl.multiple_of(source * width, width), width)
        return pltpu.make_async_copy(value, feats.at[:, at], sems.at[slot])

    def fetch(step):
        slot = lax.rem(step, slots)
        at = pl.ds(pl.multiple_of(first + step * tile, tile), tile)
        return pltpu.make_async_copy(w_ref.at[:, 0, :, at], held.at[slot], held_sems.at[slot])

    @pl.when(j == 0)
    def _():
        place = place_ref[0]
        straight = 3 if count == 5 else 4
        copies = [put(blocks[k], lax.bitwise_xor(place, k), k) for k in range(straight)]
        for copy in copies:
            copy.start()
        for step in range(slots):
            fetch(step).start()
        inside = jnp.logical_or(place == 1, place == 2)
        relayed = ((inside, 3), (jnp.logical_not(inside), 4)) if count == 5 else ()
        for chosen, k in relayed:

            @pl.when(chosen)
            def _():
                last = put(blocks[k], lax.bitwise_xor(place, 3), 3)
                last.start()
                last.wait()

        for copy in copies:
            copy.wait()

    fetch(j).wait()
    weight = held[lax.rem(j, slots)].reshape(size * width, tile)
    terms = jnp.dot(feats[...], weight, preferred_element_type=f32)
    if add_refs:
        terms = terms + add_refs[0][...].astype(f32)
    row = 0
    for low_ref in reversed(add_refs[1:]):
        row += low_ref.shape[0]
        cut = slice(feats.shape[0] - row, feats.shape[0] - row + low_ref.shape[0])
        outs[0][cut] = (terms[cut] + low_ref[...].astype(f32)).astype(bf16)
    if add_refs:
        outs[0][: feats.shape[0] - row] = terms[: feats.shape[0] - row].astype(bf16)
    else:
        for out_ref in outs:
            out_ref[...] = terms[row : row + out_ref.shape[0]].astype(bf16)
            row += out_ref.shape[0]

    @pl.when(j + slots < steps)
    def _():
        fetch(j + slots).start()


def block_terms(blocks, down_weight, part, parts, outs, adds=None, into=None):
    size, _, width, every = down_weight.shape
    rows, cols = sum(outs), every // parts
    tile = max(n for n in range(128, 513, 128) if cols % n == 0)
    slots = min(4, cols // tile)

    def spec(tall, first=0):
        return pl.BlockSpec((tall, tile), lambda j, place: (0, first + j))

    operands = [*blocks, down_weight]
    in_specs = [pl.BlockSpec(memory_space=pltpu.HBM)] * len(operands)
    out_shape = [pltpu.HBM((tall, cols), bf16) for tall in outs]
    out_specs = [spec(tall) for tall in outs]
    aliases = {}
    if adds is not None:
        operands += adds
        in_specs += [spec(value.shape[0]) for value in adds]
        out_shape = [pltpu.HBM((rows, every), bf16)]
        out_specs = [spec(rows, part * (cols // tile))]
    if into is not None:
        operands.append(into)
        in_specs.append(pl.BlockSpec(memory_space=pltpu.HBM))
        aliases = {len(operands): 0}
    return pl.pallas_call(
        functools.partial(
            terms_kernel,
            size,
            len(blocks),
            part * cols,
            None if adds is None else len(adds) - 1,
        ),
        out_shape=out_shape,
        grid_spec=pltpu.PrefetchScalarGridSpec(
            num_scalar_prefetch=1,
            grid=(cols // tile,),
            in_specs=in_specs,
            out_specs=out_specs,
            scratch_shapes=[
                pltpu.VMEM((rows, size * width), bf16),
                pltpu.VMEM((slots, size, width, tile), bf16),
                pltpu.SemaphoreType.DMA((size,)),
                pltpu.SemaphoreType.DMA((slots,)),
            ],
        ),
        input_output_aliases=aliases,
        compiler_params=pltpu.CompilerParams(vmem_limit_bytes=24 << 20),
        cost_estimate=pl.CostEstimate(
            flops=rows * size * width * cols // 4, bytes_accessed=1000, transcendentals=0
        ),
        name="terms",
    )(lax.axis_index("tensor").reshape(1), *operands)


def add_kernel(count, kept_ref, *refs):
    pieces, outs = refs[:count], refs[count:]
    rows, tall = pieces[0].shape[0], outs[0].shape[0]
    for index, piece in enumerate(pieces):
        row = index * rows
        total = kept_ref[row : row + rows].astype(f32) + piece[...].astype(f32)
        outs[row // tall][row % tall : row % tall + rows] = total.astype(bf16)


def add_pieces(kept, pieces, outs=1):
    rows, cols = kept.shape
    tile = max(n for n in range(128, 1025, 128) if cols % n == 0)

    def spec(tall):
        return pl.BlockSpec((tall, tile), lambda j: (0, j))

    return pl.pallas_call(
        functools.partial(add_kernel, len(pieces)),
        out_shape=[jax.ShapeDtypeStruct((rows // outs, cols), bf16)] * outs,
        grid=(cols // tile,),
        in_specs=[spec(rows)] + [spec(rows // len(pieces))] * len(pieces),
        out_specs=[spec(rows // outs)] * outs,
        compiler_params=pltpu.CompilerParams(vmem_limit_bytes=16 << 20),
        cost_estimate=pl.CostEstimate(flops=1000, bytes_accessed=1000, transcendentals=0),
        name="pair",
    )(kept, *pieces)


def gather_sums_kernel(*refs):
    quarters, sums, out_ref = refs[:4], refs[4:-1], refs[-1]
    rows = quarters[0].shape[0]
    for index, ref in enumerate(quarters):
        value = ref[...]
        if index // 2 < len(sums):
            at = (index % 2) * rows
            other = sums[index // 2][at : at + rows]
            value = (value.astype(f32) + other.astype(f32)).astype(bf16)
        out_ref[index * rows : (index + 1) * rows] = value


def gather_sums(quarters, sums):
    rows, cols = quarters[0].shape
    tile = max(n for n in range(128, 2049, 128) if cols % n == 0)

    def spec(tall):
        return pl.BlockSpec((tall, tile), lambda j: (0, j))

    return pl.pallas_call(
        gather_sums_kernel,
        out_shape=jax.ShapeDtypeStruct((4 * rows, cols), bf16),
        grid=(cols // tile,),
        in_specs=[spec(rows)] * 4 + [spec(2 * rows)] * len(sums),
        out_specs=spec(4 * rows),
        compiler_params=pltpu.CompilerParams(vmem_limit_bytes=24 << 20),
        cost_estimate=pl.CostEstimate(flops=1000, bytes_accessed=1000, transcendentals=0),
        name="sums",
    )(*quarters, *sums)


def example_gradients(acts_low, grads_low, local_ids, examples):
    onehot = (local_ids[:, None] == jnp.arange(examples, dtype=jnp.int32)[None, :]).astype(f32)
    counts = jnp.sum(onehot, axis=0)
    spread = (onehot[:, :, None] * acts_low[:, None, :]).reshape(onehot.shape[0], -1)
    outer_sum = lax.dot_general(
        spread,
        grads_low,
        (((0,), (0,)), ((), ())),
        precision=highest,
        preferred_element_type=f32,
    )
    basis_rank = acts_low.shape[1]
    outer_sum = outer_sum.reshape(examples, basis_rank * grads_low.shape[1]) / counts[:, None]
    return outer_sum.astype(bf16)


def gather_examples(example_grad, example_group):
    count = example_grad.shape[0]
    group_column = jnp.broadcast_to(example_group.astype(bf16)[:, None], (count, 128))
    held = jnp.concatenate([example_grad, group_column], axis=1)
    return [held] + [swap(held, step) for step in range(1, lax.axis_size("dp"))]


def order_examples(values):
    groups, place = lax.axis_size("dp"), lax.axis_index("dp")
    ordered = []
    for group in range(groups):
        value = values[0]
        for step in range(1, groups):
            value = jnp.where((place ^ group) == step, values[step], value)
        ordered.append(value)
    return jnp.concatenate(ordered, axis=0)


def fisher_and_groups(every, flat_width):
    row_count = flat_width // lax.axis_size("dp")
    col_count = flat_width // lax.axis_size("tensor")
    col_start = lax.axis_index("tensor") * col_count
    row_start = lax.axis_index("dp") * row_count
    every_group = every[:, flat_width].astype(jnp.int32)
    rows_part = lax.dynamic_slice_in_dim(every, row_start, row_count, 1)
    cols_part = lax.dynamic_slice_in_dim(every, col_start, col_count, 1)
    fisher = lax.dot_general(
        rows_part, cols_part, (((0,), (0,)), ((), ())), preferred_element_type=f32
    )
    member = (every_group[:, None] == jnp.arange(GROUPS, dtype=jnp.int32)[None, :]).astype(bf16)
    group_grad = lax.dot_general(
        member, cols_part, (((0,), (0,)), ((), ())), preferred_element_type=f32
    )
    return fisher, group_grad


def small_sums(hidden_acts, output_grad, input_basis, output_basis):
    acts_part = jnp.dot(hidden_acts, input_basis, preferred_element_type=f32)
    grads_part = lax.dot_general(
        output_grad,
        output_basis,
        (((0, 1, 2), (0, 1, 2)), ((), ())),
        preferred_element_type=f32,
    )
    return jnp.concatenate([acts_part, grads_part], axis=1)


def any_mesh(
    hidden_acts, output_grad, down_weight, input_basis, output_basis, token_example, example_group
):
    pieces = lax.all_to_all(output_grad, "dp", split_axis=1, concat_axis=3, tiled=True)
    columns = lax.all_gather(pieces, "tensor", axis=0, tiled=True)
    parts = small_sums(hidden_acts, output_grad, input_basis, output_basis)
    terms = lax.dot_general(
        columns, down_weight, (((0, 1, 2), (0, 1, 2)), ((), ())), preferred_element_type=f32
    )
    hidden_grad = lax.psum_scatter(terms.astype(bf16), "dp", scatter_dimension=0, tiled=True)
    acts_low, grads_low = jnp.split(lax.psum(parts, "tensor"), 2, axis=1)
    example_grad = example_gradients(
        acts_low, grads_low, token_example[0], example_group.shape[0]
    )
    every = order_examples(gather_examples(example_grad, example_group))
    fisher, group_grad = fisher_and_groups(every, example_grad.shape[1])
    return (hidden_grad, fisher, group_grad)


def line_of_four(
    hidden_acts, output_grad, down_weight, input_basis, output_basis, token_example, example_group
):
    tokens = hidden_acts.shape[0]
    rows = tokens // 2
    place = lax.axis_index("dp")
    turned = jnp.transpose(output_grad[0], (0, 2, 1))
    pieces = [lax.dynamic_index_in_dim(turned, place ^ k, 0, keepdims=False) for k in range(4)]
    far = []
    for half in range(2):
        cut = slice(half * rows, (half + 1) * rows)
        far.append(jnp.concatenate([swap(pieces[3][cut], 3), swap(pieces[2][cut], 2)]))
    beside, own = swap(pieces[1], 1), pieces[0]
    parts = small_sums(hidden_acts, output_grad, input_basis, output_basis)
    low = parts + across(parts, 1)

    blocks = spread_direct(after(far[0], parts))
    low = after(low, *blocks[1:])
    partner = across(low, 2)
    far[1] = after(far[1], *blocks[1:])
    later_first = across(far[1], 1)

    def far_terms(chunk, at, pieces, *earlier):
        chunk = [after(chunk[0], *earlier)] + chunk[1:] if earlier else chunk
        outs = [rows // pieces] * pieces + [rows]
        *sent, kept = block_terms(chunk, down_weight, at, 2, outs)
        return sent, kept

    def pair_sum(sent, kept, *earlier, outs=1):
        pair = add_pieces(kept, [swap(after(term, *earlier), 1) for term in sent], outs)
        return pair[0], [swap(term, 2) for term in pair]

    sent, kept = far_terms(blocks, 0, 2, beside)
    pair0, sum0 = pair_sum(sent, kept, partner, later_first)

    later = after(far[1], pair0)
    later = [far[1], later_first, across(later, 2), across(later, 3)]
    sent, kept = far_terms(blocks, 1, 2, pair0)
    pair1, sum1 = pair_sum(sent, kept, *later[2:])

    beside = spread_first(after(beside, *later[2:]))
    sent, kept = far_terms(later, 0, 2, pair1, *sum0)
    pair2, sum2 = pair_sum(sent, kept, *beside[1:])

    beside = spread_last(beside, pair2)
    own = after(own, pair2)
    own_first = across(own, 1)
    acts_low, grads_low = jnp.split(after(low, pair2, *sum1) + partner, 2, axis=1)
    example_grad = example_gradients(
        acts_low, grads_low, token_example[0], example_group.shape[0]
    )
    gathered = gather_examples(example_grad, example_group)
    sent, kept = far_terms(later, 1, 4, example_grad)
    own = [own, own_first, across(own, 2)]
    pair3, sum3 = pair_sum(sent, after(kept, own[2]), own_first, *beside, outs=2)

    own = spread_last(own, pair3)
    beside = [after(beside[0], pair3, *sum2)] + beside[1:]
    near0 = block_terms(beside, down_weight, 0, 2, [rows // 2] * 4)
    near0 = [swap(after(term, sum3[0]), 1) for term in near0]
    beside = [after(beside[0], *near0[:1])] + beside[1:]
    near1 = block_terms(beside, down_weight, 1, 2, [rows // 2] * 4)
    every = order_examples(after(gathered, near1[0]))
    fisher, group_grad = fisher_and_groups(every, example_grad.shape[1])
    own = [after(own[0], near1[0])] + own[1:]
    near1 = [swap(after(term, sum3[1], *own[3:]), 1) for term in near1]
    adds = [gather_sums(near0, sum0 + sum2)]
    (result,) = block_terms(own, down_weight, 0, 2, [tokens], adds)
    adds = [gather_sums(near1, sum1)] + sum3
    own = [after(own[0], fisher, group_grad, result)] + own[1:]
    (result,) = block_terms(own, down_weight, 1, 2, [tokens], adds, result)
    return (result, fisher, group_grad)


def per_device(hidden_acts, output_grad, down_weight, *rest):
    fits = lax.axis_size("tensor") == 4 and lax.axis_size("dp") == 4
    fits = fits and down_weight.shape[2] % 128 == 0 and down_weight.shape[3] % 1024 == 0
    fits = fits and hidden_acts.shape[0] % 64 == 0
    return (line_of_four if fits else any_mesh)(hidden_acts, output_grad, down_weight, *rest)


def solution(mesh):
    return jax.shard_map(
        per_device,
        mesh=mesh,
        in_specs=(
            P(("parts", "dp"), "tensor"),
            P("tensor", None, None, ("parts", "dp")),
            P(None, "dp", None, "tensor"),
            P("tensor", None),
            P("tensor", None, None, None),
            P(("parts", "dp"), None),
            P(("parts", "dp")),
        ),
        out_specs=(
            P(("parts", "dp"), "tensor"),
            P(("parts", "dp"), "tensor"),
            P("parts", "tensor"),
        ),
        check_vma=False,
    )
```

```python
import functools

import jax
import jax.numpy as jnp
from jax import lax
from jax.experimental import pallas as pl
from jax.experimental.pallas import tpu as pltpu
from jax.sharding import PartitionSpec as P

GROUPS = 8

highest = lax.Precision.HIGHEST
f32, bf16 = jnp.float32, jnp.bfloat16


def swap(value, step):
    size = lax.axis_size("dp")
    return lax.ppermute(value, "dp", [(d, d ^ step) for d in range(size)])


def after(value, *earlier):
    return lax.optimization_barrier((value,) + earlier)[0]


def across(value, step, places=None):
    size = lax.axis_size("tensor")
    pairs = [(t, t ^ step) for t in range(size) if places is None or t in places]
    return lax.ppermute(value, "tensor", pairs)


def spread_first(block):
    second = across(block, 2)
    return [block, across(block, 1), second]


def spread_direct(block):
    second, third = across(block, 2), across(block, 3)
    return [block, across(block, 1), second, third]


def spread_last(blocks, *earlier):
    block, _, second = blocks
    middle = across(after(block, second, *earlier), 3, (1, 2))
    ends = across(after(second, *earlier), 1, (1, 2))
    return blocks + [middle, ends]


def terms_kernel(size, count, first, lows, place_ref, *refs):
    blocks, w_ref = refs[:count], refs[count]
    feats, held, sems, held_sems = refs[-4:]
    outs = refs[count + 1 : -4]
    add_refs = []
    if lows is not None:
        add_refs, outs = outs[: 1 + lows], outs[-1:]
    width, tile = feats.shape[1] // size, outs[0].shape[1]
    j, steps = pl.program_id(0), pl.num_programs(0)
    slots = held.shape[0]

    def put(value, source, slot):
        at = pl.ds(pl.multiple_of(source * width, width), width)
        return pltpu.make_async_copy(value, feats.at[:, at], sems.at[slot])

    def fetch(step):
        slot = lax.rem(step, slots)
        at = pl.ds(pl.multiple_of(first + step * tile, tile), tile)
        return pltpu.make_async_copy(w_ref.at[:, 0, :, at], held.at[slot], held_sems.at[slot])

    @pl.when(j == 0)
    def _():
        place = place_ref[0]
        straight = 3 if count == 5 else 4
        copies = [put(blocks[k], lax.bitwise_xor(place, k), k) for k in range(straight)]
        for copy in copies:
            copy.start()
        for step in range(slots):
            fetch(step).start()
        inside = jnp.logical_or(place == 1, place == 2)
        relayed = ((inside, 3), (jnp.logical_not(inside), 4)) if count == 5 else ()
        for chosen, k in relayed:

            @pl.when(chosen)
            def _():
                last = put(blocks[k], lax.bitwise_xor(place, 3), 3)
                last.start()
                last.wait()

        for copy in copies:
            copy.wait()

    fetch(j).wait()
    weight = held[lax.rem(j, slots)].reshape(size * width, tile)
    terms = jnp.dot(feats[...], weight, preferred_element_type=f32)
    if add_refs:
        terms = terms + add_refs[0][...].astype(f32)
    row = 0
    for low_ref in reversed(add_refs[1:]):
        row += low_ref.shape[0]
        cut = slice(feats.shape[0] - row, feats.shape[0] - row + low_ref.shape[0])
        outs[0][cut] = (terms[cut] + low_ref[...].astype(f32)).astype(bf16)
    if add_refs:
        outs[0][: feats.shape[0] - row] = terms[: feats.shape[0] - row].astype(bf16)
    else:
        for out_ref in outs:
            out_ref[...] = terms[row : row + out_ref.shape[0]].astype(bf16)
            row += out_ref.shape[0]

    @pl.when(j + slots < steps)
    def _():
        fetch(j + slots).start()


def block_terms(blocks, down_weight, part, parts, outs, adds=None, into=None):
    size, _, width, every = down_weight.shape
    rows, cols = sum(outs), every // parts
    tile = max(n for n in range(128, 513, 128) if cols % n == 0)
    slots = min(4, cols // tile)

    def spec(tall, first=0):
        return pl.BlockSpec((tall, tile), lambda j, place: (0, first + j))

    operands = [*blocks, down_weight]
    in_specs = [pl.BlockSpec(memory_space=pltpu.HBM)] * len(operands)
    out_shape = [jax.ShapeDtypeStruct((tall, cols), bf16) for tall in outs]
    out_specs = [spec(tall) for tall in outs]
    aliases = {}
    if adds is not None:
        operands += adds
        in_specs += [spec(value.shape[0]) for value in adds]
        out_shape = [jax.ShapeDtypeStruct((rows, every), bf16)]
        out_specs = [spec(rows, part * (cols // tile))]
    if into is not None:
        operands.append(into)
        in_specs.append(pl.BlockSpec(memory_space=pltpu.HBM))
        aliases = {len(operands): 0}
    return pl.pallas_call(
        functools.partial(
            terms_kernel,
            size,
            len(blocks),
            part * cols,
            None if adds is None else len(adds) - 1,
        ),
        out_shape=out_shape,
        grid_spec=pltpu.PrefetchScalarGridSpec(
            num_scalar_prefetch=1,
            grid=(cols // tile,),
            in_specs=in_specs,
            out_specs=out_specs,
            scratch_shapes=[
                pltpu.VMEM((rows, size * width), bf16),
                pltpu.VMEM((slots, size, width, tile), bf16),
                pltpu.SemaphoreType.DMA((size,)),
                pltpu.SemaphoreType.DMA((slots,)),
            ],
        ),
        input_output_aliases=aliases,
        compiler_params=pltpu.CompilerParams(vmem_limit_bytes=24 << 20),
        cost_estimate=pl.CostEstimate(
            flops=rows * size * width * cols // 4, bytes_accessed=1000, transcendentals=0
        ),
        name="terms",
    )(lax.axis_index("tensor").reshape(1), *operands)


def add_kernel(count, kept_ref, *refs):
    pieces, outs = refs[:count], refs[count:]
    rows, tall = pieces[0].shape[0], outs[0].shape[0]
    for index, piece in enumerate(pieces):
        row = index * rows
        total = kept_ref[row : row + rows].astype(f32) + piece[...].astype(f32)
        outs[row // tall][row % tall : row % tall + rows] = total.astype(bf16)


def add_pieces(kept, pieces, outs=1):
    rows, cols = kept.shape
    tile = max(n for n in range(128, 1025, 128) if cols % n == 0)

    def spec(tall):
        return pl.BlockSpec((tall, tile), lambda j: (0, j))

    return pl.pallas_call(
        functools.partial(add_kernel, len(pieces)),
        out_shape=[jax.ShapeDtypeStruct((rows // outs, cols), bf16)] * outs,
        grid=(cols // tile,),
        in_specs=[spec(rows)] + [spec(rows // len(pieces))] * len(pieces),
        out_specs=[spec(rows // outs)] * outs,
        compiler_params=pltpu.CompilerParams(vmem_limit_bytes=16 << 20),
        cost_estimate=pl.CostEstimate(flops=1000, bytes_accessed=1000, transcendentals=0),
        name="pair",
    )(kept, *pieces)


def gather_sums_kernel(*refs):
    quarters, sums, out_ref = refs[:4], refs[4:-1], refs[-1]
    rows = quarters[0].shape[0]
    for index, ref in enumerate(quarters):
        value = ref[...]
        if index // 2 < len(sums):
            at = (index % 2) * rows
            other = sums[index // 2][at : at + rows]
            value = (value.astype(f32) + other.astype(f32)).astype(bf16)
        out_ref[index * rows : (index + 1) * rows] = value


def gather_sums(quarters, sums):
    rows, cols = quarters[0].shape
    tile = max(n for n in range(128, 2049, 128) if cols % n == 0)

    def spec(tall):
        return pl.BlockSpec((tall, tile), lambda j: (0, j))

    return pl.pallas_call(
        gather_sums_kernel,
        out_shape=jax.ShapeDtypeStruct((4 * rows, cols), bf16),
        grid=(cols // tile,),
        in_specs=[spec(rows)] * 4 + [spec(2 * rows)] * len(sums),
        out_specs=spec(4 * rows),
        compiler_params=pltpu.CompilerParams(vmem_limit_bytes=24 << 20),
        cost_estimate=pl.CostEstimate(flops=1000, bytes_accessed=1000, transcendentals=0),
        name="sums",
    )(*quarters, *sums)


def example_gradients(acts_low, grads_low, local_ids, examples):
    onehot = (local_ids[:, None] == jnp.arange(examples, dtype=jnp.int32)[None, :]).astype(f32)
    counts = jnp.sum(onehot, axis=0)
    spread = (onehot[:, :, None] * acts_low[:, None, :]).reshape(onehot.shape[0], -1)
    outer_sum = lax.dot_general(
        spread,
        grads_low,
        (((0,), (0,)), ((), ())),
        precision=highest,
        preferred_element_type=f32,
    )
    basis_rank = acts_low.shape[1]
    outer_sum = outer_sum.reshape(examples, basis_rank * grads_low.shape[1]) / counts[:, None]
    return outer_sum.astype(bf16)


def gather_examples(example_grad, example_group):
    count = example_grad.shape[0]
    group_column = jnp.broadcast_to(example_group.astype(bf16)[:, None], (count, 128))
    held = jnp.concatenate([example_grad, group_column], axis=1)
    return [held] + [swap(held, step) for step in range(1, lax.axis_size("dp"))]


def order_examples(values):
    groups, place = lax.axis_size("dp"), lax.axis_index("dp")
    ordered = []
    for group in range(groups):
        value = values[0]
        for step in range(1, groups):
            value = jnp.where((place ^ group) == step, values[step], value)
        ordered.append(value)
    return jnp.concatenate(ordered, axis=0)


def fisher_and_groups(every, flat_width):
    row_count = flat_width // lax.axis_size("dp")
    col_count = flat_width // lax.axis_size("tensor")
    col_start = lax.axis_index("tensor") * col_count
    row_start = lax.axis_index("dp") * row_count
    every_group = every[:, flat_width].astype(jnp.int32)
    rows_part = lax.dynamic_slice_in_dim(every, row_start, row_count, 1)
    cols_part = lax.dynamic_slice_in_dim(every, col_start, col_count, 1)
    fisher = lax.dot_general(
        rows_part, cols_part, (((0,), (0,)), ((), ())), preferred_element_type=f32
    )
    member = (every_group[:, None] == jnp.arange(GROUPS, dtype=jnp.int32)[None, :]).astype(bf16)
    group_grad = lax.dot_general(
        member, cols_part, (((0,), (0,)), ((), ())), preferred_element_type=f32
    )
    return fisher, group_grad


def small_sums(hidden_acts, output_grad, input_basis, output_basis):
    acts_part = jnp.dot(hidden_acts, input_basis, preferred_element_type=f32)
    grads_part = lax.dot_general(
        output_grad,
        output_basis,
        (((0, 1, 2), (0, 1, 2)), ((), ())),
        preferred_element_type=f32,
    )
    return jnp.concatenate([acts_part, grads_part], axis=1)


def any_mesh(
    hidden_acts, output_grad, down_weight, input_basis, output_basis, token_example, example_group
):
    pieces = lax.all_to_all(output_grad, "dp", split_axis=1, concat_axis=3, tiled=True)
    columns = lax.all_gather(pieces, "tensor", axis=0, tiled=True)
    parts = small_sums(hidden_acts, output_grad, input_basis, output_basis)
    terms = lax.dot_general(
        columns, down_weight, (((0, 1, 2), (0, 1, 2)), ((), ())), preferred_element_type=f32
    )
    hidden_grad = lax.psum_scatter(terms.astype(bf16), "dp", scatter_dimension=0, tiled=True)
    acts_low, grads_low = jnp.split(lax.psum(parts, "tensor"), 2, axis=1)
    example_grad = example_gradients(
        acts_low, grads_low, token_example[0], example_group.shape[0]
    )
    every = order_examples(gather_examples(example_grad, example_group))
    fisher, group_grad = fisher_and_groups(every, example_grad.shape[1])
    return (hidden_grad, fisher, group_grad)


def line_of_four(
    hidden_acts, output_grad, down_weight, input_basis, output_basis, token_example, example_group
):
    tokens = hidden_acts.shape[0]
    rows = tokens // 2
    place = lax.axis_index("dp")
    turned = jnp.transpose(output_grad[0], (0, 2, 1))
    pieces = [lax.dynamic_index_in_dim(turned, place ^ k, 0, keepdims=False) for k in range(4)]
    far = []
    for half in range(2):
        cut = slice(half * rows, (half + 1) * rows)
        far.append(jnp.concatenate([swap(pieces[3][cut], 3), swap(pieces[2][cut], 2)]))
    beside, own = swap(pieces[1], 1), pieces[0]
    parts = small_sums(hidden_acts, output_grad, input_basis, output_basis)
    low = parts + across(parts, 1)

    blocks = spread_direct(after(far[0], parts))
    low = after(low, *blocks[1:])
    partner = across(low, 2)
    far[1] = after(far[1], *blocks[1:])
    later_first = across(far[1], 1)

    def far_terms(chunk, at, pieces, *earlier):
        chunk = [after(chunk[0], *earlier)] + chunk[1:] if earlier else chunk
        outs = [rows // pieces] * pieces + [rows]
        *sent, kept = block_terms(chunk, down_weight, at, 2, outs)
        return sent, kept

    def pair_sum(sent, kept, *earlier, outs=1):
        pair = add_pieces(kept, [swap(after(term, *earlier), 1) for term in sent], outs)
        return pair[0], [swap(term, 2) for term in pair]

    sent, kept = far_terms(blocks, 0, 2, beside)
    pair0, sum0 = pair_sum(sent, kept, partner, later_first)

    later = after(far[1], pair0)
    later = [far[1], later_first, across(later, 2), across(later, 3)]
    sent, kept = far_terms(blocks, 1, 2, pair0)
    acts_low, grads_low = jnp.split(after(low, sent[0]) + partner, 2, axis=1)
    example_grad = example_gradients(
        acts_low, grads_low, token_example[0], example_group.shape[0]
    )
    pair1, sum1 = pair_sum(sent, kept, *later[2:], example_grad)

    beside = spread_first(after(beside, pair1))
    sent, kept = far_terms(later, 0, 2, pair1, *sum0)
    pair2, sum2 = pair_sum(sent, kept, *beside[1:])

    beside = spread_last(beside, pair2)
    own = after(own, pair2)
    own_first = across(own, 1)
    gathered = gather_examples(after(example_grad, pair1), example_group)
    sent, kept = far_terms(later, 1, 4, pair2, *sum1, *gathered)
    every = order_examples(after(gathered, sent[0]))
    fisher, group_grad = fisher_and_groups(every, example_grad.shape[1])
    own = [own, own_first, across(own, 2)]
    pair3, sum3 = pair_sum(
        sent, after(kept, own[2]), own_first, *beside, fisher, group_grad, outs=2
    )

    own = spread_last(own, pair3)
    beside = [after(beside[0], pair3, *sum2)] + beside[1:]
    near0 = block_terms(beside, down_weight, 0, 2, [rows // 2] * 4)
    near0 = [swap(after(term, sum3[0], *own[3:]), 1) for term in near0]
    beside = [after(beside[0], *near0[:1])] + beside[1:]
    near1 = block_terms(beside, down_weight, 1, 2, [rows // 2] * 4)
    own = [after(own[0], near1[0])] + own[1:]
    near1 = [swap(after(term, sum3[1], *own[3:]), 1) for term in near1]
    adds = [gather_sums(near0, sum0 + sum2)]
    (result,) = block_terms(own, down_weight, 0, 2, [tokens], adds)
    adds = [gather_sums(near1, sum1)] + sum3
    own = [after(own[0], result)] + own[1:]
    (result,) = block_terms(own, down_weight, 1, 2, [tokens], adds, result)
    return (result, fisher, group_grad)


def per_device(hidden_acts, output_grad, down_weight, *rest):
    fits = lax.axis_size("tensor") == 4 and lax.axis_size("dp") == 4
    fits = fits and down_weight.shape[2] % 128 == 0 and down_weight.shape[3] % 1024 == 0
    fits = fits and hidden_acts.shape[0] % 64 == 0
    return (line_of_four if fits else any_mesh)(hidden_acts, output_grad, down_weight, *rest)


def solution(mesh):
    return jax.shard_map(
        per_device,
        mesh=mesh,
        in_specs=(
            P(("parts", "dp"), "tensor"),
            P("tensor", None, None, ("parts", "dp")),
            P(None, "dp", None, "tensor"),
            P("tensor", None),
            P("tensor", None, None, None),
            P(("parts", "dp"), None),
            P(("parts", "dp")),
        ),
        out_specs=(
            P(("parts", "dp"), "tensor"),
            P(("parts", "dp"), "tensor"),
            P("parts", "tensor"),
        ),
        check_vma=False,
    )
```

```python
import functools

import jax
import jax.numpy as jnp
from jax import lax
from jax.experimental import pallas as pl
from jax.experimental.pallas import tpu as pltpu
from jax.sharding import PartitionSpec as P

GROUPS = 8

highest = lax.Precision.HIGHEST
f32, bf16 = jnp.float32, jnp.bfloat16


def swap(value, step):
    size = lax.axis_size("dp")
    return lax.ppermute(value, "dp", [(d, d ^ step) for d in range(size)])


def after(value, *earlier):
    return lax.optimization_barrier((value,) + earlier)[0]


def across(value, step, places=None):
    size = lax.axis_size("tensor")
    pairs = [(t, t ^ step) for t in range(size) if places is None or t in places]
    return lax.ppermute(value, "tensor", pairs)


def spread_first(block):
    second = across(block, 2)
    return [block, across(block, 1), second]


def spread_direct(block):
    second, third = across(block, 2), across(block, 3)
    return [block, across(block, 1), second, third]


def spread_last(blocks, *earlier):
    block, _, second = blocks
    middle = across(after(block, second, *earlier), 3, (1, 2))
    ends = across(after(second, *earlier), 1, (1, 2))
    return blocks + [middle, ends]


def terms_kernel(size, count, first, lows, place_ref, *refs):
    blocks, w_ref = refs[:count], refs[count]
    feats, held, sems, held_sems = refs[-4:]
    outs = refs[count + 1 : -4]
    add_refs = []
    if lows is not None:
        add_refs, outs = outs[: 1 + lows], outs[-1:]
    width, tile = feats.shape[1] // size, outs[0].shape[1]
    j, steps = pl.program_id(0), pl.num_programs(0)
    slots = held.shape[0]

    def put(value, source, slot):
        at = pl.ds(pl.multiple_of(source * width, width), width)
        return pltpu.make_async_copy(value, feats.at[:, at], sems.at[slot])

    def fetch(step):
        slot = lax.rem(step, slots)
        at = pl.ds(pl.multiple_of(first + step * tile, tile), tile)
        return pltpu.make_async_copy(w_ref.at[:, 0, :, at], held.at[slot], held_sems.at[slot])

    @pl.when(j == 0)
    def _():
        place = place_ref[0]
        straight = 3 if count == 5 else 4
        copies = [put(blocks[k], lax.bitwise_xor(place, k), k) for k in range(straight)]
        for copy in copies:
            copy.start()
        for step in range(slots):
            fetch(step).start()
        inside = jnp.logical_or(place == 1, place == 2)
        relayed = ((inside, 3), (jnp.logical_not(inside), 4)) if count == 5 else ()
        for chosen, k in relayed:

            @pl.when(chosen)
            def _():
                last = put(blocks[k], lax.bitwise_xor(place, 3), 3)
                last.start()
                last.wait()

        for copy in copies:
            copy.wait()

    fetch(j).wait()
    weight = held[lax.rem(j, slots)].reshape(size * width, tile)
    terms = jnp.dot(feats[...], weight, preferred_element_type=f32)
    if add_refs:
        terms = terms + add_refs[0][...].astype(f32)
    row = 0
    for low_ref in reversed(add_refs[1:]):
        row += low_ref.shape[0]
        cut = slice(feats.shape[0] - row, feats.shape[0] - row + low_ref.shape[0])
        outs[0][cut] = (terms[cut] + low_ref[...].astype(f32)).astype(bf16)
    if add_refs:
        outs[0][: feats.shape[0] - row] = terms[: feats.shape[0] - row].astype(bf16)
    else:
        for out_ref in outs:
            out_ref[...] = terms[row : row + out_ref.shape[0]].astype(bf16)
            row += out_ref.shape[0]

    @pl.when(j + slots < steps)
    def _():
        fetch(j + slots).start()


def block_terms(blocks, down_weight, part, parts, outs, adds=None, into=None):
    size, _, width, every = down_weight.shape
    rows, cols = sum(outs), every // parts
    tile = max(n for n in range(128, 513, 128) if cols % n == 0)
    slots = min(4, cols // tile)

    def spec(tall, first=0):
        return pl.BlockSpec((tall, tile), lambda j, place: (0, first + j))

    operands = [*blocks, down_weight]
    in_specs = [pl.BlockSpec(memory_space=pltpu.HBM)] * len(operands)
    out_shape = [jax.ShapeDtypeStruct((tall, cols), bf16) for tall in outs]
    out_specs = [spec(tall) for tall in outs]
    aliases = {}
    if adds is not None:
        operands += adds
        in_specs += [spec(value.shape[0]) for value in adds]
        out_shape = [jax.ShapeDtypeStruct((rows, every), bf16)]
        out_specs = [spec(rows, part * (cols // tile))]
    if into is not None:
        operands.append(into)
        in_specs.append(pl.BlockSpec(memory_space=pltpu.HBM))
        aliases = {len(operands): 0}
    return pl.pallas_call(
        functools.partial(
            terms_kernel,
            size,
            len(blocks),
            part * cols,
            None if adds is None else len(adds) - 1,
        ),
        out_shape=out_shape,
        grid_spec=pltpu.PrefetchScalarGridSpec(
            num_scalar_prefetch=1,
            grid=(cols // tile,),
            in_specs=in_specs,
            out_specs=out_specs,
            scratch_shapes=[
                pltpu.VMEM((rows, size * width), bf16),
                pltpu.VMEM((slots, size, width, tile), bf16),
                pltpu.SemaphoreType.DMA((size,)),
                pltpu.SemaphoreType.DMA((slots,)),
            ],
        ),
        input_output_aliases=aliases,
        compiler_params=pltpu.CompilerParams(vmem_limit_bytes=24 << 20),
        cost_estimate=pl.CostEstimate(
            flops=rows * size * width * cols // 4, bytes_accessed=1000, transcendentals=0
        ),
        name="terms",
    )(lax.axis_index("tensor").reshape(1), *operands)


def add_kernel(count, kept_ref, *refs):
    pieces, outs = refs[:count], refs[count:]
    rows, tall = pieces[0].shape[0], outs[0].shape[0]
    for index, piece in enumerate(pieces):
        row = index * rows
        total = kept_ref[row : row + rows].astype(f32) + piece[...].astype(f32)
        outs[row // tall][row % tall : row % tall + rows] = total.astype(bf16)


def add_pieces(kept, pieces, outs=1):
    rows, cols = kept.shape
    tile = max(n for n in range(128, 1025, 128) if cols % n == 0)

    def spec(tall):
        return pl.BlockSpec((tall, tile), lambda j: (0, j))

    return pl.pallas_call(
        functools.partial(add_kernel, len(pieces)),
        out_shape=[jax.ShapeDtypeStruct((rows // outs, cols), bf16)] * outs,
        grid=(cols // tile,),
        in_specs=[spec(rows)] + [spec(rows // len(pieces))] * len(pieces),
        out_specs=[spec(rows // outs)] * outs,
        compiler_params=pltpu.CompilerParams(vmem_limit_bytes=16 << 20),
        cost_estimate=pl.CostEstimate(flops=1000, bytes_accessed=1000, transcendentals=0),
        name="pair",
    )(kept, *pieces)


def gather_sums_kernel(places, *refs):
    quarters, sums, out_ref = refs[:4], refs[4:-1], refs[-1]
    rows = quarters[0].shape[0]
    for index, ref in enumerate(quarters):
        value = ref[...].astype(f32)
        for place, other in zip(places, sums):
            at = (index - place) * rows
            if 0 <= at < other.shape[0]:
                value = value + other[at : at + rows].astype(f32)
        out_ref[index * rows : (index + 1) * rows] = value.astype(bf16)


def gather_sums(quarters, sums):
    rows, cols = quarters[0].shape
    tile = max(n for n in range(128, 2049, 128) if cols % n == 0)
    places = [sum(value.shape[0] for value in sums[:k]) // rows for k in range(len(sums))]

    def spec(tall):
        return pl.BlockSpec((tall, tile), lambda j: (0, j))

    return pl.pallas_call(
        functools.partial(gather_sums_kernel, places),
        out_shape=jax.ShapeDtypeStruct((4 * rows, cols), bf16),
        grid=(cols // tile,),
        in_specs=[spec(rows)] * 4 + [spec(value.shape[0]) for value in sums],
        out_specs=spec(4 * rows),
        compiler_params=pltpu.CompilerParams(vmem_limit_bytes=24 << 20),
        cost_estimate=pl.CostEstimate(flops=1000, bytes_accessed=1000, transcendentals=0),
        name="sums",
    )(*quarters, *sums)


def example_gradients(acts_low, grads_low, local_ids, examples):
    onehot = (local_ids[:, None] == jnp.arange(examples, dtype=jnp.int32)[None, :]).astype(f32)
    counts = jnp.sum(onehot, axis=0)
    spread = (onehot[:, :, None] * acts_low[:, None, :]).reshape(onehot.shape[0], -1)
    outer_sum = lax.dot_general(
        spread,
        grads_low,
        (((0,), (0,)), ((), ())),
        precision=highest,
        preferred_element_type=f32,
    )
    basis_rank = acts_low.shape[1]
    outer_sum = outer_sum.reshape(examples, basis_rank * grads_low.shape[1]) / counts[:, None]
    return outer_sum.astype(bf16)


def gather_examples(example_grad, example_group):
    count = example_grad.shape[0]
    group_column = jnp.broadcast_to(example_group.astype(bf16)[:, None], (count, 128))
    held = jnp.concatenate([example_grad, group_column], axis=1)
    return [held] + [swap(held, step) for step in range(1, lax.axis_size("dp"))]


def order_examples(values):
    groups, place = lax.axis_size("dp"), lax.axis_index("dp")
    ordered = []
    for group in range(groups):
        value = values[0]
        for step in range(1, groups):
            value = jnp.where((place ^ group) == step, values[step], value)
        ordered.append(value)
    return jnp.concatenate(ordered, axis=0)


def fisher_and_groups(every, flat_width):
    row_count = flat_width // lax.axis_size("dp")
    col_count = flat_width // lax.axis_size("tensor")
    col_start = lax.axis_index("tensor") * col_count
    row_start = lax.axis_index("dp") * row_count
    every_group = every[:, flat_width].astype(jnp.int32)
    rows_part = lax.dynamic_slice_in_dim(every, row_start, row_count, 1)
    cols_part = lax.dynamic_slice_in_dim(every, col_start, col_count, 1)
    fisher = lax.dot_general(
        rows_part, cols_part, (((0,), (0,)), ((), ())), preferred_element_type=f32
    )
    member = (every_group[:, None] == jnp.arange(GROUPS, dtype=jnp.int32)[None, :]).astype(bf16)
    group_grad = lax.dot_general(
        member, cols_part, (((0,), (0,)), ((), ())), preferred_element_type=f32
    )
    return fisher, group_grad


def small_sums(hidden_acts, output_grad, input_basis, output_basis):
    acts_part = jnp.dot(hidden_acts, input_basis, preferred_element_type=f32)
    grads_part = lax.dot_general(
        output_grad,
        output_basis,
        (((0, 1, 2), (0, 1, 2)), ((), ())),
        preferred_element_type=f32,
    )
    return jnp.concatenate([acts_part, grads_part], axis=1)


def any_mesh(
    hidden_acts, output_grad, down_weight, input_basis, output_basis, token_example, example_group
):
    pieces = lax.all_to_all(output_grad, "dp", split_axis=1, concat_axis=3, tiled=True)
    columns = lax.all_gather(pieces, "tensor", axis=0, tiled=True)
    parts = small_sums(hidden_acts, output_grad, input_basis, output_basis)
    terms = lax.dot_general(
        columns, down_weight, (((0, 1, 2), (0, 1, 2)), ((), ())), preferred_element_type=f32
    )
    hidden_grad = lax.psum_scatter(terms.astype(bf16), "dp", scatter_dimension=0, tiled=True)
    acts_low, grads_low = jnp.split(lax.psum(parts, "tensor"), 2, axis=1)
    example_grad = example_gradients(
        acts_low, grads_low, token_example[0], example_group.shape[0]
    )
    every = order_examples(gather_examples(example_grad, example_group))
    fisher, group_grad = fisher_and_groups(every, example_grad.shape[1])
    return (hidden_grad, fisher, group_grad)


def line_of_four(
    hidden_acts, output_grad, down_weight, input_basis, output_basis, token_example, example_group
):
    tokens = hidden_acts.shape[0]
    rows = tokens // 2
    place = lax.axis_index("dp")
    turned = jnp.transpose(output_grad[0], (0, 2, 1))
    pieces = [lax.dynamic_index_in_dim(turned, place ^ k, 0, keepdims=False) for k in range(4)]
    far = []
    for half in range(2):
        cut = slice(half * rows, (half + 1) * rows)
        far.append(jnp.concatenate([swap(pieces[3][cut], 3), swap(pieces[2][cut], 2)]))
    beside, own = swap(pieces[1], 1), pieces[0]
    parts = small_sums(hidden_acts, output_grad, input_basis, output_basis)
    low = parts + across(parts, 1)

    blocks = spread_direct(after(far[0], parts))
    low = after(low, *blocks[1:])
    partner = across(low, 2)
    far[1] = after(far[1], *blocks[1:])
    later = spread_direct(far[1])

    def far_terms(chunk, at, pieces, *earlier):
        chunk = [after(chunk[0], *earlier)] + chunk[1:] if earlier else chunk
        outs = [rows // pieces] * pieces + [rows]
        *sent, kept = block_terms(chunk, down_weight, at, 2, outs)
        return sent, kept

    def pair_sum(sent, kept, *earlier, outs=1):
        pair = add_pieces(kept, [swap(after(term, *earlier), 1) for term in sent], outs)
        return pair[0], [swap(term, 2) for term in pair]

    sent0, kept0 = far_terms(blocks, 0, 2, beside)
    sent1, kept1 = far_terms(blocks, 1, 2, sent0[0])
    acts_low, grads_low = jnp.split(after(low, sent1[0]) + partner, 2, axis=1)
    example_grad = example_gradients(
        acts_low, grads_low, token_example[0], example_group.shape[0]
    )
    pair0, sum0 = pair_sum(sent0, kept0, *later[1:], example_grad)
    pair1, sum1 = pair_sum(sent1, kept1, *later[1:])

    beside = spread_first(after(beside, pair1))
    sent, kept = far_terms(later, 0, 2, pair0, pair1)
    pair2, sum2 = pair_sum(sent, kept, *beside[1:])

    beside = spread_last(beside, pair2)
    own = spread_first(after(own, pair2))
    gathered = gather_examples(after(example_grad, pair1), example_group)
    sent, kept = far_terms(later, 1, 2, pair2, *sum0, *gathered)
    every = order_examples(after(gathered, sent[0]))
    fisher, group_grad = fisher_and_groups(every, example_grad.shape[1])
    pair3, sum3 = pair_sum(sent, kept, *own, *beside, fisher, group_grad, outs=2)

    own = spread_last(own, pair3)
    beside = [after(beside[0], pair3, *sum1)] + beside[1:]
    near0 = block_terms(beside, down_weight, 0, 2, [rows // 2] * 4)
    near0 = [swap(after(term, *own[3:]), 1) for term in near0]
    adds0 = gather_sums(near0, sum0 + sum2)
    beside = [after(beside[0], near0[0], *sum2)] + beside[1:]
    near1 = block_terms(beside, down_weight, 1, 2, [rows // 2] * 4)

    near1 = [swap(after(term, sum3[0]), 1) for term in near1]
    adds1 = gather_sums(near1, sum1)
    own = [after(own[0], adds1)] + own[1:]
    (result,) = block_terms(own, down_weight, 0, 2, [tokens], [adds0])
    own = [after(own[0], result)] + own[1:]
    (result,) = block_terms(own, down_weight, 1, 2, [tokens], [adds1] + sum3, result)
    return (result, fisher, group_grad)


def per_device(hidden_acts, output_grad, down_weight, *rest):
    fits = lax.axis_size("tensor") == 4 and lax.axis_size("dp") == 4
    fits = fits and down_weight.shape[2] % 128 == 0 and down_weight.shape[3] % 1024 == 0
    fits = fits and hidden_acts.shape[0] % 64 == 0
    return (line_of_four if fits else any_mesh)(hidden_acts, output_grad, down_weight, *rest)


def solution(mesh):
    return jax.shard_map(
        per_device,
        mesh=mesh,
        in_specs=(
            P(("parts", "dp"), "tensor"),
            P("tensor", None, None, ("parts", "dp")),
            P(None, "dp", None, "tensor"),
            P("tensor", None),
            P("tensor", None, None, None),
            P(("parts", "dp"), None),
            P(("parts", "dp")),
        ),
        out_specs=(
            P(("parts", "dp"), "tensor"),
            P(("parts", "dp"), "tensor"),
            P("parts", "tensor"),
        ),
        check_vma=False,
    )
```

```python
import functools

import jax
import jax.numpy as jnp
from jax import lax
from jax.experimental import pallas as pl
from jax.experimental.pallas import tpu as pltpu
from jax.sharding import PartitionSpec as P

GROUPS = 8

highest = lax.Precision.HIGHEST
f32, bf16 = jnp.float32, jnp.bfloat16


def swap(value, step):
    size = lax.axis_size("dp")
    return lax.ppermute(value, "dp", [(d, d ^ step) for d in range(size)])


def after(value, *earlier):
    return lax.optimization_barrier((value,) + earlier)[0]


def across(value, step, places=None):
    size = lax.axis_size("tensor")
    pairs = [(t, t ^ step) for t in range(size) if places is None or t in places]
    return lax.ppermute(value, "tensor", pairs)


def spread_first(block):
    second = across(block, 2)
    return [block, across(block, 1), second]


def spread_direct(block):
    second, third = across(block, 2), across(block, 3)
    return [block, across(block, 1), second, third]


def spread_last(blocks, *earlier):
    block, _, second = blocks
    middle = across(after(block, second, *earlier), 3, (1, 2))
    ends = across(after(second, *earlier), 1, (1, 2))
    return blocks + [middle, ends]


def terms_kernel(size, count, first, lows, place_ref, *refs):
    blocks, w_ref = refs[:count], refs[count]
    feats, held, sems, held_sems = refs[-4:]
    outs = refs[count + 1 : -4]
    add_refs = []
    if lows is not None:
        add_refs, outs = outs[: 1 + lows], outs[-1:]
    width, tile = feats.shape[1] // size, outs[0].shape[1]
    j, steps = pl.program_id(0), pl.num_programs(0)
    slots = held.shape[0]

    def put(value, source, slot):
        at = pl.ds(pl.multiple_of(source * width, width), width)
        return pltpu.make_async_copy(value, feats.at[:, at], sems.at[slot])

    def fetch(step):
        slot = lax.rem(step, slots)
        at = pl.ds(pl.multiple_of(first + step * tile, tile), tile)
        return [
            pltpu.make_async_copy(
                w_ref.at[source, 0, :, at], held.at[slot, source], held_sems.at[slot, source]
            )
            for source in range(size)
        ]

    @pl.when(j == 0)
    def _():
        place = place_ref[0]
        straight = 3 if count == 5 else 4
        copies = [put(blocks[k], lax.bitwise_xor(place, k), k) for k in range(straight)]
        for copy in copies:
            copy.start()
        for step in range(slots):
            for copy in fetch(step):
                copy.start()
        inside = jnp.logical_or(place == 1, place == 2)
        relayed = ((inside, 3), (jnp.logical_not(inside), 4)) if count == 5 else ()
        for chosen, k in relayed:

            @pl.when(chosen)
            def _():
                last = put(blocks[k], lax.bitwise_xor(place, 3), 3)
                last.start()
                last.wait()

        for copy in copies:
            copy.wait()

    for copy in fetch(j):
        copy.wait()
    weight = held[lax.rem(j, slots)].reshape(size * width, tile)
    terms = jnp.dot(feats[...], weight, preferred_element_type=f32)
    if add_refs:
        terms = terms + add_refs[0][...].astype(f32)
    row = 0
    for low_ref in reversed(add_refs[1:]):
        row += low_ref.shape[0]
        cut = slice(feats.shape[0] - row, feats.shape[0] - row + low_ref.shape[0])
        outs[0][cut] = (terms[cut] + low_ref[...].astype(f32)).astype(bf16)
    if add_refs:
        outs[0][: feats.shape[0] - row] = terms[: feats.shape[0] - row].astype(bf16)
    else:
        for out_ref in outs:
            out_ref[...] = terms[row : row + out_ref.shape[0]].astype(bf16)
            row += out_ref.shape[0]

    @pl.when(j + slots < steps)
    def _():
        for copy in fetch(j + slots):
            copy.start()


def block_terms(blocks, down_weight, part, parts, outs, adds=None, into=None):
    size, _, width, every = down_weight.shape
    rows, cols = sum(outs), every // parts
    tile = max(n for n in range(128, 513, 128) if cols % n == 0)
    slots = min(5, cols // tile)

    def spec(tall, first=0):
        return pl.BlockSpec((tall, tile), lambda j, place: (0, first + j))

    operands = [*blocks, down_weight]
    in_specs = [pl.BlockSpec(memory_space=pltpu.HBM)] * len(operands)
    out_shape = [jax.ShapeDtypeStruct((tall, cols), bf16) for tall in outs]
    out_specs = [spec(tall) for tall in outs]
    aliases = {}
    if adds is not None:
        operands += adds
        in_specs += [spec(value.shape[0]) for value in adds]
        out_shape = [jax.ShapeDtypeStruct((rows, every), bf16)]
        out_specs = [spec(rows, part * (cols // tile))]
    if into is not None:
        operands.append(into)
        in_specs.append(pl.BlockSpec(memory_space=pltpu.HBM))
        aliases = {len(operands): 0}
    return pl.pallas_call(
        functools.partial(
            terms_kernel,
            size,
            len(blocks),
            part * cols,
            None if adds is None else len(adds) - 1,
        ),
        out_shape=out_shape,
        grid_spec=pltpu.PrefetchScalarGridSpec(
            num_scalar_prefetch=1,
            grid=(cols // tile,),
            in_specs=in_specs,
            out_specs=out_specs,
            scratch_shapes=[
                pltpu.VMEM((rows, size * width), bf16),
                pltpu.VMEM((slots, size, width, tile), bf16),
                pltpu.SemaphoreType.DMA((size,)),
                pltpu.SemaphoreType.DMA((slots, size)),
            ],
        ),
        input_output_aliases=aliases,
        compiler_params=pltpu.CompilerParams(vmem_limit_bytes=24 << 20),
        cost_estimate=pl.CostEstimate(
            flops=rows * size * width * cols // 4, bytes_accessed=1000, transcendentals=0
        ),
        name="terms",
    )(lax.axis_index("tensor").reshape(1), *operands)


def add_kernel(count, kept_ref, *refs):
    pieces, outs = refs[:count], refs[count:]
    rows, tall = pieces[0].shape[0], outs[0].shape[0]
    for index, piece in enumerate(pieces):
        row = index * rows
        total = kept_ref[row : row + rows].astype(f32) + piece[...].astype(f32)
        outs[row // tall][row % tall : row % tall + rows] = total.astype(bf16)


def add_pieces(kept, pieces, outs=1):
    rows, cols = kept.shape
    tile = max(n for n in range(128, 1025, 128) if cols % n == 0)

    def spec(tall):
        return pl.BlockSpec((tall, tile), lambda j: (0, j))

    return pl.pallas_call(
        functools.partial(add_kernel, len(pieces)),
        out_shape=[jax.ShapeDtypeStruct((rows // outs, cols), bf16)] * outs,
        grid=(cols // tile,),
        in_specs=[spec(rows)] + [spec(rows // len(pieces))] * len(pieces),
        out_specs=[spec(rows // outs)] * outs,
        compiler_params=pltpu.CompilerParams(vmem_limit_bytes=16 << 20),
        cost_estimate=pl.CostEstimate(flops=1000, bytes_accessed=1000, transcendentals=0),
        name="pair",
    )(kept, *pieces)


def gather_sums_kernel(places, *refs):
    quarters, sums, out_ref = refs[:4], refs[4:-1], refs[-1]
    rows = quarters[0].shape[0]
    for index, ref in enumerate(quarters):
        value = ref[...].astype(f32)
        for place, other in zip(places, sums):
            at = (index - place) * rows
            if 0 <= at < other.shape[0]:
                value = value + other[at : at + rows].astype(f32)
        out_ref[index * rows : (index + 1) * rows] = value.astype(bf16)


def gather_sums(quarters, sums):
    rows, cols = quarters[0].shape
    tile = max(n for n in range(128, 2049, 128) if cols % n == 0)
    places = [sum(value.shape[0] for value in sums[:k]) // rows for k in range(len(sums))]

    def spec(tall):
        return pl.BlockSpec((tall, tile), lambda j: (0, j))

    return pl.pallas_call(
        functools.partial(gather_sums_kernel, places),
        out_shape=jax.ShapeDtypeStruct((4 * rows, cols), bf16),
        grid=(cols // tile,),
        in_specs=[spec(rows)] * 4 + [spec(value.shape[0]) for value in sums],
        out_specs=spec(4 * rows),
        compiler_params=pltpu.CompilerParams(vmem_limit_bytes=24 << 20),
        cost_estimate=pl.CostEstimate(flops=1000, bytes_accessed=1000, transcendentals=0),
        name="sums",
    )(*quarters, *sums)


def example_gradients(acts_low, grads_low, local_ids, examples):
    onehot = (local_ids[:, None] == jnp.arange(examples, dtype=jnp.int32)[None, :]).astype(f32)
    counts = jnp.sum(onehot, axis=0)
    spread = (onehot[:, :, None] * acts_low[:, None, :]).reshape(onehot.shape[0], -1)
    outer_sum = lax.dot_general(
        spread,
        grads_low,
        (((0,), (0,)), ((), ())),
        precision=highest,
        preferred_element_type=f32,
    )
    basis_rank = acts_low.shape[1]
    outer_sum = outer_sum.reshape(examples, basis_rank * grads_low.shape[1]) / counts[:, None]
    return outer_sum.astype(bf16)


def gather_examples(example_grad, example_group):
    count = example_grad.shape[0]
    group_column = jnp.broadcast_to(example_group.astype(bf16)[:, None], (count, 128))
    held = jnp.concatenate([example_grad, group_column], axis=1)
    return [held] + [swap(held, step) for step in range(1, lax.axis_size("dp"))]


def order_examples(values):
    groups, place = lax.axis_size("dp"), lax.axis_index("dp")
    ordered = []
    for group in range(groups):
        value = values[0]
        for step in range(1, groups):
            value = jnp.where((place ^ group) == step, values[step], value)
        ordered.append(value)
    return jnp.concatenate(ordered, axis=0)


def fisher_and_groups(every, flat_width):
    row_count = flat_width // lax.axis_size("dp")
    col_count = flat_width // lax.axis_size("tensor")
    col_start = lax.axis_index("tensor") * col_count
    row_start = lax.axis_index("dp") * row_count
    every_group = every[:, flat_width].astype(jnp.int32)
    rows_part = lax.dynamic_slice_in_dim(every, row_start, row_count, 1)
    cols_part = lax.dynamic_slice_in_dim(every, col_start, col_count, 1)
    fisher = lax.dot_general(
        rows_part, cols_part, (((0,), (0,)), ((), ())), preferred_element_type=f32
    )
    member = (every_group[:, None] == jnp.arange(GROUPS, dtype=jnp.int32)[None, :]).astype(bf16)
    group_grad = lax.dot_general(
        member, cols_part, (((0,), (0,)), ((), ())), preferred_element_type=f32
    )
    return fisher, group_grad


def small_sums(hidden_acts, output_grad, input_basis, output_basis):
    acts_part = jnp.dot(hidden_acts, input_basis, preferred_element_type=f32)
    grads_part = lax.dot_general(
        output_grad,
        output_basis,
        (((0, 1, 2), (0, 1, 2)), ((), ())),
        preferred_element_type=f32,
    )
    return jnp.concatenate([acts_part, grads_part], axis=1)


def any_mesh(
    hidden_acts, output_grad, down_weight, input_basis, output_basis, token_example, example_group
):
    pieces = lax.all_to_all(output_grad, "dp", split_axis=1, concat_axis=3, tiled=True)
    columns = lax.all_gather(pieces, "tensor", axis=0, tiled=True)
    parts = small_sums(hidden_acts, output_grad, input_basis, output_basis)
    terms = lax.dot_general(
        columns, down_weight, (((0, 1, 2), (0, 1, 2)), ((), ())), preferred_element_type=f32
    )
    hidden_grad = lax.psum_scatter(terms.astype(bf16), "dp", scatter_dimension=0, tiled=True)
    acts_low, grads_low = jnp.split(lax.psum(parts, "tensor"), 2, axis=1)
    example_grad = example_gradients(
        acts_low, grads_low, token_example[0], example_group.shape[0]
    )
    every = order_examples(gather_examples(example_grad, example_group))
    fisher, group_grad = fisher_and_groups(every, example_grad.shape[1])
    return (hidden_grad, fisher, group_grad)


def line_of_four(
    hidden_acts, output_grad, down_weight, input_basis, output_basis, token_example, example_group
):
    tokens = hidden_acts.shape[0]
    rows = tokens // 2
    place = lax.axis_index("dp")
    turned = jnp.transpose(output_grad[0], (0, 2, 1))
    pieces = [lax.dynamic_index_in_dim(turned, place ^ k, 0, keepdims=False) for k in range(4)]
    far = []
    for half in range(2):
        cut = slice(half * rows, (half + 1) * rows)
        far.append(jnp.concatenate([swap(pieces[3][cut], 3), swap(pieces[2][cut], 2)]))
    beside, own = swap(pieces[1], 1), pieces[0]
    parts = small_sums(hidden_acts, output_grad, input_basis, output_basis)
    low = parts + across(parts, 1)

    blocks = spread_direct(after(far[0], parts))
    low = after(low, *blocks[1:])
    partner = across(low, 2)
    far[1] = after(far[1], *blocks[1:])
    later = spread_direct(far[1])

    def far_terms(chunk, at, pieces, *earlier):
        chunk = [after(chunk[0], *earlier)] + chunk[1:] if earlier else chunk
        outs = [rows // pieces] * pieces + [rows]
        *sent, kept = block_terms(chunk, down_weight, at, 2, outs)
        return sent, kept

    def pair_sum(sent, kept, *earlier, outs=1):
        pair = add_pieces(kept, [swap(after(term, *earlier), 1) for term in sent], outs)
        return pair[0], [swap(term, 2) for term in pair]

    sent0, kept0 = far_terms(blocks, 0, 2, beside)
    sent1, kept1 = far_terms(blocks, 1, 2, sent0[0])
    acts_low, grads_low = jnp.split(after(low, sent1[0]) + partner, 2, axis=1)
    example_grad = example_gradients(
        acts_low, grads_low, token_example[0], example_group.shape[0]
    )
    pair0, sum0 = pair_sum(sent0, kept0, *later[1:], example_grad)
    pair1, sum1 = pair_sum(sent1, kept1, *later[1:])

    beside = spread_first(after(beside, pair1))
    sent, kept = far_terms(later, 0, 2, pair0, pair1)
    pair2, sum2 = pair_sum(sent, kept, *beside[1:])

    beside = spread_last(beside, pair2)
    own = spread_first(after(own, pair2))
    gathered = gather_examples(after(example_grad, pair1), example_group)
    sent, kept = far_terms(later, 1, 2, pair2, *sum0, *gathered)
    every = order_examples(after(gathered, sent[0]))
    fisher, group_grad = fisher_and_groups(every, example_grad.shape[1])
    pair3, sum3 = pair_sum(sent, kept, *own, *beside, fisher, group_grad, outs=2)

    own = spread_last(own, pair3)
    beside = [after(beside[0], pair3, *sum1)] + beside[1:]
    near0 = block_terms(beside, down_weight, 0, 2, [rows // 2] * 4)
    near0 = [swap(after(term, *own[3:]), 1) for term in near0]
    adds0 = gather_sums(near0, sum0 + sum2)
    beside = [after(beside[0], near0[0], *sum2)] + beside[1:]
    near1 = block_terms(beside, down_weight, 1, 2, [rows // 2] * 4)

    near1 = [swap(after(term, sum3[0]), 1) for term in near1]
    adds1 = gather_sums(near1, sum1)
    own = [after(own[0], adds1)] + own[1:]
    (result,) = block_terms(own, down_weight, 0, 2, [tokens], [adds0])
    own = [after(own[0], result)] + own[1:]
    (result,) = block_terms(own, down_weight, 1, 2, [tokens], [adds1] + sum3, result)
    return (result, fisher, group_grad)


def per_device(hidden_acts, output_grad, down_weight, *rest):
    fits = lax.axis_size("tensor") == 4 and lax.axis_size("dp") == 4
    fits = fits and down_weight.shape[2] % 128 == 0 and down_weight.shape[3] % 1024 == 0
    fits = fits and hidden_acts.shape[0] % 64 == 0
    return (line_of_four if fits else any_mesh)(hidden_acts, output_grad, down_weight, *rest)


def solution(mesh):
    return jax.shard_map(
        per_device,
        mesh=mesh,
        in_specs=(
            P(("parts", "dp"), "tensor"),
            P("tensor", None, None, ("parts", "dp")),
            P(None, "dp", None, "tensor"),
            P("tensor", None),
            P("tensor", None, None, None),
            P(("parts", "dp"), None),
            P(("parts", "dp")),
        ),
        out_specs=(
            P(("parts", "dp"), "tensor"),
            P(("parts", "dp"), "tensor"),
            P("parts", "tensor"),
        ),
        check_vma=False,
    )
```

```python
import functools

import jax
import jax.numpy as jnp
from jax import lax
from jax.experimental import pallas as pl
from jax.experimental.pallas import tpu as pltpu
from jax.sharding import PartitionSpec as P

GROUPS = 8

highest = lax.Precision.HIGHEST
f32, bf16 = jnp.float32, jnp.bfloat16


def swap(value, step):
    size = lax.axis_size("dp")
    return lax.ppermute(value, "dp", [(d, d ^ step) for d in range(size)])


def after(value, *earlier):
    return lax.optimization_barrier((value,) + earlier)[0]


def across(value, step, places=None):
    size = lax.axis_size("tensor")
    pairs = [(t, t ^ step) for t in range(size) if places is None or t in places]
    return lax.ppermute(value, "tensor", pairs)


def spread_first(block):
    second = across(block, 2)
    return [block, across(block, 1), second]


def spread_direct(block):
    second, third = across(block, 2), across(block, 3)
    return [block, across(block, 1), second, third]


def spread_last(blocks, *earlier):
    block, _, second = blocks
    middle = across(after(block, second, *earlier), 3, (1, 2))
    ends = across(after(second, *earlier), 1, (1, 2))
    return blocks + [middle, ends]


def terms_kernel(size, count, first, lows, place_ref, *refs):
    blocks, w_ref = refs[:count], refs[count]
    feats, held, sems, held_sems = refs[-4:]
    outs = refs[count + 1 : -4]
    add_refs = []
    if lows is not None:
        add_refs, outs = outs[: 1 + lows], outs[-1:]
    width, tile = feats.shape[1] // size, outs[0].shape[1]
    j, steps = pl.program_id(0), pl.num_programs(0)
    slots = held.shape[0]

    def put(value, source, slot):
        at = pl.ds(pl.multiple_of(source * width, width), width)
        return pltpu.make_async_copy(value, feats.at[:, at], sems.at[slot])

    def fetch(step):
        slot = lax.rem(step, slots)
        at = pl.ds(pl.multiple_of(first + step * tile, tile), tile)
        return pltpu.make_async_copy(w_ref.at[:, 0, :, at], held.at[slot], held_sems.at[slot])

    @pl.when(j == 0)
    def _():
        place = place_ref[0]
        straight = 3 if count == 5 else 4
        copies = [put(blocks[k], lax.bitwise_xor(place, k), k) for k in range(straight)]
        for copy in copies:
            copy.start()
        for step in range(slots):
            fetch(step).start()
        inside = jnp.logical_or(place == 1, place == 2)
        relayed = ((inside, 3), (jnp.logical_not(inside), 4)) if count == 5 else ()
        for chosen, k in relayed:

            @pl.when(chosen)
            def _():
                last = put(blocks[k], lax.bitwise_xor(place, 3), 3)
                last.start()
                last.wait()

        for copy in copies:
            copy.wait()

    fetch(j).wait()
    weight = held[lax.rem(j, slots)].reshape(size * width, tile)
    narrow = 256 if tile % 256 == 0 else tile
    terms = jnp.concatenate(
        [
            jnp.dot(feats[...], weight[:, at : at + narrow], preferred_element_type=f32)
            for at in range(0, tile, narrow)
        ],
        axis=1,
    )
    if add_refs:
        terms = terms + add_refs[0][...].astype(f32)
    row = 0
    for low_ref in reversed(add_refs[1:]):
        row += low_ref.shape[0]
        cut = slice(feats.shape[0] - row, feats.shape[0] - row + low_ref.shape[0])
        outs[0][cut] = (terms[cut] + low_ref[...].astype(f32)).astype(bf16)
    if add_refs:
        outs[0][: feats.shape[0] - row] = terms[: feats.shape[0] - row].astype(bf16)
    else:
        for out_ref in outs:
            out_ref[...] = terms[row : row + out_ref.shape[0]].astype(bf16)
            row += out_ref.shape[0]

    @pl.when(j + slots < steps)
    def _():
        fetch(j + slots).start()


def block_terms(blocks, down_weight, part, parts, outs, adds=None, into=None):
    size, _, width, every = down_weight.shape
    rows, cols = sum(outs), every // parts
    tile = max(n for n in range(128, 513, 128) if cols % n == 0)
    slots = min(4, cols // tile)

    def spec(tall, first=0):
        return pl.BlockSpec((tall, tile), lambda j, place: (0, first + j))

    operands = [*blocks, down_weight]
    in_specs = [pl.BlockSpec(memory_space=pltpu.HBM)] * len(operands)
    out_shape = [jax.ShapeDtypeStruct((tall, cols), bf16) for tall in outs]
    out_specs = [spec(tall) for tall in outs]
    aliases = {}
    if adds is not None:
        operands += adds
        in_specs += [spec(value.shape[0]) for value in adds]
        out_shape = [jax.ShapeDtypeStruct((rows, every), bf16)]
        out_specs = [spec(rows, part * (cols // tile))]
    if into is not None:
        operands.append(into)
        in_specs.append(pl.BlockSpec(memory_space=pltpu.HBM))
        aliases = {len(operands): 0}
    return pl.pallas_call(
        functools.partial(
            terms_kernel,
            size,
            len(blocks),
            part * cols,
            None if adds is None else len(adds) - 1,
        ),
        out_shape=out_shape,
        grid_spec=pltpu.PrefetchScalarGridSpec(
            num_scalar_prefetch=1,
            grid=(cols // tile,),
            in_specs=in_specs,
            out_specs=out_specs,
            scratch_shapes=[
                pltpu.VMEM((rows, size * width), bf16),
                pltpu.VMEM((slots, size, width, tile), bf16),
                pltpu.SemaphoreType.DMA((size,)),
                pltpu.SemaphoreType.DMA((slots,)),
            ],
        ),
        input_output_aliases=aliases,
        compiler_params=pltpu.CompilerParams(vmem_limit_bytes=24 << 20),
        cost_estimate=pl.CostEstimate(
            flops=rows * size * width * cols // 4, bytes_accessed=1000, transcendentals=0
        ),
        name="terms",
    )(lax.axis_index("tensor").reshape(1), *operands)


def add_kernel(count, kept_ref, *refs):
    pieces, outs = refs[:count], refs[count:]
    rows, tall = pieces[0].shape[0], outs[0].shape[0]
    for index, piece in enumerate(pieces):
        row = index * rows
        total = kept_ref[row : row + rows].astype(f32) + piece[...].astype(f32)
        outs[row // tall][row % tall : row % tall + rows] = total.astype(bf16)


def add_pieces(kept, pieces, outs=1):
    rows, cols = kept.shape
    tile = max(n for n in range(128, 1025, 128) if cols % n == 0)

    def spec(tall):
        return pl.BlockSpec((tall, tile), lambda j: (0, j))

    return pl.pallas_call(
        functools.partial(add_kernel, len(pieces)),
        out_shape=[jax.ShapeDtypeStruct((rows // outs, cols), bf16)] * outs,
        grid=(cols // tile,),
        in_specs=[spec(rows)] + [spec(rows // len(pieces))] * len(pieces),
        out_specs=[spec(rows // outs)] * outs,
        compiler_params=pltpu.CompilerParams(vmem_limit_bytes=16 << 20),
        cost_estimate=pl.CostEstimate(flops=1000, bytes_accessed=1000, transcendentals=0),
        name="pair",
    )(kept, *pieces)


def gather_sums_kernel(places, *refs):
    quarters, sums, out_ref = refs[:4], refs[4:-1], refs[-1]
    rows = quarters[0].shape[0]
    for index, ref in enumerate(quarters):
        value = ref[...].astype(f32)
        for place, other in zip(places, sums):
            at = (index - place) * rows
            if 0 <= at < other.shape[0]:
                value = value + other[at : at + rows].astype(f32)
        out_ref[index * rows : (index + 1) * rows] = value.astype(bf16)


def gather_sums(quarters, sums):
    rows, cols = quarters[0].shape
    tile = max(n for n in range(128, 2049, 128) if cols % n == 0)
    places = [sum(value.shape[0] for value in sums[:k]) // rows for k in range(len(sums))]

    def spec(tall):
        return pl.BlockSpec((tall, tile), lambda j: (0, j))

    return pl.pallas_call(
        functools.partial(gather_sums_kernel, places),
        out_shape=jax.ShapeDtypeStruct((4 * rows, cols), bf16),
        grid=(cols // tile,),
        in_specs=[spec(rows)] * 4 + [spec(value.shape[0]) for value in sums],
        out_specs=spec(4 * rows),
        compiler_params=pltpu.CompilerParams(vmem_limit_bytes=24 << 20),
        cost_estimate=pl.CostEstimate(flops=1000, bytes_accessed=1000, transcendentals=0),
        name="sums",
    )(*quarters, *sums)


def example_gradients(acts_low, grads_low, local_ids, examples):
    onehot = (local_ids[:, None] == jnp.arange(examples, dtype=jnp.int32)[None, :]).astype(f32)
    counts = jnp.sum(onehot, axis=0)
    spread = (onehot[:, :, None] * acts_low[:, None, :]).reshape(onehot.shape[0], -1)
    outer_sum = lax.dot_general(
        spread,
        grads_low,
        (((0,), (0,)), ((), ())),
        precision=highest,
        preferred_element_type=f32,
    )
    basis_rank = acts_low.shape[1]
    outer_sum = outer_sum.reshape(examples, basis_rank * grads_low.shape[1]) / counts[:, None]
    return outer_sum.astype(bf16)


def gather_examples(example_grad, example_group):
    count = example_grad.shape[0]
    group_column = jnp.broadcast_to(example_group.astype(bf16)[:, None], (count, 128))
    held = jnp.concatenate([example_grad, group_column], axis=1)
    return [held] + [swap(held, step) for step in range(1, lax.axis_size("dp"))]


def order_examples(values):
    groups, place = lax.axis_size("dp"), lax.axis_index("dp")
    ordered = []
    for group in range(groups):
        value = values[0]
        for step in range(1, groups):
            value = jnp.where((place ^ group) == step, values[step], value)
        ordered.append(value)
    return jnp.concatenate(ordered, axis=0)


def fisher_and_groups(every, flat_width):
    row_count = flat_width // lax.axis_size("dp")
    col_count = flat_width // lax.axis_size("tensor")
    col_start = lax.axis_index("tensor") * col_count
    row_start = lax.axis_index("dp") * row_count
    every_group = every[:, flat_width].astype(jnp.int32)
    rows_part = lax.dynamic_slice_in_dim(every, row_start, row_count, 1)
    cols_part = lax.dynamic_slice_in_dim(every, col_start, col_count, 1)
    fisher = lax.dot_general(
        rows_part, cols_part, (((0,), (0,)), ((), ())), preferred_element_type=f32
    )
    member = (every_group[:, None] == jnp.arange(GROUPS, dtype=jnp.int32)[None, :]).astype(bf16)
    group_grad = lax.dot_general(
        member, cols_part, (((0,), (0,)), ((), ())), preferred_element_type=f32
    )
    return fisher, group_grad


def small_sums(hidden_acts, output_grad, input_basis, output_basis):
    acts_part = jnp.dot(hidden_acts, input_basis, preferred_element_type=f32)
    grads_part = lax.dot_general(
        output_grad,
        output_basis,
        (((0, 1, 2), (0, 1, 2)), ((), ())),
        preferred_element_type=f32,
    )
    return jnp.concatenate([acts_part, grads_part], axis=1)


def any_mesh(
    hidden_acts, output_grad, down_weight, input_basis, output_basis, token_example, example_group
):
    pieces = lax.all_to_all(output_grad, "dp", split_axis=1, concat_axis=3, tiled=True)
    columns = lax.all_gather(pieces, "tensor", axis=0, tiled=True)
    parts = small_sums(hidden_acts, output_grad, input_basis, output_basis)
    terms = lax.dot_general(
        columns, down_weight, (((0, 1, 2), (0, 1, 2)), ((), ())), preferred_element_type=f32
    )
    hidden_grad = lax.psum_scatter(terms.astype(bf16), "dp", scatter_dimension=0, tiled=True)
    acts_low, grads_low = jnp.split(lax.psum(parts, "tensor"), 2, axis=1)
    example_grad = example_gradients(
        acts_low, grads_low, token_example[0], example_group.shape[0]
    )
    every = order_examples(gather_examples(example_grad, example_group))
    fisher, group_grad = fisher_and_groups(every, example_grad.shape[1])
    return (hidden_grad, fisher, group_grad)


def line_of_four(
    hidden_acts, output_grad, down_weight, input_basis, output_basis, token_example, example_group
):
    tokens = hidden_acts.shape[0]
    rows = tokens // 2
    place = lax.axis_index("dp")
    turned = jnp.transpose(output_grad[0], (0, 2, 1))
    pieces = [lax.dynamic_index_in_dim(turned, place ^ k, 0, keepdims=False) for k in range(4)]
    far = []
    for half in range(2):
        cut = slice(half * rows, (half + 1) * rows)
        far.append(jnp.concatenate([swap(pieces[3][cut], 3), swap(pieces[2][cut], 2)]))
    beside, own = swap(pieces[1], 1), pieces[0]
    parts = small_sums(hidden_acts, output_grad, input_basis, output_basis)
    low = parts + across(parts, 1)

    blocks = spread_direct(after(far[0], parts))
    low = after(low, *blocks[1:])
    partner = across(low, 2)
    far[1] = after(far[1], *blocks[1:])
    later = spread_direct(far[1])

    def far_terms(chunk, at, pieces, *earlier):
        chunk = [after(chunk[0], *earlier)] + chunk[1:] if earlier else chunk
        outs = [rows // pieces] * pieces + [rows]
        *sent, kept = block_terms(chunk, down_weight, at, 2, outs)
        return sent, kept

    def pair_sum(sent, kept, *earlier, outs=1):
        pair = add_pieces(kept, [swap(after(term, *earlier), 1) for term in sent], outs)
        return pair[0], [swap(term, 2) for term in pair]

    sent0, kept0 = far_terms(blocks, 0, 2, beside)
    sent1, kept1 = far_terms(blocks, 1, 2, sent0[0])
    acts_low, grads_low = jnp.split(after(low, sent1[0]) + partner, 2, axis=1)
    example_grad = example_gradients(
        acts_low, grads_low, token_example[0], example_group.shape[0]
    )
    pair0, sum0 = pair_sum(sent0, kept0, *later[1:], example_grad)
    pair1, sum1 = pair_sum(sent1, kept1, *later[1:])

    beside = spread_first(after(beside, pair1))
    sent, kept = far_terms(later, 0, 2, pair0, pair1)
    pair2, sum2 = pair_sum(sent, kept, *beside[1:])

    beside = spread_last(beside, pair2)
    own = spread_first(after(own, pair2))
    gathered = gather_examples(after(example_grad, pair1), example_group)
    sent, kept = far_terms(later, 1, 2, pair2, *sum0, *gathered)
    every = order_examples(after(gathered, sent[0]))
    fisher, group_grad = fisher_and_groups(every, example_grad.shape[1])
    pair3, sum3 = pair_sum(sent, kept, *own, *beside, fisher, group_grad, outs=2)

    own = spread_last(own, pair3)
    beside = [after(beside[0], pair3, *sum1)] + beside[1:]
    near0 = block_terms(beside, down_weight, 0, 2, [rows // 2] * 4)
    near0 = [swap(after(term, *own[3:]), 1) for term in near0]
    adds0 = gather_sums(near0, sum0 + sum2)
    beside = [after(beside[0], near0[0], *sum2)] + beside[1:]
    near1 = block_terms(beside, down_weight, 1, 2, [rows // 2] * 4)

    near1 = [swap(after(term, sum3[0]), 1) for term in near1]
    adds1 = gather_sums(near1, sum1)
    own = [after(own[0], adds1)] + own[1:]
    (result,) = block_terms(own, down_weight, 0, 2, [tokens], [adds0])
    own = [after(own[0], result)] + own[1:]
    (result,) = block_terms(own, down_weight, 1, 2, [tokens], [adds1] + sum3, result)
    return (result, fisher, group_grad)


def per_device(hidden_acts, output_grad, down_weight, *rest):
    fits = lax.axis_size("tensor") == 4 and lax.axis_size("dp") == 4
    fits = fits and down_weight.shape[2] % 128 == 0 and down_weight.shape[3] % 1024 == 0
    fits = fits and hidden_acts.shape[0] % 64 == 0
    return (line_of_four if fits else any_mesh)(hidden_acts, output_grad, down_weight, *rest)


def solution(mesh):
    return jax.shard_map(
        per_device,
        mesh=mesh,
        in_specs=(
            P(("parts", "dp"), "tensor"),
            P("tensor", None, None, ("parts", "dp")),
            P(None, "dp", None, "tensor"),
            P("tensor", None),
            P("tensor", None, None, None),
            P(("parts", "dp"), None),
            P(("parts", "dp")),
        ),
        out_specs=(
            P(("parts", "dp"), "tensor"),
            P(("parts", "dp"), "tensor"),
            P("parts", "tensor"),
        ),
        check_vma=False,
    )
```
